128 devices in a mesh: depth: 16 (over z_lo, x, core), rows: 8 (over z_hi, y).
Axes of the slice: x: 4, y: 4, z: 4 (z_hi: 2, z_lo: 2; z = z_hi * 2 + z_lo), core: 2. Of those that a mesh axis runs over, the one named last changes fastest.
Arguments:
- x_now: float32 [2, 16, 2048, 2048], P(None, 'depth', 'rows'), may hold values from -150 to 150
- x_prev: float32 [2, 16, 2048, 2048], P(None, 'depth', 'rows'), may hold values from -6 to 6
- hologram: float32 [2, 2048, 2048], P(None, 'rows'), may hold values from -48 to 48
- depths: float32 [16], P('depth'), may hold values from 150 to 600
Outputs:
- x_next: float32 [2, 16, 2048, 2048], P(None, 'depth', 'rows')
The draws below stay inside these ranges and needn't reach their ends.
All inputs are finite; a program needn't handle non-finite values.
Results may differ from the reference program's by a relative error of at most 0.00016.
Values sent between devices are 32-bit elements; how exact they have to be, the bound alone decides.
No kernel may reach another device: no remote copies, remote signals or barrier semaphores. Data moves between devices by JAX's collectives and lax.ppermute only.
A program may use at most 192 MiB of HBM per device.

```python
import math
import jax
import jax.numpy as jnp
from jax import lax

N = 2048
TV_ITERS = 2
PLANES = 16


def draw_x_now(key, part):
    key = jax.random.fold_in(key, 7)
    noise_key, row_key, col_key = jax.random.split(key, 3)
    plane_pos = jnp.arange(PLANES, dtype=jnp.float32) / max(PLANES - 1, 1)
    row_pos = jnp.arange(N, dtype=jnp.float32) / (N - 1)
    rise = 3.0
    level = 0.25
    noise = jnp.clip(jax.random.normal(noise_key, (2, PLANES, N, N), jnp.float32), -6.0, 6.0)
    row_rough = jnp.exp(jax.random.uniform(row_key, (N,), jnp.float32, -1.15, 1.15))
    col_rough = jnp.exp(jax.random.uniform(col_key, (N,), jnp.float32, -1.15, 1.15))
    plane_env = jnp.power(rise, plane_pos)
    row_env = jnp.power(rise, row_pos) * row_rough
    envelope = plane_env[:, None, None] * row_env[None, :, None] * col_rough[None, None, :]
    return level * noise * envelope[None]


def steps_of(stream_key, dims, shards, low, top_value):
    gain = 1.0
    for axis_at, blocks in shards:
        steps = jax.random.uniform(jax.random.fold_in(jax.random.fold_in(stream_key, 6), axis_at), (blocks,), jnp.float32, low / len(shards), top_value / len(shards))
        gain = gain * jnp.repeat(jnp.exp(steps), dims[axis_at] // blocks).reshape((-1,) + (1,) * (len(dims) - 1 - axis_at))
    return gain


def bell_draw(rng, extent, deviation, limit, cuts=(), held_as=jnp.bfloat16):
    factor_of = steps_of(rng, extent, cuts, -0.22, 0.18) if cuts else 1.0
    entries = jax.random.normal(rng, extent, jnp.float32) * deviation * factor_of
    return jnp.minimum(jnp.maximum(entries, -limit), limit).astype(held_as)


def setup_inputs(seed: int = 0) -> dict:
    splits = jax.random.split(jax.random.key(seed), 5)
    return {
        "x_now": draw_x_now(jax.random.fold_in(splits[4], 71), 0),
        "x_prev": bell_draw(splits[1], (2, PLANES, N, N), 1.0, 6.0, ((1, 16), (2, 8)), jnp.float32),
        "hologram": bell_draw(splits[2], (2, N, N), (2 * PLANES ** 0.5), 48.0, ((1, 8),), jnp.float32),
        "depths": jnp.clip(150.0 + 450.0 * jax.random.uniform(splits[3], (PLANES,), jnp.float32) ** steps_of(splits[3], (PLANES,), ((0, 16),), -0.2, 0.2), 150.0, 600.0),
    }


ALPHA_TWIST = 1.8
BETA_TWIST = 1.2
LAMBDA_TV = 0.2
STEP_TV = 1.0 / 12.0
EPSILON = 1e-06
WAVENUMBER = 4.0 * math.pi

def spatial_freq(count):
    index = jnp.arange(count, dtype=jnp.int32)
    signed = jnp.where(index < count // 2, index, index - count)
    return signed.astype(jnp.float32) * (2.0 * math.pi / count)

def phase_rate(qx_grid, qy_grid):
    square = qx_grid * qx_grid + qy_grid * qy_grid
    return -square / (WAVENUMBER + jnp.sqrt(WAVENUMBER * WAVENUMBER - square))

def gradient(inner):
    zero_plane = jnp.zeros_like(inner[:, :1])
    zero_row = jnp.zeros_like(inner[:, :, :1])
    zero_col = jnp.zeros_like(inner[:, :, :, :1])
    grad_z = jnp.concatenate([inner[:, 1:] - inner[:, :-1], zero_plane], axis=1)
    grad_y = jnp.concatenate([inner[:, :, 1:] - inner[:, :, :-1], zero_row], axis=2)
    grad_x = jnp.concatenate([inner[:, :, :, 1:] - inner[:, :, :, :-1], zero_col], axis=3)
    return (grad_z, grad_y, grad_x)

def divergence(dual_z, dual_y, dual_x):
    part_z = dual_z - jnp.concatenate([jnp.zeros_like(dual_z[:, :1]), dual_z[:, :-1]], axis=1)
    part_y = dual_y - jnp.concatenate([jnp.zeros_like(dual_y[:, :, :1]), dual_y[:, :, :-1]], axis=2)
    part_x = dual_x - jnp.concatenate([jnp.zeros_like(dual_x[:, :, :, :1]), dual_x[:, :, :, :-1]], axis=3)
    return part_z + part_y + part_x

def reference(x_now, x_prev, hologram, depths):
    field = x_now[0] + 1j * x_now[1]
    spectra = jnp.fft.fft2(field, norm='ortho')
    rate = phase_rate(spatial_freq(N)[None, :], spatial_freq(N)[:, None])
    phase = depths[:, None, None] * rate[None]
    transfer = jnp.cos(phase) + 1j * jnp.sin(phase)
    predicted = lax.optimization_barrier(jnp.sum(transfer * spectra, axis=0))
    holo_spec = jnp.fft.fft2(hologram[0] + 1j * hologram[1], norm='ortho')
    residual = holo_spec - predicted
    back = jnp.fft.ifft2(jnp.conj(transfer) * residual[None], norm='ortho')
    updated = field + back / PLANES
    parts = jnp.stack([jnp.real(updated), jnp.imag(updated)]).astype(jnp.float32)
    mean_square = jnp.mean(parts * parts)
    strength = LAMBDA_TV * jnp.sqrt(mean_square + EPSILON)
    zeros = jnp.zeros_like(parts)
    duals = (zeros, zeros, zeros)
    for step in range(TV_ITERS):
        inner = divergence(*duals) - parts / strength
        grad_z, grad_y, grad_x = gradient(inner)
        denom = 1.0 + STEP_TV * jnp.sqrt(grad_z * grad_z + grad_y * grad_y + grad_x * grad_x)
        duals = ((duals[0] + STEP_TV * grad_z) / denom, (duals[1] + STEP_TV * grad_y) / denom, (duals[2] + STEP_TV * grad_x) / denom)
    denoised = parts - strength * divergence(*duals)
    return (1.0 - ALPHA_TWIST) * x_prev + (ALPHA_TWIST - BETA_TWIST) * x_now + BETA_TWIST * denoised
```

```python
import functools
import math

import jax
import jax.numpy as jnp
import ml_dtypes
import numpy as np
from jax import lax
from jax.experimental import pallas as pl
from jax.experimental.pallas import tpu as pltpu
from jax.sharding import PartitionSpec as P

ALPHA_TWIST = 1.8
BETA_TWIST = 1.2
LAMBDA_TV = 0.2
STEP_TV = 1.0 / 12.0
EPSILON = 1e-06
WAVENUMBER = 4.0 * math.pi

N = 2048
PLANES = 16
ROWS = 256
RADIX = 8
PART = 256
EXT = ROWS + 16
F32 = jnp.float32
BF16 = jnp.bfloat16
MIB = 1024 * 1024


def split_np(table):
    high = table.astype(np.float32).astype(ml_dtypes.bfloat16)
    low = (table - high.astype(np.float64)).astype(np.float32).astype(ml_dtypes.bfloat16)
    return high, low


def dft_blocks(scale):
    index = np.arange(PART)
    angle = 2.0 * np.pi * ((index[:, None] * index[None, :]) % PART) / PART
    cos = np.cos(angle) * scale
    sin = np.sin(angle) * scale
    forward = np.block([[cos, -sin], [sin, cos]])
    inverse = np.block([[cos, sin], [-sin, cos]])
    return forward, inverse


def twiddles():
    index = np.arange(PART)
    angle = 2.0 * np.pi * (np.arange(RADIX)[:, None] * index[None, :]) / N
    return np.stack([np.cos(angle), -np.sin(angle)], axis=1).astype(np.float32)


def dft4(a, b, c, d, sign):
    t0 = (a[0] + c[0], a[1] + c[1])
    t1 = (a[0] - c[0], a[1] - c[1])
    t2 = (b[0] + d[0], b[1] + d[1])
    t3 = (b[0] - d[0], b[1] - d[1])
    if sign > 0:
        turned = (-t3[1], t3[0])
    else:
        turned = (t3[1], -t3[0])
    return (
        (t0[0] + t2[0], t0[1] + t2[1]),
        (t1[0] + turned[0], t1[1] + turned[1]),
        (t0[0] - t2[0], t0[1] - t2[1]),
        (t1[0] - turned[0], t1[1] - turned[1]),
    )


def dft8(v, sign):
    even = dft4(v[0], v[2], v[4], v[6], sign)
    odd = dft4(v[1], v[3], v[5], v[7], sign)
    half = math.sqrt(0.5)
    o1, o2, o3 = odd[1], odd[2], odd[3]
    if sign > 0:
        w1 = ((o1[0] - o1[1]) * half, (o1[0] + o1[1]) * half)
        w2 = (-o2[1], o2[0])
        w3 = ((-o3[0] - o3[1]) * half, (o3[0] - o3[1]) * half)
    else:
        w1 = ((o1[0] + o1[1]) * half, (o1[1] - o1[0]) * half)
        w2 = (o2[1], -o2[0])
        w3 = ((o3[1] - o3[0]) * half, (-o3[0] - o3[1]) * half)
    turned = (odd[0], w1, w2, w3)
    low = [(even[k][0] + turned[k][0], even[k][1] + turned[k][1]) for k in range(4)]
    high = [(even[k][0] - turned[k][0], even[k][1] - turned[k][1]) for k in range(4)]
    return low + high


def split(x):
    high = x.astype(BF16)
    return high, (x - high.astype(F32)).astype(BF16)


def dot(a, b, contract):
    return lax.dot_general(a, b, (contract, ((), ())), preferred_element_type=F32)


def dot3(a_high, a_low, b_high, b_low, contract):
    return (
        dot(a_high, b_high, contract) + dot(a_high, b_low, contract) + dot(a_low, b_high, contract)
    )


NT = ((1,), (1,))
NN = ((1,), (0,))


def forward_radix(load, tw_ref, hi, lo, rows, half):
    lanes = slice(half * 128, half * 128 + 128)
    out = dft8([load(i) for i in range(RADIX)], -1)
    for k in range(RADIX):
        re, im = out[k]
        if k:
            c = tw_ref[k, 0:1, lanes]
            s = tw_ref[k, 1:2, lanes]
            re, im = re * c - im * s, re * s + im * c
        for part, value in ((0, re), (1, im)):
            high, low = split(value)
            at = slice(part * PART + half * 128, part * PART + half * 128 + 128)
            hi[k, rows, at] = high
            lo[k, rows, at] = low


def params(limit_mib):
    return pltpu.CompilerParams(vmem_limit_bytes=limit_mib * MIB)


def whole(shape):
    return pl.BlockSpec(shape, lambda *_: (0,) * len(shape))


def rows_body(x_ref, gh_ref, gl_ref, tw_ref, y_ref, ss_ref, hi, lo):
    k = pl.program_id(0)

    @pl.when(k == 0)
    def _():
        def chunk(t, total):
            rows = pl.ds(pl.multiple_of(t * 16, 16), 16)
            for half in range(2):

                def load(i):
                    at = slice(i * PART + half * 128, i * PART + half * 128 + 128)
                    return (x_ref[0, 0, rows, at], x_ref[1, 0, rows, at])

                patches = [load(i) for i in range(RADIX)]
                for re, im in patches:
                    total = total + (re * re + im * im)
                forward_radix(lambda i: patches[i], tw_ref, hi, lo, rows, half)
            return total

        ss_ref[...] = lax.fori_loop(0, ROWS // 16, chunk, jnp.zeros((16, 128), F32))

    gh, gl = gh_ref, gl_ref
    high, low = hi[k], lo[k]
    for part in range(2):
        at = slice(part * PART, part * PART + PART)
        out = dot3(gh[at, :], gl[at, :], high, low, NT)
        y_ref[0, :, part] = out.reshape(16, 16, ROWS)


def rows_forward(x_now, gt_high, gt_low, tw):
    return pl.pallas_call(
        rows_body,
        grid=(RADIX,),
        in_specs=[
            whole((2, 1, ROWS, N)),
            whole((2 * PART, 2 * PART)),
            whole((2 * PART, 2 * PART)),
            whole((RADIX, 2, PART)),
        ],
        out_specs=[
            pl.BlockSpec((1, 16, 2, 16, ROWS), lambda k: (k, 0, 0, 0, 0)),
            whole((16, 128)),
        ],
        out_shape=[
            jax.ShapeDtypeStruct((RADIX, 16, 2, 16, ROWS), F32),
            jax.ShapeDtypeStruct((16, 128), F32),
        ],
        scratch_shapes=[
            pltpu.VMEM((RADIX, ROWS, 2 * PART), BF16),
            pltpu.VMEM((RADIX, ROWS, 2 * PART), BF16),
        ],
        compiler_params=params(40),
        cost_estimate=pl.CostEstimate(
            flops=4 * 10**9, bytes_accessed=10 * MIB, transcendentals=0
        ),
        name="rows_forward",
    )(x_now, gt_high, gt_low, tw)


def holo_body(x_ref, gh_ref, gl_ref, tw_ref, y_ref, hi, lo):
    def chunk(t, carry):
        rows = pl.ds(pl.multiple_of(t * 16, 16), 16)
        for half in range(2):

            def load(i):
                at = slice(i * PART + half * 128, i * PART + half * 128 + 128)
                return (x_ref[0, rows, at], x_ref[1, rows, at])

            forward_radix(load, tw_ref, hi, lo, rows, half)
        return carry

    lax.fori_loop(0, ROWS // 16, chunk, 0)

    def per_k(k, carry):
        out = dot3(gh_ref[...], gl_ref[...], hi[k], lo[k], NT)
        y_ref[k] = out.reshape(2, 16, ROWS)
        return carry

    lax.fori_loop(0, RADIX, per_k, 0)


def holo_forward(hologram, gt_high, gt_low, tw):
    return pl.pallas_call(
        holo_body,
        out_shape=jax.ShapeDtypeStruct((RADIX, 2, 16, ROWS), F32),
        scratch_shapes=[
            pltpu.VMEM((RADIX, ROWS, 2 * PART), BF16),
            pltpu.VMEM((RADIX, ROWS, 2 * PART), BF16),
        ],
        in_specs=[pl.BlockSpec(memory_space=pltpu.VMEM)] * 4,
        out_specs=pl.BlockSpec(memory_space=pltpu.VMEM),
        compiler_params=params(40),
        cost_estimate=pl.CostEstimate(
            flops=4 * 10**8, bytes_accessed=5 * MIB, transcendentals=0
        ),
        name="holo_forward",
    )(hologram, gt_high, gt_low, tw)


def cos_sin(phase):
    turns = jnp.floor(phase * (2.0 / math.pi) + 0.5)
    rest = phase - turns * 1.5703125
    rest = rest - turns * 4.837512969970703e-4
    rest = rest - turns * 7.549789948768648e-8
    z = rest * rest
    sin = rest + rest * z * (
        -1.6666654611e-1 + z * (8.3321608736e-3 + z * -1.9515295891e-4)
    )
    cos = (
        1.0
        - 0.5 * z
        + z
        * z
        * (4.166664568298827e-2 + z * (-1.388731625493765e-3 + z * 2.443315711809948e-5))
    )
    quarter = turns.astype(jnp.int32) & 3
    odd = (quarter & 1) == 1
    base_cos = jnp.where(odd, sin, cos)
    base_sin = jnp.where(odd, cos, sin)
    out_cos = jnp.where((quarter == 1) | (quarter == 2), -base_cos, base_cos)
    out_sin = jnp.where(quarter >= 2, -base_sin, base_sin)
    return out_cos, out_sin


def transfer_body(depth_ref, rate_ref, t_ref):
    rate = rate_ref[0]
    for p in range(PLANES):
        cos, sin = cos_sin(depth_ref[0, p] * rate)
        rows = slice(p * 16, p * 16 + 16)
        t_ref[0, 0, rows, :] = cos
        t_ref[0, 1, rows, :] = sin


def transfer(depth_all, rate):
    return pl.pallas_call(
        transfer_body,
        grid=(RADIX,),
        in_specs=[
            pl.BlockSpec(memory_space=pltpu.SMEM),
            pl.BlockSpec((1, 16, PART), lambda k: (k, 0, 0)),
        ],
        out_specs=pl.BlockSpec((1, 2, PLANES * 16, PART), lambda k: (k, 0, 0, 0)),
        out_shape=jax.ShapeDtypeStruct((RADIX, 2, PLANES * 16, PART), F32),
        compiler_params=params(16),
        cost_estimate=pl.CostEstimate(
            flops=10**7, bytes_accessed=4 * MIB, transcendentals=0
        ),
        name="transfer",
    )(depth_all, rate)


COLS = PLANES * 16
WITH_HOLO = COLS + 16


def spectral_body(
    z_ref, h_ref, t_ref, gh_ref, gl_ref, ih_ref, il_ref, tw_ref, o_ref, norm_ref,
    hi, lo, spec, bhi, blo, back,
):
    k = pl.program_id(0)

    @pl.when(k == 0)
    def _():
        norm_ref[...] = jnp.zeros_like(norm_ref)

        def chunk(p, carry):
            rows = pl.ds(pl.multiple_of(p * 16, 16), 16)
            for half in range(2):
                at = slice(half * 128, half * 128 + 128)

                def load(i):
                    return (z_ref[i, p, 0, :, at], z_ref[i, p, 1, :, at])

                forward_radix(load, tw_ref, hi, lo, rows, half)
            return carry

        lax.fori_loop(0, PLANES, chunk, 0)
        for half in range(2):
            at = slice(half * 128, half * 128 + 128)

            def load_holo(i):
                return (h_ref[i, 0, :, at], h_ref[i, 1, :, at])

            forward_radix(load_holo, tw_ref, hi, lo, slice(COLS, WITH_HOLO), half)

    spec[...] = dot3(hi[k], lo[k], gh_ref[...], gl_ref[...], NN)

    for half in range(2):
        at = slice(half * 128, half * 128 + 128)
        at_im = slice(PART + half * 128, PART + half * 128 + 128)

        def gather(p, total):
            rows = pl.ds(pl.multiple_of(p * 16, 16), 16)
            xr, xi = spec[rows, at], spec[rows, at_im]
            tr, ti = t_ref[0, 0, rows, at], t_ref[0, 1, rows, at]
            return (total[0] + (tr * xr - ti * xi), total[1] + (tr * xi + ti * xr))

        zero = jnp.zeros((16, 128), F32)
        pred = lax.fori_loop(0, PLANES, gather, (zero, zero), unroll=4)
        holo = (spec[COLS:WITH_HOLO, at], spec[COLS:WITH_HOLO, at_im])
        res = (holo[0] - pred[0], holo[1] - pred[1])
        norm_ref[...] += res[0] * (holo[0] + pred[0]) + res[1] * (holo[1] + pred[1])

        def scatter(p, carry):
            rows = pl.ds(pl.multiple_of(p * 16, 16), 16)
            tr, ti = t_ref[0, 0, rows, at], t_ref[0, 1, rows, at]
            br = tr * res[0] + ti * res[1]
            bi = tr * res[1] - ti * res[0]
            for where, value in ((at, br), (at_im, bi)):
                high, low = split(value)
                bhi[rows, where] = high
                blo[rows, where] = low
            return carry

        lax.fori_loop(0, PLANES, scatter, 0, unroll=4)

    c = tw_ref[k, 0:1, :]
    s = tw_ref[k, 1:2, :]
    out = dot3(bhi[...], blo[...], ih_ref[...], il_ref[...], NN)
    re, im = out[:, :PART], out[:, PART:]
    back[k, 0] = re * c + im * s
    back[k, 1] = im * c - re * s

    @pl.when(k == RADIX - 1)
    def _():
        def chunk(p, carry):
            rows = pl.ds(pl.multiple_of(p * 16, 16), 16)
            for half in range(2):
                at = slice(half * 128, half * 128 + 128)
                out = dft8([(back[i, 0, rows, at], back[i, 1, rows, at]) for i in range(RADIX)], 1)
                for i in range(RADIX):
                    o_ref[i, p, 0, :, at] = out[i][0]
                    o_ref[i, p, 1, :, at] = out[i][1]
            return carry

        lax.fori_loop(0, PLANES, chunk, 0)


def spectral(z, holo, trans, g_high, g_low, i_high, i_low, tw):
    table = whole((2 * PART, 2 * PART))
    return pl.pallas_call(
        spectral_body,
        grid=(RADIX,),
        in_specs=[
            whole((RADIX, PLANES, 2, 16, PART)),
            whole((RADIX, 2, 16, PART)),
            pl.BlockSpec((1, 2, COLS, PART), lambda k: (k, 0, 0, 0)),
            table,
            table,
            table,
            table,
            whole((RADIX, 2, PART)),
        ],
        out_specs=[whole((RADIX, PLANES, 2, 16, PART)), whole((16, 128))],
        out_shape=[
            jax.ShapeDtypeStruct((RADIX, PLANES, 2, 16, PART), F32),
            jax.ShapeDtypeStruct((16, 128), F32),
        ],
        scratch_shapes=[
            pltpu.VMEM((RADIX, WITH_HOLO, 2 * PART), BF16),
            pltpu.VMEM((RADIX, WITH_HOLO, 2 * PART), BF16),
            pltpu.VMEM((WITH_HOLO, 2 * PART), F32),
            pltpu.VMEM((COLS, 2 * PART), BF16),
            pltpu.VMEM((COLS, 2 * PART), BF16),
            pltpu.VMEM((RADIX, 2, COLS, PART), F32),
        ],
        compiler_params=params(56),
        cost_estimate=pl.CostEstimate(
            flops=8 * 10**9, bytes_accessed=14 * MIB, transcendentals=0
        ),
        name="spectral",
    )(z, holo, trans, g_high, g_low, i_high, i_low, tw)


def rows_back_body(
    w_ref, x_ref, ih_ref, il_ref, tw_ref, re_ref, im_ref, top_ref, bot_ref, back
):
    k = pl.program_id(0)
    parts = [w_ref[0, :, c].reshape(PART, ROWS).T for c in range(2)]
    high, low = split(jnp.concatenate(parts, axis=1))
    out = dot3(high, low, ih_ref[...], il_ref[...], NN)
    c = tw_ref[k, 0:1, :]
    s = tw_ref[k, 1:2, :]
    re, im = out[:, :PART], out[:, PART:]
    back[k, 0] = re * c + im * s
    back[k, 1] = im * c - re * s

    @pl.when(k == RADIX - 1)
    def _():
        def chunk(t, carry):
            rows = pl.ds(pl.multiple_of(t * 16, 16), 16)
            for half in range(2):
                at = slice(half * 128, half * 128 + 128)
                out = dft8([(back[i, 0, rows, at], back[i, 1, rows, at]) for i in range(RADIX)], 1)
                for i in range(RADIX):
                    to = slice(i * PART + half * 128, i * PART + half * 128 + 128)
                    re_ref[rows, to] = x_ref[0, 0, rows, to] + out[i][0]
                    im_ref[rows, to] = x_ref[1, 0, rows, to] + out[i][1]
            return carry

        lax.fori_loop(0, ROWS // 16, chunk, 0)
        top_ref[0] = re_ref[0:8, :]
        top_ref[1] = im_ref[0:8, :]
        bot_ref[0] = re_ref[ROWS - 8 : ROWS, :]
        bot_ref[1] = im_ref[ROWS - 8 : ROWS, :]


def rows_back(w, x_now, i_high, i_low, tw):
    table = whole((2 * PART, 2 * PART))
    return pl.pallas_call(
        rows_back_body,
        grid=(RADIX,),
        in_specs=[
            pl.BlockSpec((1, 16, 2, 16, ROWS), lambda k: (k, 0, 0, 0, 0)),
            whole((2, 1, ROWS, N)),
            table,
            table,
            whole((RADIX, 2, PART)),
        ],
        out_specs=[whole((ROWS, N)), whole((ROWS, N)), whole((2, 8, N)), whole((2, 8, N))],
        out_shape=[
            jax.ShapeDtypeStruct((ROWS, N), F32),
            jax.ShapeDtypeStruct((ROWS, N), F32),
            jax.ShapeDtypeStruct((2, 8, N), F32),
            jax.ShapeDtypeStruct((2, 8, N), F32),
        ],
        scratch_shapes=[pltpu.VMEM((RADIX, 2, ROWS, PART), F32)],
        compiler_params=params(48),
        cost_estimate=pl.CostEstimate(
            flops=4 * 10**9, bytes_accessed=13 * MIB, transcendentals=0
        ),
        name="rows_back",
    )(w, x_now, i_high, i_low, tw)


TILES = EXT // 8


def below(x, after):
    row = lax.broadcasted_iota(jnp.int32, x.shape, 0)
    return pltpu.roll(jnp.where(row == 0, after, x), 7, 0)


def above(x, before):
    row = lax.broadcasted_iota(jnp.int32, x.shape, 0)
    return pltpu.roll(jnp.where(row == 7, before, x), 1, 0)


def right_of(x):
    return pltpu.roll(x, N - 1, 1)


def left_of(x):
    return pltpu.roll(x, 1, 1)


def weight(gz, gy, gx):
    return 1.0 / (1.0 + jnp.sqrt(gz * gz + gy * gy + gx * gx))


def masks(t, row_base):
    row = lax.broadcasted_iota(jnp.int32, (8, N), 0) + (row_base + t * 8 - 8)
    col = lax.broadcasted_iota(jnp.int32, (8, N), 1)
    return (row >= 0) & (row < N - 1), col < N - 1


def tv_first_body(
    comp, num_ref, at_ref, own, nxt, prv, own_h, nxt_h, prv_h, inner_ref, dual_ref, ext, sems
):
    copies = []
    for which, (main, halo) in enumerate(((own, own_h), (nxt, nxt_h), (prv, prv_h))):
        copies += [
            pltpu.make_async_copy(
                main, ext.at[which, pl.ds(8, ROWS), :], sems.at[which, 0]
            ),
            pltpu.make_async_copy(
                halo.at[0, comp], ext.at[which, pl.ds(0, 8), :], sems.at[which, 1]
            ),
            pltpu.make_async_copy(
                halo.at[1, comp], ext.at[which, pl.ds(ROWS + 8, 8), :], sems.at[which, 2]
            ),
        ]
    for copy in copies:
        copy.start()
    for copy in copies:
        copy.wait()
    scale = num_ref[0]
    inverse = num_ref[1]
    keep_next = num_ref[2]
    keep_prev = num_ref[3]
    row_base = at_ref[0]

    def tile(t, before):
        rows = pl.ds(pl.multiple_of(t * 8, 8), 8)
        later = pl.ds(pl.multiple_of(jnp.minimum(t + 1, TILES - 1) * 8, 8), 8)
        row_ok, col_ok = masks(t, row_base)
        u = ext[0, rows, :]
        q = ext[2, rows, :]
        gz = (ext[1, rows, :] - u) * (scale * keep_next)
        gy = jnp.where(row_ok, (below(u, ext[0, later, :]) - u) * scale, 0.0)
        gx = jnp.where(col_ok, (right_of(u) - u) * scale, 0.0)
        w = weight(gz, gy, gx)
        dz, dy, dx = gz * w, gy * w, gx * w
        gz = (u - q) * (scale * keep_prev)
        gy = jnp.where(row_ok, (below(q, ext[2, later, :]) - q) * scale, 0.0)
        gx = jnp.where(col_ok, (right_of(q) - q) * scale, 0.0)
        dq = gz * weight(gz, gy, gx)
        div = (dz - dq) + (dy - above(dy, before)) + (dx - left_of(dx))
        inner_ref[rows, :] = (div + u * inverse) * STEP_TV
        dual_ref[0, rows, :] = dz
        dual_ref[1, rows, :] = dy
        dual_ref[2, rows, :] = dx
        dual_ref[3, rows, :] = dq
        return dy

    lax.fori_loop(0, TILES, tile, jnp.zeros((8, N), F32))


def tv_first(comp, numbers, place, own, nxt, prv, own_h, nxt_h, prv_h):
    smem = pl.BlockSpec(memory_space=pltpu.SMEM)
    anywhere = pl.BlockSpec(memory_space=pl.ANY)
    vmem = pl.BlockSpec(memory_space=pltpu.VMEM)
    return pl.pallas_call(
        functools.partial(tv_first_body, comp),
        in_specs=[smem, smem] + [anywhere] * 6,
        out_specs=[vmem, vmem],
        out_shape=[
            jax.ShapeDtypeStruct((EXT, N), F32),
            jax.ShapeDtypeStruct((4, EXT, N), F32),
        ],
        scratch_shapes=[
            pltpu.VMEM((3, EXT, N), F32),
            pltpu.SemaphoreType.DMA((3, 3)),
        ],
        compiler_params=params(40),
        cost_estimate=pl.CostEstimate(
            flops=10**8, bytes_accessed=17 * MIB, transcendentals=2 * 10**6
        ),
        name="tv_first",
    )(numbers, place, own, nxt, prv, own_h, nxt_h, prv_h)


def tv_second_body(
    comp, num_ref, at_ref, own, nxt, prv, dual, parts, x_prev, x_now, *rest
):
    out_ref = rest[-1]
    strength = num_ref[4]
    keep_next = num_ref[2]
    keep_prev = num_ref[3]
    row_base = at_ref[0]

    def duals(t):
        rows = pl.ds(pl.multiple_of(t * 8, 8), 8)
        later = pl.ds(pl.multiple_of(t * 8 + 8, 8), 8)
        row_ok, col_ok = masks(t, row_base)
        u = own[rows, :]
        gz = (nxt[rows, :] - u) * keep_next
        gy = jnp.where(row_ok, below(u, own[later, :]) - u, 0.0)
        gx = jnp.where(col_ok, right_of(u) - u, 0.0)
        w = weight(gz, gy, gx)
        return rows, later, row_ok, col_ok, u, gz, gy, gx, w

    _, _, _, _, _, _, gy0, _, w0 = duals(0)
    first = (dual[1, 0:8, :] + gy0) * w0

    def tile(t, before):
        rows, later, row_ok, col_ok, u, gz, gy, gx, w = duals(t)
        dz = (dual[0, rows, :] + gz) * w
        dy = (dual[1, rows, :] + gy) * w
        dx = (dual[2, rows, :] + gx) * w
        q = prv[rows, :]
        gz = (u - q) * keep_prev
        gy = jnp.where(row_ok, below(q, prv[later, :]) - q, 0.0)
        gx = jnp.where(col_ok, right_of(q) - q, 0.0)
        dq = (dual[3, rows, :] + gz) * weight(gz, gy, gx)
        div = (dz - dq) + (dy - above(dy, before)) + (dx - left_of(dx))
        main = pl.ds(pl.multiple_of(t * 8 - 8, 8), 8)
        denoised = parts[main, :] - strength * div
        out_ref[0, 0, main, :] = (
            (1.0 - ALPHA_TWIST) * x_prev[0, 0, main, :]
            + (ALPHA_TWIST - BETA_TWIST) * x_now[0, 0, main, :]
            + BETA_TWIST * denoised
        )
        return dy

    lax.fori_loop(1, TILES - 1, tile, first)


def tv_second(comp, numbers, place, own, nxt, prv, dual, parts, x_prev, x_now, into):
    smem = pl.BlockSpec(memory_space=pltpu.SMEM)
    anywhere = pl.BlockSpec(memory_space=pl.ANY)
    block = pl.BlockSpec((1, 1, ROWS, N), lambda i: (comp, 0, 0, 0))
    args = [numbers, place, own, nxt, prv, dual, parts, x_prev, x_now]
    specs = [
        smem,
        smem,
        whole((EXT, N)),
        whole((EXT, N)),
        whole((EXT, N)),
        whole((4, EXT, N)),
        whole((ROWS, N)),
        block,
        block,
    ]
    aliases = {}
    if into is not None:
        args.append(into)
        specs.append(anywhere)
        aliases = {len(args) - 1: 0}
    return pl.pallas_call(
        functools.partial(tv_second_body, comp),
        grid=(1,),
        in_specs=specs,
        out_specs=block,
        out_shape=jax.ShapeDtypeStruct((2, 1, ROWS, N), F32),
        input_output_aliases=aliases,
        compiler_params=params(60),
        cost_estimate=pl.CostEstimate(
            flops=10**8, bytes_accessed=23 * MIB, transcendentals=2 * 10**6
        ),
        name="tv_second",
    )(*args)


def from_behind(x, axis, by):
    count = lax.axis_size(axis)
    pairs = [(i, i + by) for i in range(count) if 0 <= i + by < count]
    return lax.ppermute(x, axis, pairs)


def swap_sum(x, axis, bits):
    count = lax.axis_size(axis)
    for bit in bits:
        x = x + lax.ppermute(x, axis, [(i, i ^ bit) for i in range(count)])
    return x


def signed_freq(freq):
    signed = jnp.where(freq < N // 2, freq, freq - N)
    return signed.astype(F32) * (2.0 * math.pi / N)


def phase_rate(qx_grid, qy_grid):
    square = qx_grid * qx_grid + qy_grid * qy_grid
    return -square / (WAVENUMBER + jnp.sqrt(WAVENUMBER * WAVENUMBER - square))


def shards(x_now, x_prev, hologram, depths):
    d = lax.axis_index("depth")
    r = lax.axis_index("rows")
    forward, inverse = dft_blocks(1.0 / math.sqrt(N))
    g_high, g_low = split_np(forward)
    i_high, i_low = split_np(inverse)
    p_high, p_low = split_np(inverse / PLANES)
    t_high, t_low = split_np(forward.T)
    pick = np.stack([t_high, t_low]).reshape(2, 2, 16, 16, 2 * PART)
    pick = np.ascontiguousarray(pick.transpose(2, 0, 1, 3, 4)).reshape(16, 2, 32, 2 * PART)
    tw = jnp.asarray(twiddles())

    chosen = lax.dynamic_index_in_dim(jnp.asarray(pick), d, 0, keepdims=False)
    holo = holo_forward(hologram, chosen[0], chosen[1], tw)
    holo = lax.all_to_all(holo, "rows", 0, 0, tiled=True)

    lane = lax.broadcasted_iota(jnp.int32, (1, 128), 1)
    depth_all = swap_sum(jnp.where(lane == d, depths[0], 0.0), "depth", (1, 2, 4, 8))
    kx = r + RADIX * (16 * d + jnp.arange(16, dtype=jnp.int32))
    ky = (
        jnp.arange(RADIX, dtype=jnp.int32)[:, None]
        + RADIX * jnp.arange(PART, dtype=jnp.int32)[None, :]
    )
    rate = phase_rate(signed_freq(kx)[None, :, None], signed_freq(ky)[:, None, :])
    trans = transfer(depth_all, rate)

    sent, squares = rows_forward(x_now, jnp.asarray(t_high), jnp.asarray(t_low), tw)
    both = ("rows", "depth")
    got = lax.all_to_all(sent.reshape(128, 2, 16, ROWS), both, 0, 0, tiled=True)
    back, cross = spectral(
        got.reshape(RADIX, PLANES, 2, 16, ROWS),
        holo,
        trans,
        jnp.asarray(g_high),
        jnp.asarray(g_low),
        jnp.asarray(i_high),
        jnp.asarray(i_low),
        tw,
    )
    ret = lax.all_to_all(back.reshape(128, 2, 16, ROWS), both, 0, 0, tiled=True)

    total = jnp.sum(squares) + jnp.sum(cross) / PLANES
    total = jnp.full((1, 128), total)
    total = swap_sum(swap_sum(total, "rows", (1, 2, 4)), "depth", (1, 2, 4, 8))[0, 0]
    mean_square = jnp.maximum(total, 0.0) / (2.0 * PLANES * N * N)
    strength = LAMBDA_TV * jnp.sqrt(mean_square + EPSILON)
    numbers = jnp.stack(
        [
            -STEP_TV / strength,
            -1.0 / strength,
            (d < PLANES - 1).astype(F32),
            (d > 0).astype(F32),
            strength,
        ]
    )
    place = jnp.stack([r * ROWS])

    re, im, top, bot = rows_back(
        ret.reshape(RADIX, PLANES, 2, 16, ROWS), x_now, jnp.asarray(p_high), jnp.asarray(p_low), tw
    )
    own = (re, im)
    halo = jnp.stack([from_behind(bot, "rows", 1), from_behind(top, "rows", -1)])
    nxt = [from_behind(own[0], "depth", -1)]
    prv = [from_behind(own[0], "depth", 1)]
    halo_next = from_behind(halo, "depth", -1)
    halo_prev = from_behind(halo, "depth", 1)
    nxt.append(from_behind(own[1], "depth", -1))
    prv.append(from_behind(own[1], "depth", 1))

    out = None
    firsts = [
        tv_first(c, numbers, place, own[c], nxt[c], prv[c], halo, halo_next, halo_prev)
        for c in range(2)
    ]
    for c in range(2):
        inner, dual = firsts[c]
        out = tv_second(
            c,
            numbers,
            place,
            inner,
            from_behind(inner, "depth", -1),
            from_behind(inner, "depth", 1),
            dual,
            own[c],
            x_prev,
            x_now,
            out,
        )
    return out


def solution(mesh):
    return jax.shard_map(
        shards,
        mesh=mesh,
        in_specs=(
            P(None, "depth", "rows", None),
            P(None, "depth", "rows", None),
            P(None, "rows", None),
            P("depth"),
        ),
        out_specs=P(None, "depth", "rows", None),
        check_vma=False,
    )
```

```python
import functools
import math

import jax
import jax.numpy as jnp
import ml_dtypes
import numpy as np
from jax import lax
from jax.experimental import pallas as pl
from jax.experimental.pallas import tpu as pltpu
from jax.sharding import PartitionSpec as P

ALPHA_TWIST = 1.8
BETA_TWIST = 1.2
LAMBDA_TV = 0.2
STEP_TV = 1.0 / 12.0
EPSILON = 1e-06
WAVENUMBER = 4.0 * math.pi

N = 2048
PLANES = 16
ROWS = 256
RADIX = 8
PART = 256
EXT = ROWS + 16
F32 = jnp.float32
BF16 = jnp.bfloat16
MIB = 1024 * 1024


def split_np(table):
    high = table.astype(np.float32).astype(ml_dtypes.bfloat16)
    low = (table - high.astype(np.float64)).astype(np.float32).astype(ml_dtypes.bfloat16)
    return high, low


def dft_blocks(scale):
    index = np.arange(PART)
    angle = 2.0 * np.pi * ((index[:, None] * index[None, :]) % PART) / PART
    cos = np.cos(angle) * scale
    sin = np.sin(angle) * scale
    forward = np.block([[cos, -sin], [sin, cos]])
    inverse = np.block([[cos, sin], [-sin, cos]])
    return forward, inverse


def twiddles():
    index = np.arange(PART)
    angle = 2.0 * np.pi * (np.arange(RADIX)[:, None] * index[None, :]) / N
    return np.stack([np.cos(angle), -np.sin(angle)], axis=1).astype(np.float32)


def dft4(a, b, c, d, sign):
    t0 = (a[0] + c[0], a[1] + c[1])
    t1 = (a[0] - c[0], a[1] - c[1])
    t2 = (b[0] + d[0], b[1] + d[1])
    t3 = (b[0] - d[0], b[1] - d[1])
    if sign > 0:
        turned = (-t3[1], t3[0])
    else:
        turned = (t3[1], -t3[0])
    return (
        (t0[0] + t2[0], t0[1] + t2[1]),
        (t1[0] + turned[0], t1[1] + turned[1]),
        (t0[0] - t2[0], t0[1] - t2[1]),
        (t1[0] - turned[0], t1[1] - turned[1]),
    )


def dft8(v, sign):
    even = dft4(v[0], v[2], v[4], v[6], sign)
    odd = dft4(v[1], v[3], v[5], v[7], sign)
    half = math.sqrt(0.5)
    o1, o2, o3 = odd[1], odd[2], odd[3]
    if sign > 0:
        w1 = ((o1[0] - o1[1]) * half, (o1[0] + o1[1]) * half)
        w2 = (-o2[1], o2[0])
        w3 = ((-o3[0] - o3[1]) * half, (o3[0] - o3[1]) * half)
    else:
        w1 = ((o1[0] + o1[1]) * half, (o1[1] - o1[0]) * half)
        w2 = (o2[1], -o2[0])
        w3 = ((o3[1] - o3[0]) * half, (-o3[0] - o3[1]) * half)
    turned = (odd[0], w1, w2, w3)
    low = [(even[k][0] + turned[k][0], even[k][1] + turned[k][1]) for k in range(4)]
    high = [(even[k][0] - turned[k][0], even[k][1] - turned[k][1]) for k in range(4)]
    return low + high


def split(x):
    high = x.astype(BF16)
    return high, (x - high.astype(F32)).astype(BF16)


def dot(a, b, contract):
    return lax.dot_general(a, b, (contract, ((), ())), preferred_element_type=F32)


def dot3(a_high, a_low, b_high, b_low, contract):
    return (
        dot(a_high, b_high, contract) + dot(a_high, b_low, contract) + dot(a_low, b_high, contract)
    )


NT = ((1,), (1,))
NN = ((1,), (0,))


def forward_radix(load, tw_ref, hi, lo, rows, half):
    lanes = slice(half * 128, half * 128 + 128)
    out = dft8([load(i) for i in range(RADIX)], -1)
    for k in range(RADIX):
        re, im = out[k]
        if k:
            c = tw_ref[k, 0:1, lanes]
            s = tw_ref[k, 1:2, lanes]
            re, im = re * c - im * s, re * s + im * c
        for part, value in ((0, re), (1, im)):
            high, low = split(value)
            at = slice(part * PART + half * 128, part * PART + half * 128 + 128)
            hi[k, rows, at] = high
            lo[k, rows, at] = low


def params(limit_mib):
    return pltpu.CompilerParams(vmem_limit_bytes=limit_mib * MIB)


def whole(shape):
    return pl.BlockSpec(shape, lambda *_: (0,) * len(shape))


def rows_body(x_ref, gh_ref, gl_ref, tw_ref, y_ref, ss_ref, hi, lo):
    k = pl.program_id(0)

    @pl.when(k == 0)
    def _():
        def chunk(t, total):
            rows = pl.ds(pl.multiple_of(t * 16, 16), 16)
            for half in range(2):

                def load(i):
                    at = slice(i * PART + half * 128, i * PART + half * 128 + 128)
                    return (x_ref[0, 0, rows, at], x_ref[1, 0, rows, at])

                patches = [load(i) for i in range(RADIX)]
                for re, im in patches:
                    total = total + (re * re + im * im)
                forward_radix(lambda i: patches[i], tw_ref, hi, lo, rows, half)
            return total

        ss_ref[...] = lax.fori_loop(0, ROWS // 16, chunk, jnp.zeros((16, 128), F32))

    gh, gl = gh_ref, gl_ref
    high, low = hi[k], lo[k]
    for part in range(2):
        at = slice(part * PART, part * PART + PART)
        out = dot3(gh[at, :], gl[at, :], high, low, NT)
        y_ref[0, :, part] = out.reshape(16, 16, ROWS)


def rows_forward(x_now, gt_high, gt_low, tw):
    return pl.pallas_call(
        rows_body,
        grid=(RADIX,),
        in_specs=[
            whole((2, 1, ROWS, N)),
            whole((2 * PART, 2 * PART)),
            whole((2 * PART, 2 * PART)),
            whole((RADIX, 2, PART)),
        ],
        out_specs=[
            pl.BlockSpec((1, 16, 2, 16, ROWS), lambda k: (k, 0, 0, 0, 0)),
            whole((16, 128)),
        ],
        out_shape=[
            jax.ShapeDtypeStruct((RADIX, 16, 2, 16, ROWS), F32),
            jax.ShapeDtypeStruct((16, 128), F32),
        ],
        scratch_shapes=[
            pltpu.VMEM((RADIX, ROWS, 2 * PART), BF16),
            pltpu.VMEM((RADIX, ROWS, 2 * PART), BF16),
        ],
        compiler_params=params(62),
        cost_estimate=pl.CostEstimate(
            flops=4 * 10**9, bytes_accessed=10 * MIB, transcendentals=0
        ),
        name="rows_forward",
    )(x_now, gt_high, gt_low, tw)


def holo_body(depth_ref, x_ref, gh_ref, gl_ref, tw_ref, y_ref, hi, lo):
    def chunk(t, carry):
        rows = pl.ds(pl.multiple_of(t * 16, 16), 16)
        for half in range(2):

            def load(i):
                at = slice(i * PART + half * 128, i * PART + half * 128 + 128)
                return (x_ref[0, rows, at], x_ref[1, rows, at])

            forward_radix(load, tw_ref, hi, lo, rows, half)
        return carry

    lax.fori_loop(0, ROWS // 16, chunk, 0)
    y_ref[...] = jnp.full(y_ref.shape, depth_ref[0], F32)

    def per_k(k, carry):
        out = dot3(gh_ref[...], gl_ref[...], hi[k], lo[k], NT)
        for part in range(2):
            for half in range(2):
                y_ref[k, :, part * 2 + half, :] = out[
                    part * 16 : part * 16 + 16, half * 128 : half * 128 + 128
                ]
        return carry

    lax.fori_loop(0, RADIX, per_k, 0)


def holo_forward(depths, hologram, gt_high, gt_low, tw):
    return pl.pallas_call(
        holo_body,
        out_shape=jax.ShapeDtypeStruct((RADIX, 16, 8, 128), F32),
        scratch_shapes=[
            pltpu.VMEM((RADIX, ROWS, 2 * PART), BF16),
            pltpu.VMEM((RADIX, ROWS, 2 * PART), BF16),
        ],
        in_specs=[pl.BlockSpec(memory_space=pltpu.SMEM)]
        + [pl.BlockSpec(memory_space=pltpu.VMEM)] * 4,
        out_specs=pl.BlockSpec(memory_space=pltpu.VMEM),
        compiler_params=params(62),
        cost_estimate=pl.CostEstimate(
            flops=4 * 10**8, bytes_accessed=5 * MIB, transcendentals=0
        ),
        name="holo_forward",
    )(depths, hologram, gt_high, gt_low, tw)


def cos_sin(phase):
    turns = jnp.floor(phase * (2.0 / math.pi) + 0.5)
    rest = phase - turns * 1.5703125
    rest = rest - turns * 4.837512969970703e-4
    rest = rest - turns * 7.549789948768648e-8
    z = rest * rest
    sin = rest + rest * z * (
        -1.6666654611e-1 + z * (8.3321608736e-3 + z * -1.9515295891e-4)
    )
    cos = (
        1.0
        - 0.5 * z
        + z
        * z
        * (4.166664568298827e-2 + z * (-1.388731625493765e-3 + z * 2.443315711809948e-5))
    )
    quarter = turns.astype(jnp.int32) & 3
    odd = (quarter & 1) == 1
    base_cos = jnp.where(odd, sin, cos)
    base_sin = jnp.where(odd, cos, sin)
    out_cos = jnp.where((quarter == 1) | (quarter == 2), -base_cos, base_cos)
    out_sin = jnp.where(quarter >= 2, -base_sin, base_sin)
    return out_cos, out_sin


def transfer_body(depth_ref, rate_ref, t_ref):
    rate = rate_ref[0]
    for p in range(PLANES):
        cos, sin = cos_sin(depth_ref[0, p] * rate)
        rows = slice(p * 16, p * 16 + 16)
        t_ref[0, 0, rows, :] = cos
        t_ref[0, 1, rows, :] = sin


def transfer(depth_all, rate):
    return pl.pallas_call(
        transfer_body,
        grid=(RADIX,),
        in_specs=[
            pl.BlockSpec(memory_space=pltpu.SMEM),
            pl.BlockSpec((1, 16, PART), lambda k: (k, 0, 0)),
        ],
        out_specs=pl.BlockSpec((1, 2, PLANES * 16, PART), lambda k: (k, 0, 0, 0)),
        out_shape=jax.ShapeDtypeStruct((RADIX, 2, PLANES * 16, PART), F32),
        compiler_params=params(62),
        cost_estimate=pl.CostEstimate(
            flops=10**7, bytes_accessed=4 * MIB, transcendentals=0
        ),
        name="transfer",
    )(depth_all, rate)


COLS = PLANES * 16
MESSAGE = 72
WITH_HOLO = COLS + 16


def spectral_body(
    z_ref, h_ref, t_ref, sq_ref, gh_ref, gl_ref, ih_ref, il_ref, tw_ref, o_ref, norm_ref,
    hi, lo, spec, bhi, blo, back,
):
    k = pl.program_id(0)

    @pl.when(k == 0)
    def _():
        norm_ref[...] = jnp.zeros_like(norm_ref)

        def chunk(p, carry):
            rows = pl.ds(pl.multiple_of(p * 16, 16), 16)
            for half in range(2):
                at = slice(half * 128, half * 128 + 128)

                def load(i):
                    return (z_ref[i, p, 0, :, at], z_ref[i, p, 1, :, at])

                forward_radix(load, tw_ref, hi, lo, rows, half)
            return carry

        lax.fori_loop(0, PLANES, chunk, 0)
        for half in range(2):

            def load_holo(i):
                return (h_ref[i, :, half, :], h_ref[i, :, 2 + half, :])

            forward_radix(load_holo, tw_ref, hi, lo, slice(COLS, WITH_HOLO), half)

    spec[...] = dot3(hi[k], lo[k], gh_ref[...], gl_ref[...], NN)

    for half in range(2):
        at = slice(half * 128, half * 128 + 128)
        at_im = slice(PART + half * 128, PART + half * 128 + 128)

        def gather(p, total):
            rows = pl.ds(pl.multiple_of(p * 16, 16), 16)
            xr, xi = spec[rows, at], spec[rows, at_im]
            tr, ti = t_ref[0, 0, rows, at], t_ref[0, 1, rows, at]
            return (total[0] + (tr * xr - ti * xi), total[1] + (tr * xi + ti * xr))

        zero = jnp.zeros((16, 128), F32)
        pred = lax.fori_loop(0, PLANES, gather, (zero, zero), unroll=4)
        holo = (spec[COLS:WITH_HOLO, at], spec[COLS:WITH_HOLO, at_im])
        res = (holo[0] - pred[0], holo[1] - pred[1])
        norm_ref[...] += res[0] * (holo[0] + pred[0]) + res[1] * (holo[1] + pred[1])

        def scatter(p, carry):
            rows = pl.ds(pl.multiple_of(p * 16, 16), 16)
            tr, ti = t_ref[0, 0, rows, at], t_ref[0, 1, rows, at]
            br = tr * res[0] + ti * res[1]
            bi = tr * res[1] - ti * res[0]
            for where, value in ((at, br), (at_im, bi)):
                high, low = split(value)
                bhi[rows, where] = high
                blo[rows, where] = low
            return carry

        lax.fori_loop(0, PLANES, scatter, 0, unroll=4)

    c = tw_ref[k, 0:1, :]
    s = tw_ref[k, 1:2, :]
    out = dot3(bhi[...], blo[...], ih_ref[...], il_ref[...], NN)
    re, im = out[:, :PART], out[:, PART:]
    back[k, 0] = re * c + im * s
    back[k, 1] = im * c - re * s

    @pl.when(k == RADIX - 1)
    def _():
        square = sq_ref[...] + norm_ref[...] * (1.0 / PLANES)
        square = square[:8, :] + square[8:, :]

        def chunk(p, carry):
            rows = pl.ds(pl.multiple_of(p * 16, 16), 16)
            for i in range(RADIX):
                o_ref[i, p, 64:MESSAGE, :] = square
            for half in range(2):
                at = slice(half * 128, half * 128 + 128)
                out = dft8([(back[i, 0, rows, at], back[i, 1, rows, at]) for i in range(RADIX)], 1)
                for i in range(RADIX):
                    o_ref[i, p, half * 16 : half * 16 + 16, :] = out[i][0]
                    o_ref[i, p, half * 16 + 32 : half * 16 + 48, :] = out[i][1]
            return carry

        lax.fori_loop(0, PLANES, chunk, 0)


def spectral(z, holo, trans, squares, g_high, g_low, i_high, i_low, tw):
    table = whole((2 * PART, 2 * PART))
    return pl.pallas_call(
        spectral_body,
        grid=(RADIX,),
        in_specs=[
            whole((RADIX, PLANES, 2, 16, PART)),
            whole((RADIX, 16, 8, 128)),
            pl.BlockSpec((1, 2, COLS, PART), lambda k: (k, 0, 0, 0)),
            whole((16, 128)),
            table,
            table,
            table,
            table,
            whole((RADIX, 2, PART)),
        ],
        out_specs=whole((RADIX, PLANES, MESSAGE, 128)),
        out_shape=jax.ShapeDtypeStruct((RADIX, PLANES, MESSAGE, 128), F32),
        scratch_shapes=[
            pltpu.VMEM((16, 128), F32),
            pltpu.VMEM((RADIX, WITH_HOLO, 2 * PART), BF16),
            pltpu.VMEM((RADIX, WITH_HOLO, 2 * PART), BF16),
            pltpu.VMEM((WITH_HOLO, 2 * PART), F32),
            pltpu.VMEM((COLS, 2 * PART), BF16),
            pltpu.VMEM((COLS, 2 * PART), BF16),
            pltpu.VMEM((RADIX, 2, COLS, PART), F32),
        ],
        compiler_params=params(62),
        cost_estimate=pl.CostEstimate(
            flops=8 * 10**9, bytes_accessed=14 * MIB, transcendentals=0
        ),
        name="spectral",
    )(z, holo, trans, squares, g_high, g_low, i_high, i_low, tw)


def rows_back_body(
    w_ref, x_ref, ih_ref, il_ref, tw_ref, re_ref, im_ref, top_ref, bot_ref, sum_ref, back
):
    k = pl.program_id(0)
    @pl.when(k == 0)
    def _():
        sum_ref[...] = jnp.zeros_like(sum_ref)

    sum_ref[...] += jnp.sum(w_ref[0, :, 64:MESSAGE, :], axis=0)
    parts = []
    for c in range(2):
        halves = [w_ref[0, :, c * 32 + h * 16 : c * 32 + h * 16 + 16, :] for h in range(2)]
        parts.append(jnp.concatenate([h.reshape(PART, 128).T for h in halves], axis=0))
    high, low = split(jnp.concatenate(parts, axis=1))
    out = dot3(high, low, ih_ref[...], il_ref[...], NN)
    c = tw_ref[k, 0:1, :]
    s = tw_ref[k, 1:2, :]
    re, im = out[:, :PART], out[:, PART:]
    back[k, 0] = re * c + im * s
    back[k, 1] = im * c - re * s

    @pl.when(k == RADIX - 1)
    def _():
        def chunk(t, carry):
            rows = pl.ds(pl.multiple_of(t * 16, 16), 16)
            for half in range(2):
                at = slice(half * 128, half * 128 + 128)
                out = dft8([(back[i, 0, rows, at], back[i, 1, rows, at]) for i in range(RADIX)], 1)
                for i in range(RADIX):
                    to = slice(i * PART + half * 128, i * PART + half * 128 + 128)
                    re_ref[rows, to] = x_ref[0, 0, rows, to] + out[i][0]
                    im_ref[rows, to] = x_ref[1, 0, rows, to] + out[i][1]
            return carry

        lax.fori_loop(0, ROWS // 16, chunk, 0)
        top_ref[0] = re_ref[0:8, :]
        top_ref[1] = im_ref[0:8, :]
        bot_ref[0] = re_ref[ROWS - 8 : ROWS, :]
        bot_ref[1] = im_ref[ROWS - 8 : ROWS, :]


def rows_back(w, x_now, i_high, i_low, tw):
    table = whole((2 * PART, 2 * PART))
    return pl.pallas_call(
        rows_back_body,
        grid=(RADIX,),
        in_specs=[
            pl.BlockSpec((1, 16, MESSAGE, 128), lambda k: (k, 0, 0, 0)),
            whole((2, 1, ROWS, N)),
            table,
            table,
            whole((RADIX, 2, PART)),
        ],
        out_specs=[
            whole((ROWS, N)),
            whole((ROWS, N)),
            whole((2, 8, N)),
            whole((2, 8, N)),
            whole((8, 128)),
        ],
        out_shape=[
            jax.ShapeDtypeStruct((ROWS, N), F32),
            jax.ShapeDtypeStruct((ROWS, N), F32),
            jax.ShapeDtypeStruct((2, 8, N), F32),
            jax.ShapeDtypeStruct((2, 8, N), F32),
            jax.ShapeDtypeStruct((8, 128), F32),
        ],
        scratch_shapes=[pltpu.VMEM((RADIX, 2, ROWS, PART), F32)],
        compiler_params=params(62),
        cost_estimate=pl.CostEstimate(
            flops=4 * 10**9, bytes_accessed=13 * MIB, transcendentals=0
        ),
        name="rows_back",
    )(w, x_now, i_high, i_low, tw)


TILES = EXT // 8
WIDE = 512
STAGES = 4


def shift_up(x, after):
    row = lax.broadcasted_iota(jnp.int32, x.shape, 0)
    return pltpu.roll(jnp.where(row == 0, after, x), 7, 0)


def shift_down(x, before):
    row = lax.broadcasted_iota(jnp.int32, x.shape, 0)
    return pltpu.roll(jnp.where(row == 7, before, x), 1, 0)


def from_right(x, after):
    if after is None:
        col = lax.broadcasted_iota(jnp.int32, x.shape, 1)
        return jnp.where(col == WIDE - 1, x, pltpu.roll(x, WIDE - 1, 1))
    return pltpu.roll(jnp.concatenate([x, after], axis=1), WIDE + 127, 1)[:, :WIDE]


def from_left(x, before):
    if before is None:
        col = lax.broadcasted_iota(jnp.int32, x.shape, 1)
        return jnp.where(col == 0, 0.0, pltpu.roll(x, 1, 1))
    return pltpu.roll(jnp.concatenate([before, x], axis=1), 1, 1)[:, 128:]


def reciprocal(x):
    guess = pl.reciprocal(x, approx=True)
    return guess * (2.0 - x * guess)


def norm(gz, gy, gx):
    square = gz * gz + gy * gy + gx * gx
    return square * lax.rsqrt(square + 1e-30)


def patch(ref, lead, rows, start):
    at = slice(start, start + WIDE)
    after = None
    if start + WIDE < N:
        after = ref[lead + (rows, slice(start + WIDE, start + WIDE + 128))]
    return ref[lead + (rows, at)], after


def tv_first_body(
    comp, num_ref, at_ref, own, nxt, prv, own_h, nxt_h, prv_h, inner_out, dual_out,
    ext, inner, dual, in_sems, halo_sems, out_sems,
):
    size = ROWS // STAGES
    mains = []
    halos = []
    for which, (main, halo) in enumerate(((own, own_h), (nxt, nxt_h), (prv, prv_h))):
        mains.append(
            [
                pltpu.make_async_copy(
                    main.at[pl.ds(q * size, size), :],
                    ext.at[which, pl.ds(8 + q * size, size), :],
                    in_sems.at[which, q],
                )
                for q in range(STAGES)
            ]
        )
        halos.append(
            [
                pltpu.make_async_copy(
                    halo.at[end, comp],
                    ext.at[which, pl.ds(end * (ROWS + 8), 8), :],
                    halo_sems.at[which, end],
                )
                for end in range(2)
            ]
        )
    for q in range(STAGES):
        for which in range(3):
            if q == 0:
                halos[which][0].start()
            mains[which][q].start()
            if q == STAGES - 1:
                halos[which][1].start()
    scale = num_ref[0]
    inverse = num_ref[1]
    size_of = num_ref[5]
    keep_next = num_ref[2]
    keep_prev = num_ref[3]
    band = at_ref[0]

    def tile(t, carry):
        rows = pl.ds(pl.multiple_of(t * 8, 8), 8)
        later = pl.ds(pl.multiple_of(jnp.minimum(t + 1, TILES - 1) * 8, 8), 8)
        earlier = pl.ds(pl.multiple_of(jnp.maximum(t - 1, 0) * 8, 8), 8)
        left = None
        for start in range(0, N, WIDE):
            at = slice(start, start + WIDE)
            u, u_after = patch(ext, (0,), rows, start)
            q, q_after = patch(ext, (2,), rows, start)
            gz = (ext[1, rows, at] - u) * keep_next
            gy = shift_up(u, ext[0, later, at]) - u
            gx = from_right(u, u_after) - u
            w = scale * reciprocal(1.0 + size_of * norm(gz, gy, gx))
            dz, dy, dx = gz * w, gy * w, gx * w
            gz = (u - q) * keep_prev
            gy = shift_up(q, ext[2, later, at]) - q
            gx = from_right(q, q_after) - q
            dq = gz * (scale * reciprocal(1.0 + size_of * norm(gz, gy, gx)))
            above = shift_down(dy, dual[1, earlier, at])
            div = (dz - dq) + (dy - above) + (dx - from_left(dx, left))
            left = dx[:, WIDE - 128 :]
            inner[rows, at] = (div + u * inverse) * STEP_TV
            dual[0, rows, at] = dz
            dual[1, rows, at] = dy
            dual[2, rows, at] = dx
            dual[3, rows, at] = dq
        return carry

    outs = []
    done = 0
    for q in range(STAGES):
        for which in range(3):
            if q == 0:
                halos[which][0].wait()
            mains[which][q].wait()
            if q == STAGES - 1:
                halos[which][1].wait()
        if q == 0:

            @pl.when(band == 0)
            def _():
                for which in range(3):
                    ext[which, 7:8, :] = ext[which, 8:9, :]

        if q == STAGES - 1:

            @pl.when(band == N // ROWS - 1)
            def _():
                for which in range(3):
                    ext[which, ROWS + 8 : ROWS + 9, :] = ext[which, ROWS + 7 : ROWS + 8, :]

        upto = TILES if q == STAGES - 1 else (q + 1) * size // 8
        lax.fori_loop(done, upto, tile, 0)
        if q == 0:

            @pl.when(band == 0)
            def _():
                inner[7:8, :] = inner[8:9, :]

        if q == STAGES - 1:

            @pl.when(band == N // ROWS - 1)
            def _():
                inner[ROWS + 8 : ROWS + 9, :] = inner[ROWS + 7 : ROWS + 8, :]

        span = pl.ds(done * 8, (upto - done) * 8)
        outs += [
            pltpu.make_async_copy(inner.at[span, :], inner_out.at[span, :], out_sems.at[0, q]),
            pltpu.make_async_copy(dual.at[:, span, :], dual_out.at[:, span, :], out_sems.at[1, q]),
        ]
        outs[-2].start()
        outs[-1].start()
        done = upto
    for copy in outs:
        copy.wait()


def tv_first(comp, numbers, place, own, nxt, prv, own_h, nxt_h, prv_h):
    smem = pl.BlockSpec(memory_space=pltpu.SMEM)
    anywhere = pl.BlockSpec(memory_space=pl.ANY)
    return pl.pallas_call(
        functools.partial(tv_first_body, comp),
        in_specs=[smem, smem] + [anywhere] * 6,
        out_specs=[anywhere, anywhere],
        out_shape=[
            jax.ShapeDtypeStruct((EXT, N), F32),
            jax.ShapeDtypeStruct((4, EXT, N), F32),
        ],
        scratch_shapes=[
            pltpu.VMEM((3, EXT, N), F32),
            pltpu.VMEM((EXT, N), F32),
            pltpu.VMEM((4, EXT, N), F32),
            pltpu.SemaphoreType.DMA((3, STAGES)),
            pltpu.SemaphoreType.DMA((3, 2)),
            pltpu.SemaphoreType.DMA((2, STAGES)),
        ],
        compiler_params=params(62),
        cost_estimate=pl.CostEstimate(
            flops=10**8, bytes_accessed=17 * MIB, transcendentals=2 * 10**6
        ),
        name="tv_first",
    )(numbers, place, own, nxt, prv, own_h, nxt_h, prv_h)


def tv_second_body(
    comp, num_ref, own_in, nxt_in, prv_in, dual_in, parts_in, x_prev_in, x_now_in, *rest
):
    out_ref, inner, dual, plain, below, sems, out_sems = rest[-7:]
    size = ROWS // STAGES
    copies = []
    for q in range(STAGES):
        first = 0 if q == 0 else q * size + 16
        span = pl.ds(first, (q + 1) * size + 16 - first)
        main = pl.ds(q * size, size)
        pairs = [(ref.at[span, :], inner.at[i, span, :]) for i, ref in enumerate((own_in, nxt_in, prv_in))]
        pairs += [
            (dual_in.at[:, span, :], dual.at[:, span, :]),
            (parts_in.at[main, :], plain.at[0, main, :]),
            (x_prev_in.at[comp, 0, main, :], plain.at[1, main, :]),
            (x_now_in.at[comp, 0, main, :], plain.at[2, main, :]),
        ]
        copies.append(
            [pltpu.make_async_copy(a, b, sems.at[i, q]) for i, (a, b) in enumerate(pairs)]
        )
        for copy in copies[-1]:
            copy.start()
    strength = num_ref[4]
    keep_next = num_ref[2]
    keep_prev = num_ref[3]

    def tile(t, carry):
        rows = pl.ds(pl.multiple_of(t * 8, 8), 8)
        later = pl.ds(pl.multiple_of(t * 8 + 8, 8), 8)
        main = pl.ds(pl.multiple_of(jnp.maximum(t - 1, 0) * 8, 8), 8)
        left = None
        for start in range(0, N, WIDE):
            at = slice(start, start + WIDE)
            u, u_after = patch(inner, (0,), rows, start)
            q, q_after = patch(inner, (2,), rows, start)
            gz = (inner[1, rows, at] - u) * keep_next
            gy = shift_up(u, inner[0, later, at]) - u
            gx = from_right(u, u_after) - u
            w = reciprocal(1.0 + norm(gz, gy, gx))
            dz = (dual[0, rows, at] + gz) * w
            dy = (dual[1, rows, at] + gy) * w
            dx = (dual[2, rows, at] + gx) * w
            gz = (u - q) * keep_prev
            gy = shift_up(q, inner[2, later, at]) - q
            gx = from_right(q, q_after) - q
            dq = (dual[3, rows, at] + gz) * reciprocal(1.0 + norm(gz, gy, gx))
            above = shift_down(dy, below[:, at])
            below[:, at] = dy
            div = (dz - dq) + (dy - above) + (dx - from_left(dx, left))
            left = dx[:, WIDE - 128 :]
            denoised = plain[0, main, at] - strength * div
            plain[1, main, at] = (
                (1.0 - ALPHA_TWIST) * plain[1, main, at]
                + (ALPHA_TWIST - BETA_TWIST) * plain[2, main, at]
                + BETA_TWIST * denoised
            )
        return carry

    def first_rows(start):
        at = slice(start, start + WIDE)
        u, u_after = patch(inner, (0,), slice(0, 8), start)
        gz = (inner[1, 0:8, at] - u) * keep_next
        gy = shift_up(u, inner[0, 8:16, at]) - u
        gx = from_right(u, u_after) - u
        below[:, at] = (dual[1, 0:8, at] + gy) * reciprocal(1.0 + norm(gz, gy, gx))

    outs = []
    for q in range(STAGES):
        for copy in copies[q]:
            copy.wait()
        if q == 0:
            for start in range(0, N, WIDE):
                first_rows(start)
        lax.fori_loop(1 + q * size // 8, 1 + (q + 1) * size // 8, tile, 0)
        main = pl.ds(q * size, size)
        outs.append(
            pltpu.make_async_copy(
                plain.at[1, main, :], out_ref.at[comp, 0, main, :], out_sems.at[q]
            )
        )
        outs[-1].start()
    for copy in outs:
        copy.wait()


def tv_second(comp, numbers, own, nxt, prv, dual, parts, x_prev, x_now, into):
    smem = pl.BlockSpec(memory_space=pltpu.SMEM)
    anywhere = pl.BlockSpec(memory_space=pl.ANY)
    args = [numbers, own, nxt, prv, dual, parts, x_prev, x_now]
    aliases = {}
    if into is not None:
        args.append(into)
        aliases = {len(args) - 1: 0}
    return pl.pallas_call(
        functools.partial(tv_second_body, comp),
        in_specs=[smem] + [anywhere] * (len(args) - 1),
        out_specs=anywhere,
        out_shape=jax.ShapeDtypeStruct((2, 1, ROWS, N), F32),
        scratch_shapes=[
            pltpu.VMEM((3, EXT, N), F32),
            pltpu.VMEM((4, EXT, N), F32),
            pltpu.VMEM((3, ROWS, N), F32),
            pltpu.VMEM((8, N), F32),
            pltpu.SemaphoreType.DMA((7, STAGES)),
            pltpu.SemaphoreType.DMA((STAGES,)),
        ],
        input_output_aliases=aliases,
        compiler_params=params(62),
        cost_estimate=pl.CostEstimate(
            flops=10**8, bytes_accessed=23 * MIB, transcendentals=2 * 10**6
        ),
        name="tv_second",
    )(*args)


def from_behind(x, axis, by):
    count = lax.axis_size(axis)
    pairs = [(i, i + by) for i in range(count) if 0 <= i + by < count]
    return lax.ppermute(x, axis, pairs)


def tie(x, *after):
    return lax.optimization_barrier((x,) + after)[0]


def signed_freq(freq):
    signed = jnp.where(freq < N // 2, freq, freq - N)
    return signed.astype(F32) * (2.0 * math.pi / N)


def phase_rate(qx_grid, qy_grid):
    square = qx_grid * qx_grid + qy_grid * qy_grid
    return -square / (WAVENUMBER + jnp.sqrt(WAVENUMBER * WAVENUMBER - square))


def shards(x_now, x_prev, hologram, depths):
    d = lax.axis_index("depth")
    r = lax.axis_index("rows")
    forward, inverse = dft_blocks(1.0 / math.sqrt(N))
    g_high, g_low = split_np(forward)
    i_high, i_low = split_np(inverse)
    p_high, p_low = split_np(inverse / PLANES)
    t_high, t_low = split_np(forward.T)
    pick = np.stack([t_high, t_low]).reshape(2, 2, 16, 16, 2 * PART)
    pick = np.ascontiguousarray(pick.transpose(3, 0, 1, 2, 4)).reshape(16, 2, 32, 2 * PART)
    tw = jnp.asarray(twiddles())
    both = ("rows", "depth")

    chosen = lax.dynamic_index_in_dim(jnp.asarray(pick), d, 0, keepdims=False)
    holo = holo_forward(depths, hologram, chosen[0], chosen[1], tw)
    holo = lax.all_to_all(holo.reshape(128, 8, 128), both, 0, 0, tiled=True)
    depth_all = holo[:PLANES, 4, 0].reshape(1, PLANES)
    kx = r + RADIX * (16 * d + jnp.arange(16, dtype=jnp.int32))
    ky = (
        jnp.arange(RADIX, dtype=jnp.int32)[:, None]
        + RADIX * jnp.arange(PART, dtype=jnp.int32)[None, :]
    )
    rate = phase_rate(signed_freq(kx)[None, :, None], signed_freq(ky)[:, None, :])
    trans = transfer(depth_all, rate)

    sent, squares = rows_forward(x_now, jnp.asarray(t_high), jnp.asarray(t_low), tw)
    got = lax.all_to_all(sent.reshape(128, 2, 16, ROWS), both, 0, 0, tiled=True)
    back = spectral(
        got.reshape(RADIX, PLANES, 2, 16, ROWS),
        holo.reshape(RADIX, PLANES, 8, 128),
        trans,
        squares,
        jnp.asarray(g_high),
        jnp.asarray(g_low),
        jnp.asarray(i_high),
        jnp.asarray(i_low),
        tw,
    )
    ret = lax.all_to_all(back.reshape(128, MESSAGE, 128), both, 0, 0, tiled=True)
    re, im, top, bot, sums = rows_back(
        ret.reshape(RADIX, PLANES, MESSAGE, 128),
        x_now,
        jnp.asarray(p_high),
        jnp.asarray(p_low),
        tw,
    )

    total = jnp.sum(sums)
    mean_square = jnp.maximum(total, 0.0) / (2.0 * PLANES * N * N)
    strength = LAMBDA_TV * jnp.sqrt(mean_square + EPSILON)
    numbers = jnp.stack(
        [
            -STEP_TV / strength,
            -1.0 / strength,
            (d < PLANES - 1).astype(F32),
            (d > 0).astype(F32),
            strength,
            STEP_TV / strength,
        ]
    )
    place = jnp.stack([r])

    halo = jnp.stack([from_behind(bot, "rows", 1), from_behind(top, "rows", -1)])
    own = [re, im]
    nxt = [from_behind(re, "depth", -1)]
    prv = [from_behind(re, "depth", 1)]
    halo_next = from_behind(halo, "depth", -1)
    halo_prev = from_behind(halo, "depth", 1)
    own[1] = tie(im, nxt[0], prv[0], halo_next, halo_prev)
    nxt.append(from_behind(own[1], "depth", -1))
    prv.append(from_behind(own[1], "depth", 1))

    inner_re, dual_re = tv_first(0, numbers, place, re, nxt[0], prv[0], halo, halo_next, halo_prev)
    nxt_re = from_behind(inner_re, "depth", -1)
    prv_re = from_behind(inner_re, "depth", 1)
    inner_im, dual_im = tv_first(
        1, numbers, place, own[1], nxt[1], prv[1], halo, halo_next, halo_prev
    )
    nxt_im = from_behind(inner_im, "depth", -1)
    prv_im = from_behind(inner_im, "depth", 1)
    out = tv_second(
        0, numbers, inner_re, nxt_re, prv_re, dual_re, re, x_prev, x_now, None
    )
    return tv_second(
        1, numbers, inner_im, nxt_im, prv_im, dual_im, own[1], x_prev, x_now, out
    )


def solution(mesh):
    return jax.shard_map(
        shards,
        mesh=mesh,
        in_specs=(
            P(None, "depth", "rows", None),
            P(None, "depth", "rows", None),
            P(None, "rows", None),
            P("depth"),
        ),
        out_specs=P(None, "depth", "rows", None),
        check_vma=False,
    )
```

```python
import functools
import math

import jax
import jax.numpy as jnp
import ml_dtypes
import numpy as np
from jax import lax
from jax.experimental import pallas as pl
from jax.experimental.pallas import tpu as pltpu
from jax.sharding import PartitionSpec as P

ALPHA_TWIST = 1.8
BETA_TWIST = 1.2
LAMBDA_TV = 0.2
STEP_TV = 1.0 / 12.0
EPSILON = 1e-06
WAVENUMBER = 4.0 * math.pi

N = 2048
PLANES = 16
ROWS = 256
RADIX = 8
PART = 256
EXT = ROWS + 16
PACK = ROWS + 8
F32 = jnp.float32
BF16 = jnp.bfloat16
MIB = 1024 * 1024


def split_np(table):
    high = table.astype(np.float32).astype(ml_dtypes.bfloat16)
    low = (table - high.astype(np.float64)).astype(np.float32).astype(ml_dtypes.bfloat16)
    return high, low


def dft_blocks(scale):
    index = np.arange(PART)
    angle = 2.0 * np.pi * ((index[:, None] * index[None, :]) % PART) / PART
    cos = np.cos(angle) * scale
    sin = np.sin(angle) * scale
    forward = np.block([[cos, -sin], [sin, cos]])
    inverse = np.block([[cos, sin], [-sin, cos]])
    return forward, inverse


def halo_table(inverse):
    rows = inverse[:PART].reshape(16, 2, 8, 2 * PART)
    return np.ascontiguousarray(rows.transpose(1, 0, 2, 3)).reshape(PART, 2 * PART)


def twiddles():
    index = np.arange(PART)
    angle = 2.0 * np.pi * (np.arange(RADIX)[:, None] * index[None, :]) / N
    return np.stack([np.cos(angle), -np.sin(angle)], axis=1).astype(np.float32)


def dft4(a, b, c, d, sign):
    t0 = (a[0] + c[0], a[1] + c[1])
    t1 = (a[0] - c[0], a[1] - c[1])
    t2 = (b[0] + d[0], b[1] + d[1])
    t3 = (b[0] - d[0], b[1] - d[1])
    if sign > 0:
        turned = (-t3[1], t3[0])
    else:
        turned = (t3[1], -t3[0])
    return (
        (t0[0] + t2[0], t0[1] + t2[1]),
        (t1[0] + turned[0], t1[1] + turned[1]),
        (t0[0] - t2[0], t0[1] - t2[1]),
        (t1[0] - turned[0], t1[1] - turned[1]),
    )


def dft8(v, sign):
    even = dft4(v[0], v[2], v[4], v[6], sign)
    odd = dft4(v[1], v[3], v[5], v[7], sign)
    half = math.sqrt(0.5)
    o1, o2, o3 = odd[1], odd[2], odd[3]
    if sign > 0:
        w1 = ((o1[0] - o1[1]) * half, (o1[0] + o1[1]) * half)
        w2 = (-o2[1], o2[0])
        w3 = ((-o3[0] - o3[1]) * half, (o3[0] - o3[1]) * half)
    else:
        w1 = ((o1[0] + o1[1]) * half, (o1[1] - o1[0]) * half)
        w2 = (o2[1], -o2[0])
        w3 = ((o3[1] - o3[0]) * half, (-o3[0] - o3[1]) * half)
    turned = (odd[0], w1, w2, w3)
    low = [(even[k][0] + turned[k][0], even[k][1] + turned[k][1]) for k in range(4)]
    high = [(even[k][0] - turned[k][0], even[k][1] - turned[k][1]) for k in range(4)]
    return low + high


def split(x):
    high = x.astype(BF16)
    return high, (x - high.astype(F32)).astype(BF16)


def dot(a, b, contract):
    return lax.dot_general(a, b, (contract, ((), ())), preferred_element_type=F32)


def dot3(a_high, a_low, b_high, b_low, contract):
    return (
        dot(a_high, b_high, contract) + dot(a_high, b_low, contract) + dot(a_low, b_high, contract)
    )


NT = ((1,), (1,))
NN = ((1,), (0,))


def forward_radix(load, tw_ref, hi, lo, rows, half):
    lanes = slice(half * 128, half * 128 + 128)
    out = dft8([load(i) for i in range(RADIX)], -1)
    for k in range(RADIX):
        re, im = out[k]
        if k:
            c = tw_ref[k, 0:1, lanes]
            s = tw_ref[k, 1:2, lanes]
            re, im = re * c - im * s, re * s + im * c
        for part, value in ((0, re), (1, im)):
            high, low = split(value)
            at = slice(part * PART + half * 128, part * PART + half * 128 + 128)
            hi[k, rows, at] = high
            lo[k, rows, at] = low


def params(limit_mib):
    return pltpu.CompilerParams(vmem_limit_bytes=limit_mib * MIB)


def whole(shape):
    return pl.BlockSpec(shape, lambda *_: (0,) * len(shape))


def stage_copies(pairs, sems):
    copies = [pltpu.make_async_copy(a, b, sems.at[i]) for i, (a, b) in enumerate(pairs)]
    for copy in copies:
        copy.start()
    return copies


def quarter(q):
    return pl.ds(q * (ROWS // 4), ROWS // 4)


def rows_body(x_in, g_in, tw_ref, y_ref, ss_ref, hi, lo, x_ref, g_ref, sems):
    k = pl.program_id(0)

    @pl.when(k == 0)
    def _():
        pairs = [(x_in.at[:, :, quarter(q), :], x_ref.at[:, :, quarter(q), :]) for q in range(4)]
        copies = stage_copies(pairs + [(g_in, g_ref)], sems)

        def chunk(t, total):
            rows = pl.ds(pl.multiple_of(t * 16, 16), 16)
            for half in range(2):

                def load(i):
                    at = slice(i * PART + half * 128, i * PART + half * 128 + 128)
                    return (x_ref[0, 0, rows, at], x_ref[1, 0, rows, at])

                patches = [load(i) for i in range(RADIX)]
                for re, im in patches:
                    total = total + (re * re + im * im)
                forward_radix(lambda i: patches[i], tw_ref, hi, lo, rows, half)
            return total

        total = jnp.zeros((16, 128), F32)
        for q in range(4):
            copies[q].wait()
            total = lax.fori_loop(q * 4, q * 4 + 4, chunk, total)
        ss_ref[...] = total
        copies[4].wait()

    gh, gl = g_ref.at[0], g_ref.at[1]
    high, low = hi[k], lo[k]
    for part in range(2):
        at = slice(part * PART, part * PART + PART)
        out = dot3(gh[at, :], gl[at, :], high, low, NT)
        y_ref[0, :, part] = out.reshape(16, 16, ROWS)


def rows_forward(x_now, table, tw):
    anywhere = pl.BlockSpec(memory_space=pl.ANY)
    return pl.pallas_call(
        rows_body,
        grid=(RADIX,),
        in_specs=[
            anywhere,
            anywhere,
            whole((RADIX, 2, PART)),
        ],
        out_specs=[
            pl.BlockSpec((1, 16, 2, 16, ROWS), lambda k: (k, 0, 0, 0, 0)),
            whole((16, 128)),
        ],
        out_shape=[
            jax.ShapeDtypeStruct((RADIX, 16, 2, 16, ROWS), F32),
            jax.ShapeDtypeStruct((16, 128), F32),
        ],
        scratch_shapes=[
            pltpu.VMEM((RADIX, ROWS, 2 * PART), BF16),
            pltpu.VMEM((RADIX, ROWS, 2 * PART), BF16),
            pltpu.VMEM((2, 1, ROWS, N), F32),
            pltpu.VMEM((2, 2 * PART, 2 * PART), BF16),
            pltpu.SemaphoreType.DMA((5,)),
        ],
        compiler_params=params(62),
        cost_estimate=pl.CostEstimate(
            flops=4 * 10**9, bytes_accessed=10 * MIB, transcendentals=0
        ),
        name="rows_forward",
    )(x_now, table, tw)


def holo_body(depth_ref, x_in, gh_ref, gl_ref, tw_ref, y_ref, hi, lo, x_ref, sems):
    pairs = [(x_in.at[:, quarter(q), :], x_ref.at[:, quarter(q), :]) for q in range(4)]
    copies = stage_copies(pairs, sems)

    def chunk(t, carry):
        rows = pl.ds(pl.multiple_of(t * 16, 16), 16)
        for half in range(2):

            def load(i):
                at = slice(i * PART + half * 128, i * PART + half * 128 + 128)
                return (x_ref[0, rows, at], x_ref[1, rows, at])

            forward_radix(load, tw_ref, hi, lo, rows, half)
        return carry

    for q in range(4):
        copies[q].wait()
        lax.fori_loop(q * 4, q * 4 + 4, chunk, 0)
    y_ref[...] = jnp.full(y_ref.shape, depth_ref[0], F32)

    def per_k(k, carry):
        out = dot3(gh_ref[...], gl_ref[...], hi[k], lo[k], NT)
        for part in range(2):
            for half in range(2):
                y_ref[k, :, part * 2 + half, :] = out[
                    part * 16 : part * 16 + 16, half * 128 : half * 128 + 128
                ]
        return carry

    lax.fori_loop(0, RADIX, per_k, 0)


def holo_forward(depths, hologram, gt_high, gt_low, tw):
    return pl.pallas_call(
        holo_body,
        out_shape=jax.ShapeDtypeStruct((RADIX, 16, 8, 128), F32),
        scratch_shapes=[
            pltpu.VMEM((RADIX, ROWS, 2 * PART), BF16),
            pltpu.VMEM((RADIX, ROWS, 2 * PART), BF16),
            pltpu.VMEM((2, ROWS, N), F32),
            pltpu.SemaphoreType.DMA((4,)),
        ],
        in_specs=[
            pl.BlockSpec(memory_space=pltpu.SMEM),
            pl.BlockSpec(memory_space=pl.ANY),
        ]
        + [pl.BlockSpec(memory_space=pltpu.VMEM)] * 3,
        out_specs=pl.BlockSpec(memory_space=pltpu.VMEM),
        compiler_params=params(62),
        cost_estimate=pl.CostEstimate(
            flops=4 * 10**8, bytes_accessed=5 * MIB, transcendentals=0
        ),
        name="holo_forward",
    )(depths, hologram, gt_high, gt_low, tw)


def cos_sin(phase):
    turns = jnp.floor(phase * (2.0 / math.pi) + 0.5)
    rest = phase - turns * 1.5703125
    rest = rest - turns * 4.837512969970703e-4
    rest = rest - turns * 7.549789948768648e-8
    z = rest * rest
    sin = rest + rest * z * (
        -1.6666654611e-1 + z * (8.3321608736e-3 + z * -1.9515295891e-4)
    )
    cos = (
        1.0
        - 0.5 * z
        + z
        * z
        * (4.166664568298827e-2 + z * (-1.388731625493765e-3 + z * 2.443315711809948e-5))
    )
    quarter = turns.astype(jnp.int32) & 3
    odd = (quarter & 1) == 1
    base_cos = jnp.where(odd, sin, cos)
    base_sin = jnp.where(odd, cos, sin)
    out_cos = jnp.where((quarter == 1) | (quarter == 2), -base_cos, base_cos)
    out_sin = jnp.where(quarter >= 2, -base_sin, base_sin)
    return out_cos, out_sin


def transfer_body(depth_ref, rate_ref, t_ref):
    rate = rate_ref[0]
    for p in range(PLANES):
        cos, sin = cos_sin(depth_ref[0, p] * rate)
        rows = slice(p * 16, p * 16 + 16)
        t_ref[0, 0, rows, :] = cos
        t_ref[0, 1, rows, :] = sin


def transfer(depth_all, rate):
    return pl.pallas_call(
        transfer_body,
        grid=(RADIX,),
        in_specs=[
            pl.BlockSpec(memory_space=pltpu.SMEM),
            pl.BlockSpec((1, 16, PART), lambda k: (k, 0, 0)),
        ],
        out_specs=pl.BlockSpec((1, 2, PLANES * 16, PART), lambda k: (k, 0, 0, 0)),
        out_shape=jax.ShapeDtypeStruct((RADIX, 2, PLANES * 16, PART), F32),
        compiler_params=params(62),
        cost_estimate=pl.CostEstimate(
            flops=10**7, bytes_accessed=4 * MIB, transcendentals=0
        ),
        name="transfer",
    )(depth_all, rate)


COLS = PLANES * 16
MESSAGE = 72
WITH_HOLO = COLS + 16


def planes_of(q):
    return pl.ds(q * 4, 4)


def spectral_body(
    z_in, h_ref, t_ref, sq_ref, g_in, tw_ref, o_out, norm_ref,
    hi, lo, spec, bhi, blo, back, z_ref, g_ref, o_ref, sems, out_sems,
):
    k = pl.program_id(0)

    @pl.when(k == 0)
    def _():
        norm_ref[...] = jnp.zeros_like(norm_ref)
        pairs = [(z_in.at[:, planes_of(q)], z_ref.at[:, planes_of(q)]) for q in range(4)]
        copies = stage_copies(pairs + [(g_in, g_ref)], sems)

        def chunk(p, carry):
            rows = pl.ds(pl.multiple_of(p * 16, 16), 16)
            for half in range(2):
                at = slice(half * 128, half * 128 + 128)

                def load(i):
                    return (z_ref[i, p, 0, :, at], z_ref[i, p, 1, :, at])

                forward_radix(load, tw_ref, hi, lo, rows, half)
            return carry

        for q in range(4):
            copies[q].wait()
            lax.fori_loop(q * 4, q * 4 + 4, chunk, 0)
        copies[4].wait()
        for half in range(2):

            def load_holo(i):
                return (h_ref[i, :, half, :], h_ref[i, :, 2 + half, :])

            forward_radix(load_holo, tw_ref, hi, lo, slice(COLS, WITH_HOLO), half)

    spec[...] = dot3(hi[k], lo[k], g_ref[0], g_ref[1], NN)

    for half in range(2):
        at = slice(half * 128, half * 128 + 128)
        at_im = slice(PART + half * 128, PART + half * 128 + 128)

        def gather(p, total):
            rows = pl.ds(pl.multiple_of(p * 16, 16), 16)
            xr, xi = spec[rows, at], spec[rows, at_im]
            tr, ti = t_ref[0, 0, rows, at], t_ref[0, 1, rows, at]
            return (total[0] + (tr * xr - ti * xi), total[1] + (tr * xi + ti * xr))

        zero = jnp.zeros((16, 128), F32)
        pred = lax.fori_loop(0, PLANES, gather, (zero, zero), unroll=4)
        holo = (spec[COLS:WITH_HOLO, at], spec[COLS:WITH_HOLO, at_im])
        res = (holo[0] - pred[0], holo[1] - pred[1])
        norm_ref[...] += res[0] * (holo[0] + pred[0]) + res[1] * (holo[1] + pred[1])

        def scatter(p, carry):
            rows = pl.ds(pl.multiple_of(p * 16, 16), 16)
            tr, ti = t_ref[0, 0, rows, at], t_ref[0, 1, rows, at]
            br = tr * res[0] + ti * res[1]
            bi = tr * res[1] - ti * res[0]
            for where, value in ((at, br), (at_im, bi)):
                high, low = split(value)
                bhi[rows, where] = high
                blo[rows, where] = low
            return carry

        lax.fori_loop(0, PLANES, scatter, 0, unroll=4)

    c = tw_ref[k, 0:1, :]
    s = tw_ref[k, 1:2, :]
    out = dot3(bhi[...], blo[...], g_ref[2], g_ref[3], NN)
    re, im = out[:, :PART], out[:, PART:]
    back[k, 0] = re * c + im * s
    back[k, 1] = im * c - re * s

    @pl.when(k == RADIX - 1)
    def _():
        square = sq_ref[...] + norm_ref[...] * (1.0 / PLANES)
        square = square[:8, :] + square[8:, :]
        square = square + pltpu.roll(square, 64, 1)
        lane = lax.broadcasted_iota(jnp.int32, (8, 128), 1)
        square = jnp.where(lane < 64, 0.0, square)

        def chunk(p, carry):
            rows = pl.ds(pl.multiple_of(p * 16, 16), 16)
            for half in range(2):
                at = slice(half * 128, half * 128 + 128)
                out = dft8([(back[i, 0, rows, at], back[i, 1, rows, at]) for i in range(RADIX)], 1)
                for i in range(RADIX):
                    o_ref[i, p, half * 16 : half * 16 + 16, :] = out[i][0]
                    o_ref[i, p, half * 16 + 32 : half * 16 + 48, :] = out[i][1]
            for i in range(RADIX):
                tile = square
                for high in range(2):
                    for c in range(2):
                        low_rows = slice(c * 32 + high * 8, c * 32 + high * 8 + 8)
                        high_rows = slice(c * 32 + 16 + high * 8, c * 32 + 24 + high * 8)
                        edge = jnp.where(
                            lane < 2,
                            o_ref[min(i + 1, RADIX - 1), p, low_rows, :],
                            o_ref[max(i - 1, 0), p, high_rows, :],
                        )
                        base = high * 8 + c * 4
                        edge = pltpu.roll(edge, base + 2, 1)
                        tile = jnp.where((lane >= base) & (lane < base + 4), edge, tile)
                o_ref[i, p, 64:MESSAGE, :] = tile
            return carry

        sends = []
        for q in range(4):
            lax.fori_loop(q * 4, q * 4 + 4, chunk, 0)
            sends.append(
                pltpu.make_async_copy(
                    o_ref.at[:, planes_of(q)], o_out.at[:, planes_of(q)], out_sems.at[q]
                )
            )
            sends[-1].start()
        for send in sends:
            send.wait()


def spectral(z, holo, trans, squares, table, tw):
    anywhere = pl.BlockSpec(memory_space=pl.ANY)
    return pl.pallas_call(
        spectral_body,
        grid=(RADIX,),
        in_specs=[
            anywhere,
            whole((RADIX, 16, 8, 128)),
            pl.BlockSpec((1, 2, COLS, PART), lambda k: (k, 0, 0, 0)),
            whole((16, 128)),
            anywhere,
            whole((RADIX, 2, PART)),
        ],
        out_specs=anywhere,
        out_shape=jax.ShapeDtypeStruct((RADIX, PLANES, MESSAGE, 128), F32),
        scratch_shapes=[
            pltpu.VMEM((16, 128), F32),
            pltpu.VMEM((RADIX, WITH_HOLO, 2 * PART), BF16),
            pltpu.VMEM((RADIX, WITH_HOLO, 2 * PART), BF16),
            pltpu.VMEM((WITH_HOLO, 2 * PART), F32),
            pltpu.VMEM((COLS, 2 * PART), BF16),
            pltpu.VMEM((COLS, 2 * PART), BF16),
            pltpu.VMEM((RADIX, 2, COLS, PART), F32),
            pltpu.VMEM((RADIX, PLANES, 2, 16, PART), F32),
            pltpu.VMEM((4, 2 * PART, 2 * PART), BF16),
            pltpu.VMEM((RADIX, PLANES, MESSAGE, 128), F32),
            pltpu.SemaphoreType.DMA((5,)),
            pltpu.SemaphoreType.DMA((4,)),
        ],
        compiler_params=params(62),
        cost_estimate=pl.CostEstimate(
            flops=8 * 10**9, bytes_accessed=14 * MIB, transcendentals=0
        ),
        name="spectral",
    )(z, holo, trans, squares, table, tw)


def rows_back_body(
    w_ref, x_in, xt_ref, xb_ref, ih_ref, il_ref, eh_ref, el_ref, tw_ref, re_out, im_out, sum_ref,
    back, edge_back, x_ref, parts, x_sem, out_sems,
):
    k = pl.program_id(0)
    fetch = pltpu.make_async_copy(x_in, x_ref, x_sem)

    @pl.when(k == 0)
    def _():
        fetch.start()
        sum_ref[...] = jnp.zeros_like(sum_ref)

    tiles = w_ref[0, :, 64:MESSAGE, :]
    lane = lax.broadcasted_iota(jnp.int32, (8, 128), 1)
    sum_ref[...] += jnp.where(lane < 64, 0.0, jnp.sum(tiles, axis=0))
    turned = tiles.reshape(128, 128).T
    edge = jnp.concatenate([turned[0:8, :], turned[8:16, :]], axis=1)
    edge_high, edge_low = split(jnp.concatenate([edge, jnp.zeros_like(edge)], axis=0))
    mixed = dot3(edge_high, edge_low, eh_ref[...], el_ref[...], NN)[0:8, :]
    swapped = pltpu.roll(mixed, 4, 0)
    edge_re = mixed[:, :PART] - swapped[:, PART:]
    edge_im = mixed[:, PART:] + swapped[:, :PART]

    halves = []
    for c in range(2):
        for h in range(2):
            rows = slice(c * 32 + h * 16, c * 32 + h * 16 + 16)
            halves.append(w_ref[0, :, rows, :].reshape(PART, 128).T)
    turned = [jnp.concatenate(halves[c * 2 : c * 2 + 2], axis=0) for c in range(2)]
    high, low = split(jnp.concatenate(turned, axis=1))
    out = dot3(high, low, ih_ref[...], il_ref[...], NN)
    c = tw_ref[k, 0:1, :]
    s = tw_ref[k, 1:2, :]
    re, im = out[:, :PART], out[:, PART:]
    back[k, 0] = re * c + im * s
    back[k, 1] = im * c - re * s
    edge_back[k, 0] = edge_re * c + edge_im * s
    edge_back[k, 1] = edge_im * c - edge_re * s

    @pl.when(k == RADIX - 1)
    def _():
        fetch.wait()
        low_rows = lax.broadcasted_iota(jnp.int32, (8, 128), 0) < 4
        for half in range(2):
            at = slice(half * 128, half * 128 + 128)
            out = dft8([(edge_back[i, 0, :, at], edge_back[i, 1, :, at]) for i in range(RADIX)], 1)
            for i in range(RADIX):
                to = slice(i * PART + half * 128, i * PART + half * 128 + 128)
                for c in range(2):
                    value = pltpu.roll(out[i][c], 6, 0)
                    x = jnp.where(low_rows, xb_ref[c, 0, :, to], xt_ref[c, 0, :, to])
                    parts[c, ROWS:PACK, to] = value + x

        def chunk(t, carry):
            rows = pl.ds(pl.multiple_of(t * 16, 16), 16)
            for half in range(2):
                at = slice(half * 128, half * 128 + 128)
                out = dft8([(back[i, 0, rows, at], back[i, 1, rows, at]) for i in range(RADIX)], 1)
                for i in range(RADIX):
                    to = slice(i * PART + half * 128, i * PART + half * 128 + 128)
                    for c in range(2):
                        parts[c, rows, to] = x_ref[c, 0, rows, to] + out[i][c]
            return carry

        sends = []
        for q in range(4):
            lax.fori_loop(q * 4, q * 4 + 4, chunk, 0)
            span = pl.ds(q * 64, 72 if q == 3 else 64)
            for c, target in enumerate((re_out, im_out)):
                sends.append(
                    pltpu.make_async_copy(
                        parts.at[c, span, :], target.at[span, :], out_sems.at[c, q]
                    )
                )
                sends[-1].start()
        for send in sends:
            send.wait()


def rows_back(w, x_now, x_top, x_bottom, i_high, i_low, e_high, e_low, tw):
    table = whole((2 * PART, 2 * PART))
    edge_table = whole((PART, 2 * PART))
    anywhere = pl.BlockSpec(memory_space=pl.ANY)
    return pl.pallas_call(
        rows_back_body,
        grid=(RADIX,),
        in_specs=[
            pl.BlockSpec((1, 16, MESSAGE, 128), lambda k: (k, 0, 0, 0)),
            anywhere,
            whole((2, 1, 8, N)),
            whole((2, 1, 8, N)),
            table,
            table,
            edge_table,
            edge_table,
            whole((RADIX, 2, PART)),
        ],
        out_specs=[anywhere, anywhere, whole((8, 128))],
        out_shape=[
            jax.ShapeDtypeStruct((PACK, N), F32),
            jax.ShapeDtypeStruct((PACK, N), F32),
            jax.ShapeDtypeStruct((8, 128), F32),
        ],
        scratch_shapes=[
            pltpu.VMEM((RADIX, 2, ROWS, PART), F32),
            pltpu.VMEM((RADIX, 2, 8, PART), F32),
            pltpu.VMEM((2, 1, ROWS, N), F32),
            pltpu.VMEM((2, PACK, N), F32),
            pltpu.SemaphoreType.DMA,
            pltpu.SemaphoreType.DMA((2, 4)),
        ],
        compiler_params=params(62),
        cost_estimate=pl.CostEstimate(
            flops=4 * 10**9, bytes_accessed=13 * MIB, transcendentals=0
        ),
        name="rows_back",
    )(w, x_now, x_top, x_bottom, i_high, i_low, e_high, e_low, tw)


TILES = EXT // 8
WIDE = 512
STAGES = 4


def shift_up(x, after):
    row = lax.broadcasted_iota(jnp.int32, x.shape, 0)
    return pltpu.roll(jnp.where(row == 0, after, x), 7, 0)


def shift_down(x, before):
    row = lax.broadcasted_iota(jnp.int32, x.shape, 0)
    return pltpu.roll(jnp.where(row == 7, before, x), 1, 0)


def from_right(x, after):
    if after is None:
        col = lax.broadcasted_iota(jnp.int32, x.shape, 1)
        return jnp.where(col == WIDE - 1, x, pltpu.roll(x, WIDE - 1, 1))
    return pltpu.roll(jnp.concatenate([x, after], axis=1), WIDE + 127, 1)[:, :WIDE]


def from_left(x, before):
    if before is None:
        col = lax.broadcasted_iota(jnp.int32, x.shape, 1)
        return jnp.where(col == 0, 0.0, pltpu.roll(x, 1, 1))
    return pltpu.roll(jnp.concatenate([before, x], axis=1), 1, 1)[:, 128:]


def reciprocal(x):
    guess = pl.reciprocal(x, approx=True)
    return guess * (2.0 - x * guess)


def norm(gz, gy, gx):
    square = gz * gz + gy * gy + gx * gx
    return square * lax.rsqrt(square + 1e-30)


def patch(ref, lead, rows, start):
    at = slice(start, start + WIDE)
    after = None
    if start + WIDE < N:
        after = ref[lead + (rows, slice(start + WIDE, start + WIDE + 128))]
    return ref[lead + (rows, at)], after


def arrivals(source, target, q, first, last, sems, edge_sems):
    copies = [
        pltpu.make_async_copy(
            source.at[pl.ds(first, last - first), :],
            target.at[pl.ds(first + 8, last - first), :],
            sems.at[q],
        )
    ]
    halo = source.at[pl.ds(ROWS, 8), :]
    if q == 0:
        copies.append(pltpu.make_async_copy(halo, target.at[pl.ds(0, 8), :], edge_sems.at[0]))
    if q == STAGES - 1:
        copies.append(
            pltpu.make_async_copy(halo, target.at[pl.ds(ROWS + 8, 8), :], edge_sems.at[1])
        )
    return copies


def tv_first_body(
    num_ref, at_ref, own, nxt, prv, inner_out, dual_out,
    ext, inner, dual, in_sems, edge_sems, out_sems,
):
    size = ROWS // STAGES
    mains = []
    for q in range(STAGES):
        mains.append([])
        for which, main in enumerate((own, nxt, prv)):
            mains[q] += arrivals(
                main,
                ext.at[which],
                q,
                q * size,
                (q + 1) * size,
                in_sems.at[which],
                edge_sems.at[which],
            )
        for copy in mains[q]:
            copy.start()
    scale = num_ref[0]
    inverse = num_ref[1]
    size_of = num_ref[5]
    keep_next = num_ref[2]
    keep_prev = num_ref[3]
    band = at_ref[0]

    def tile(t, carry):
        rows = pl.ds(pl.multiple_of(t * 8, 8), 8)
        later = pl.ds(pl.multiple_of(jnp.minimum(t + 1, TILES - 1) * 8, 8), 8)
        earlier = pl.ds(pl.multiple_of(jnp.maximum(t - 1, 0) * 8, 8), 8)
        left = None
        for start in range(0, N, WIDE):
            at = slice(start, start + WIDE)
            u, u_after = patch(ext, (0,), rows, start)
            q, q_after = patch(ext, (2,), rows, start)
            gz = (ext[1, rows, at] - u) * keep_next
            gy = shift_up(u, ext[0, later, at]) - u
            gx = from_right(u, u_after) - u
            w = scale * reciprocal(1.0 + size_of * norm(gz, gy, gx))
            dz, dy, dx = gz * w, gy * w, gx * w
            gz = (u - q) * keep_prev
            gy = shift_up(q, ext[2, later, at]) - q
            gx = from_right(q, q_after) - q
            dq = gz * (scale * reciprocal(1.0 + size_of * norm(gz, gy, gx)))
            above = shift_down(dy, dual[1, earlier, at])
            div = (dz - dq) + (dy - above) + (dx - from_left(dx, left))
            left = dx[:, WIDE - 128 :]
            inner[rows, at] = (div + u * inverse) * STEP_TV
            dual[0, rows, at] = dz
            dual[1, rows, at] = dy
            dual[2, rows, at] = dx
            dual[3, rows, at] = dq
        return carry

    outs = []
    done = 0
    for q in range(STAGES):
        for copy in mains[q]:
            copy.wait()
        if q == 0:

            @pl.when(band == 0)
            def _():
                for which in range(3):
                    ext[which, 7:8, :] = ext[which, 8:9, :]

        if q == STAGES - 1:

            @pl.when(band == N // ROWS - 1)
            def _():
                for which in range(3):
                    ext[which, ROWS + 8 : ROWS + 9, :] = ext[which, ROWS + 7 : ROWS + 8, :]

        upto = TILES if q == STAGES - 1 else (q + 1) * size // 8
        lax.fori_loop(done, upto, tile, 0)
        if q == 0:

            @pl.when(band == 0)
            def _():
                inner[7:8, :] = inner[8:9, :]

        if q == STAGES - 1:

            @pl.when(band == N // ROWS - 1)
            def _():
                inner[ROWS + 8 : ROWS + 9, :] = inner[ROWS + 7 : ROWS + 8, :]

            row = lax.broadcasted_iota(jnp.int32, (8, N), 0)
            inner[0:8, :] = jnp.where(row < 4, inner[ROWS + 8 : EXT, :], inner[0:8, :])
            outs.append(
                pltpu.make_async_copy(
                    inner.at[pl.ds(0, 8), :], inner_out.at[pl.ds(ROWS, 8), :], out_sems.at[2, 0]
                )
            )
            outs[-1].start()

        first = max(done, 1)
        last = min(upto, TILES - 1)
        span = pl.ds(done * 8, (upto - done) * 8)
        outs += [
            pltpu.make_async_copy(
                inner.at[pl.ds(first * 8, (last - first) * 8), :],
                inner_out.at[pl.ds(first * 8 - 8, (last - first) * 8), :],
                out_sems.at[0, q],
            ),
            pltpu.make_async_copy(dual.at[:, span, :], dual_out.at[:, span, :], out_sems.at[1, q]),
        ]
        outs[-2].start()
        outs[-1].start()
        done = upto
    for copy in outs:
        copy.wait()


def tv_first(numbers, place, own, nxt, prv):
    smem = pl.BlockSpec(memory_space=pltpu.SMEM)
    anywhere = pl.BlockSpec(memory_space=pl.ANY)
    return pl.pallas_call(
        tv_first_body,
        in_specs=[smem, smem] + [anywhere] * 3,
        out_specs=[anywhere, anywhere],
        out_shape=[
            jax.ShapeDtypeStruct((PACK, N), F32),
            jax.ShapeDtypeStruct((4, EXT, N), F32),
        ],
        scratch_shapes=[
            pltpu.VMEM((3, EXT, N), F32),
            pltpu.VMEM((EXT, N), F32),
            pltpu.VMEM((4, EXT, N), F32),
            pltpu.SemaphoreType.DMA((3, STAGES)),
            pltpu.SemaphoreType.DMA((3, 2)),
            pltpu.SemaphoreType.DMA((3, STAGES)),
        ],
        compiler_params=params(62),
        cost_estimate=pl.CostEstimate(
            flops=10**8, bytes_accessed=17 * MIB, transcendentals=2 * 10**6
        ),
        name="tv_first",
    )(numbers, place, own, nxt, prv)


def tv_second_body(
    comp, num_ref, own_in, nxt_in, prv_in, dual_in, parts_in, x_prev_in, x_now_in, *rest
):
    out_ref, inner, dual, plain, below, sems, edge_sems, out_sems = rest[-8:]
    size = ROWS // STAGES
    copies = []
    for q in range(STAGES):
        first = 0 if q == 0 else q * size + 16
        span = pl.ds(first, (q + 1) * size + 16 - first)
        main = pl.ds(q * size, size)
        begin = 0 if q == 0 else q * size + 8
        end = min((q + 1) * size + 8, ROWS)
        blocks = []
        for i, ref in enumerate((own_in, nxt_in, prv_in)):
            blocks += arrivals(ref, inner.at[i], q, begin, end, sems.at[i], edge_sems.at[i])
        pairs = [
            (dual_in.at[:, span, :], dual.at[:, span, :]),
            (parts_in.at[main, :], plain.at[0, main, :]),
            (x_prev_in.at[comp, 0, main, :], plain.at[1, main, :]),
            (x_now_in.at[comp, 0, main, :], plain.at[2, main, :]),
        ]
        copies.append(
            blocks
            + [pltpu.make_async_copy(a, b, sems.at[i + 3, q]) for i, (a, b) in enumerate(pairs)]
        )
        for copy in copies[-1]:
            copy.start()
    strength = num_ref[4]
    keep_next = num_ref[2]
    keep_prev = num_ref[3]

    def tile(t, carry):
        rows = pl.ds(pl.multiple_of(t * 8, 8), 8)
        later = pl.ds(pl.multiple_of(t * 8 + 8, 8), 8)
        main = pl.ds(pl.multiple_of(jnp.maximum(t - 1, 0) * 8, 8), 8)
        left = None
        for start in range(0, N, WIDE):
            at = slice(start, start + WIDE)
            u, u_after = patch(inner, (0,), rows, start)
            q, q_after = patch(inner, (2,), rows, start)
            gz = (inner[1, rows, at] - u) * keep_next
            gy = shift_up(u, inner[0, later, at]) - u
            gx = from_right(u, u_after) - u
            w = reciprocal(1.0 + norm(gz, gy, gx))
            dz = (dual[0, rows, at] + gz) * w
            dy = (dual[1, rows, at] + gy) * w
            dx = (dual[2, rows, at] + gx) * w
            gz = (u - q) * keep_prev
            gy = shift_up(q, inner[2, later, at]) - q
            gx = from_right(q, q_after) - q
            dq = (dual[3, rows, at] + gz) * reciprocal(1.0 + norm(gz, gy, gx))
            above = shift_down(dy, below[:, at])
            below[:, at] = dy
            div = (dz - dq) + (dy - above) + (dx - from_left(dx, left))
            left = dx[:, WIDE - 128 :]
            denoised = plain[0, main, at] - strength * div
            plain[1, main, at] = (
                (1.0 - ALPHA_TWIST) * plain[1, main, at]
                + (ALPHA_TWIST - BETA_TWIST) * plain[2, main, at]
                + BETA_TWIST * denoised
            )
        return carry

    def first_rows(start):
        at = slice(start, start + WIDE)
        u, u_after = patch(inner, (0,), slice(0, 8), start)
        gz = (inner[1, 0:8, at] - u) * keep_next
        gy = shift_up(u, inner[0, 8:16, at]) - u
        gx = from_right(u, u_after) - u
        below[:, at] = (dual[1, 0:8, at] + gy) * reciprocal(1.0 + norm(gz, gy, gx))

    outs = []
    for q in range(STAGES):
        for copy in copies[q]:
            copy.wait()
        if q == 0:
            for start in range(0, N, WIDE):
                first_rows(start)
        lax.fori_loop(1 + q * size // 8, 1 + (q + 1) * size // 8, tile, 0)
        main = pl.ds(q * size, size)
        outs.append(
            pltpu.make_async_copy(
                plain.at[1, main, :], out_ref.at[comp, 0, main, :], out_sems.at[q]
            )
        )
        outs[-1].start()
    for copy in outs:
        copy.wait()


def tv_second(comp, numbers, own, nxt, prv, dual, parts, x_prev, x_now, into):
    smem = pl.BlockSpec(memory_space=pltpu.SMEM)
    anywhere = pl.BlockSpec(memory_space=pl.ANY)
    args = [numbers, own, nxt, prv, dual, parts, x_prev, x_now]
    aliases = {}
    if into is not None:
        args.append(into)
        aliases = {len(args) - 1: 0}
    return pl.pallas_call(
        functools.partial(tv_second_body, comp),
        in_specs=[smem] + [anywhere] * (len(args) - 1),
        out_specs=anywhere,
        out_shape=jax.ShapeDtypeStruct((2, 1, ROWS, N), F32),
        scratch_shapes=[
            pltpu.VMEM((3, EXT, N), F32),
            pltpu.VMEM((4, EXT, N), F32),
            pltpu.VMEM((3, ROWS, N), F32),
            pltpu.VMEM((8, N), F32),
            pltpu.SemaphoreType.DMA((7, STAGES)),
            pltpu.SemaphoreType.DMA((3, 2)),
            pltpu.SemaphoreType.DMA((STAGES,)),
        ],
        input_output_aliases=aliases,
        compiler_params=params(62),
        cost_estimate=pl.CostEstimate(
            flops=10**8, bytes_accessed=23 * MIB, transcendentals=2 * 10**6
        ),
        name="tv_second",
    )(*args)


def from_behind(x, axis, by):
    count = lax.axis_size(axis)
    pairs = [(i, i + by) for i in range(count) if 0 <= i + by < count]
    return lax.ppermute(x, axis, pairs)


def signed_freq(freq):
    signed = jnp.where(freq < N // 2, freq, freq - N)
    return signed.astype(F32) * (2.0 * math.pi / N)


def phase_rate(qx_grid, qy_grid):
    square = qx_grid * qx_grid + qy_grid * qy_grid
    return -square / (WAVENUMBER + jnp.sqrt(WAVENUMBER * WAVENUMBER - square))


def shards(x_now, x_prev, hologram, depths):
    d = lax.axis_index("depth")
    r = lax.axis_index("rows")
    forward, inverse = dft_blocks(1.0 / math.sqrt(N))
    g_high, g_low = split_np(forward)
    i_high, i_low = split_np(inverse)
    p_high, p_low = split_np(inverse / PLANES)
    e_high, e_low = split_np(halo_table(inverse / PLANES))
    t_high, t_low = split_np(forward.T)
    pick = np.stack([t_high, t_low]).reshape(2, 2, 16, 16, 2 * PART)
    pick = np.ascontiguousarray(pick.transpose(3, 0, 1, 2, 4)).reshape(16, 2, 32, 2 * PART)
    tw = jnp.asarray(twiddles())
    both = ("rows", "depth")

    chosen = lax.dynamic_index_in_dim(jnp.asarray(pick), d, 0, keepdims=False)
    holo = holo_forward(depths, hologram, chosen[0], chosen[1], tw)
    holo = lax.all_to_all(holo.reshape(128, 8, 128), both, 0, 0, tiled=True)
    depth_all = holo[:PLANES, 4, 0].reshape(1, PLANES)
    kx = r + RADIX * (16 * d + jnp.arange(16, dtype=jnp.int32))
    ky = (
        jnp.arange(RADIX, dtype=jnp.int32)[:, None]
        + RADIX * jnp.arange(PART, dtype=jnp.int32)[None, :]
    )
    rate = phase_rate(signed_freq(kx)[None, :, None], signed_freq(ky)[:, None, :])
    trans = transfer(depth_all, rate)

    sent, squares = rows_forward(x_now, jnp.asarray(np.stack([t_high, t_low])), tw)
    got = lax.all_to_all(sent.reshape(128, 2, 16, ROWS), both, 0, 0, tiled=True)
    x_top = from_behind(x_now[:, :, ROWS - 8 :], "rows", 1)
    x_bottom = from_behind(x_now[:, :, :8], "rows", -1)
    back = spectral(
        got.reshape(RADIX, PLANES, 2, 16, ROWS),
        holo.reshape(RADIX, PLANES, 8, 128),
        trans,
        squares,
        jnp.asarray(np.stack([g_high, g_low, i_high, i_low])),
        tw,
    )
    ret = lax.all_to_all(back.reshape(128, MESSAGE, 128), both, 0, 0, tiled=True)
    re, im, sums = rows_back(
        ret.reshape(RADIX, PLANES, MESSAGE, 128),
        x_now,
        x_top,
        x_bottom,
        jnp.asarray(p_high),
        jnp.asarray(p_low),
        jnp.asarray(e_high),
        jnp.asarray(e_low),
        tw,
    )

    total = jnp.sum(sums)
    mean_square = jnp.maximum(total, 0.0) / (2.0 * PLANES * N * N)
    strength = LAMBDA_TV * jnp.sqrt(mean_square + EPSILON)
    numbers = jnp.stack(
        [
            -STEP_TV / strength,
            -1.0 / strength,
            (d < PLANES - 1).astype(F32),
            (d > 0).astype(F32),
            strength,
            STEP_TV / strength,
        ]
    )
    place = jnp.stack([r])

    own = (re, im)
    nxt = [from_behind(part, "depth", -1) for part in own]
    prv = [from_behind(part, "depth", 1) for part in own]
    out = None
    firsts = [tv_first(numbers, place, own[c], nxt[c], prv[c]) for c in range(2)]
    ahead = [from_behind(inner, "depth", -1) for inner, _ in firsts]
    behind = [from_behind(inner, "depth", 1) for inner, _ in firsts]
    for c in range(2):
        inner, dual = firsts[c]
        out = tv_second(
            c, numbers, inner, ahead[c], behind[c], dual, own[c], x_prev, x_now, out
        )
    return out


def solution(mesh):
    return jax.shard_map(
        shards,
        mesh=mesh,
        in_specs=(
            P(None, "depth", "rows", None),
            P(None, "depth", "rows", None),
            P(None, "rows", None),
            P("depth"),
        ),
        out_specs=P(None, "depth", "rows", None),
        check_vma=False,
    )
```

```python
import functools
import math

import jax
import jax.numpy as jnp
import ml_dtypes
import numpy as np
from jax import lax
from jax.experimental import pallas as pl
from jax.experimental.pallas import tpu as pltpu
from jax.sharding import PartitionSpec as P

ALPHA_TWIST = 1.8
BETA_TWIST = 1.2
LAMBDA_TV = 0.2
STEP_TV = 1.0 / 12.0
EPSILON = 1e-06
WAVENUMBER = 4.0 * math.pi

N = 2048
PLANES = 16
ROWS = 256
RADIX = 8
PART = 256
EXT = ROWS + 16
PACK = ROWS + 8
HALF = ROWS // 2
F32 = jnp.float32
BF16 = jnp.bfloat16
MIB = 1024 * 1024


def split_np(table):
    high = table.astype(np.float32).astype(ml_dtypes.bfloat16)
    low = (table - high.astype(np.float64)).astype(np.float32).astype(ml_dtypes.bfloat16)
    return high, low


def dft_blocks(scale):
    index = np.arange(PART)
    angle = 2.0 * np.pi * ((index[:, None] * index[None, :]) % PART) / PART
    cos = np.cos(angle) * scale
    sin = np.sin(angle) * scale
    forward = np.block([[cos, -sin], [sin, cos]])
    inverse = np.block([[cos, sin], [-sin, cos]])
    return forward, inverse


def halo_table(inverse):
    rows = inverse[:PART].reshape(16, 2, 8, 2 * PART)
    return np.ascontiguousarray(rows.transpose(1, 0, 2, 3)).reshape(PART, 2 * PART)


def twiddles():
    index = np.arange(PART)
    angle = 2.0 * np.pi * (np.arange(RADIX)[:, None] * index[None, :]) / N
    return np.stack([np.cos(angle), -np.sin(angle)], axis=1).astype(np.float32)


def dft4(a, b, c, d, sign):
    t0 = (a[0] + c[0], a[1] + c[1])
    t1 = (a[0] - c[0], a[1] - c[1])
    t2 = (b[0] + d[0], b[1] + d[1])
    t3 = (b[0] - d[0], b[1] - d[1])
    if sign > 0:
        turned = (-t3[1], t3[0])
    else:
        turned = (t3[1], -t3[0])
    return (
        (t0[0] + t2[0], t0[1] + t2[1]),
        (t1[0] + turned[0], t1[1] + turned[1]),
        (t0[0] - t2[0], t0[1] - t2[1]),
        (t1[0] - turned[0], t1[1] - turned[1]),
    )


def dft8(v, sign):
    even = dft4(v[0], v[2], v[4], v[6], sign)
    odd = dft4(v[1], v[3], v[5], v[7], sign)
    half = math.sqrt(0.5)
    o1, o2, o3 = odd[1], odd[2], odd[3]
    if sign > 0:
        w1 = ((o1[0] - o1[1]) * half, (o1[0] + o1[1]) * half)
        w2 = (-o2[1], o2[0])
        w3 = ((-o3[0] - o3[1]) * half, (o3[0] - o3[1]) * half)
    else:
        w1 = ((o1[0] + o1[1]) * half, (o1[1] - o1[0]) * half)
        w2 = (o2[1], -o2[0])
        w3 = ((o3[1] - o3[0]) * half, (-o3[0] - o3[1]) * half)
    turned = (odd[0], w1, w2, w3)
    low = [(even[k][0] + turned[k][0], even[k][1] + turned[k][1]) for k in range(4)]
    high = [(even[k][0] - turned[k][0], even[k][1] - turned[k][1]) for k in range(4)]
    return low + high


def split(x):
    high = x.astype(BF16)
    return high, (x - high.astype(F32)).astype(BF16)


def dot(a, b, contract):
    return lax.dot_general(a, b, (contract, ((), ())), preferred_element_type=F32)


def dot3(a_high, a_low, b_high, b_low, contract):
    return (
        dot(a_high, b_high, contract) + dot(a_high, b_low, contract) + dot(a_low, b_high, contract)
    )


NT = ((1,), (1,))
NN = ((1,), (0,))


def forward_radix(load, tw_ref, hi, lo, rows, half):
    lanes = slice(half * 128, half * 128 + 128)
    out = dft8([load(i) for i in range(RADIX)], -1)
    for k in range(RADIX):
        re, im = out[k]
        if k:
            c = tw_ref[k, 0:1, lanes]
            s = tw_ref[k, 1:2, lanes]
            re, im = re * c - im * s, re * s + im * c
        for part, value in ((0, re), (1, im)):
            high, low = split(value)
            at = slice(part * PART + half * 128, part * PART + half * 128 + 128)
            hi[k, rows, at] = high
            lo[k, rows, at] = low


def params(limit_mib):
    return pltpu.CompilerParams(vmem_limit_bytes=limit_mib * MIB)


def whole(shape):
    return pl.BlockSpec(shape, lambda *_: (0,) * len(shape))


def stage_copies(pairs, sems):
    copies = [pltpu.make_async_copy(a, b, sems.at[i]) for i, (a, b) in enumerate(pairs)]
    for copy in copies:
        copy.start()
    return copies


def quarter(q):
    return pl.ds(q * (ROWS // 4), ROWS // 4)


def rows_body(x_in, g_in, tw_ref, y_out, ss_ref, hi, lo, x_ref, g_ref, y_ref, sems, out_sems):
    pairs = [(x_in.at[:, :, quarter(q), :], x_ref.at[:, :, quarter(q), :]) for q in range(4)]
    copies = stage_copies(pairs + [(g_in, g_ref)], sems)

    def chunk(t, total):
        rows = pl.ds(pl.multiple_of(t * 16, 16), 16)
        for half in range(2):

            def load(i):
                at = slice(i * PART + half * 128, i * PART + half * 128 + 128)
                return (x_ref[0, 0, rows, at], x_ref[1, 0, rows, at])

            patches = [load(i) for i in range(RADIX)]
            for re, im in patches:
                total = total + (re * re + im * im)
            forward_radix(lambda i: patches[i], tw_ref, hi, lo, rows, half)
        return total

    total = jnp.zeros((16, 128), F32)
    for q in range(4):
        copies[q].wait()
        total = lax.fori_loop(q * 4, q * 4 + 4, chunk, total)
    ss_ref[...] = total
    copies[4].wait()

    def send(k):
        return pltpu.make_async_copy(y_ref.at[k], y_out.at[k], out_sems.at[k])

    def per_k(k, carry):
        high, low = hi[k], lo[k]
        for part in range(2):
            at = slice(part * PART, part * PART + PART)
            out = dot3(g_ref[0, at, :], g_ref[1, at, :], high, low, NT)
            y_ref[k, :, part] = out.reshape(16, 16, ROWS)
        send(k).start()
        return carry

    def finish(k, carry):
        send(k).wait()
        return carry

    lax.fori_loop(0, RADIX, per_k, 0)
    lax.fori_loop(0, RADIX, finish, 0)


def rows_forward(x_now, table, tw):
    anywhere = pl.BlockSpec(memory_space=pl.ANY)
    vmem = pl.BlockSpec(memory_space=pltpu.VMEM)
    return pl.pallas_call(
        rows_body,
        in_specs=[anywhere, anywhere, vmem],
        out_specs=[anywhere, vmem],
        out_shape=[
            jax.ShapeDtypeStruct((RADIX, 16, 2, 16, ROWS), F32),
            jax.ShapeDtypeStruct((16, 128), F32),
        ],
        scratch_shapes=[
            pltpu.VMEM((RADIX, ROWS, 2 * PART), BF16),
            pltpu.VMEM((RADIX, ROWS, 2 * PART), BF16),
            pltpu.VMEM((2, 1, ROWS, N), F32),
            pltpu.VMEM((2, 2 * PART, 2 * PART), BF16),
            pltpu.VMEM((RADIX, 16, 2, 16, ROWS), F32),
            pltpu.SemaphoreType.DMA((5,)),
            pltpu.SemaphoreType.DMA((RADIX,)),
        ],
        compiler_params=params(62),
        cost_estimate=pl.CostEstimate(
            flops=4 * 10**9, bytes_accessed=10 * MIB, transcendentals=0
        ),
        name="rows_forward",
    )(x_now, table, tw)


def holo_body(depth_ref, x_in, gh_ref, gl_ref, tw_ref, y_ref, hi, lo, x_ref, sems):
    pairs = [(x_in.at[:, quarter(q), :], x_ref.at[:, quarter(q), :]) for q in range(4)]
    copies = stage_copies(pairs, sems)

    def chunk(t, carry):
        rows = pl.ds(pl.multiple_of(t * 16, 16), 16)
        for half in range(2):

            def load(i):
                at = slice(i * PART + half * 128, i * PART + half * 128 + 128)
                return (x_ref[0, rows, at], x_ref[1, rows, at])

            forward_radix(load, tw_ref, hi, lo, rows, half)
        return carry

    for q in range(4):
        copies[q].wait()
        lax.fori_loop(q * 4, q * 4 + 4, chunk, 0)
    y_ref[...] = jnp.full(y_ref.shape, depth_ref[0], F32)

    def per_k(k, carry):
        out = dot3(gh_ref[...], gl_ref[...], hi[k], lo[k], NT)
        for part in range(2):
            for half in range(2):
                y_ref[k, :, part * 2 + half, :] = out[
                    part * 16 : part * 16 + 16, half * 128 : half * 128 + 128
                ]
        return carry

    lax.fori_loop(0, RADIX, per_k, 0)


def holo_forward(depths, hologram, gt_high, gt_low, tw):
    return pl.pallas_call(
        holo_body,
        out_shape=jax.ShapeDtypeStruct((RADIX, 16, 8, 128), F32),
        scratch_shapes=[
            pltpu.VMEM((RADIX, ROWS, 2 * PART), BF16),
            pltpu.VMEM((RADIX, ROWS, 2 * PART), BF16),
            pltpu.VMEM((2, ROWS, N), F32),
            pltpu.SemaphoreType.DMA((4,)),
        ],
        in_specs=[
            pl.BlockSpec(memory_space=pltpu.SMEM),
            pl.BlockSpec(memory_space=pl.ANY),
        ]
        + [pl.BlockSpec(memory_space=pltpu.VMEM)] * 3,
        out_specs=pl.BlockSpec(memory_space=pltpu.VMEM),
        compiler_params=params(62),
        cost_estimate=pl.CostEstimate(
            flops=4 * 10**8, bytes_accessed=5 * MIB, transcendentals=0
        ),
        name="holo_forward",
    )(depths, hologram, gt_high, gt_low, tw)


def cos_sin(phase):
    turns = jnp.floor(phase * (2.0 / math.pi) + 0.5)
    rest = phase - turns * 1.5703125
    rest = rest - turns * 4.837512969970703e-4
    rest = rest - turns * 7.549789948768648e-8
    z = rest * rest
    sin = rest + rest * z * (
        -1.6666654611e-1 + z * (8.3321608736e-3 + z * -1.9515295891e-4)
    )
    cos = (
        1.0
        - 0.5 * z
        + z
        * z
        * (4.166664568298827e-2 + z * (-1.388731625493765e-3 + z * 2.443315711809948e-5))
    )
    quarter = turns.astype(jnp.int32) & 3
    odd = (quarter & 1) == 1
    base_cos = jnp.where(odd, sin, cos)
    base_sin = jnp.where(odd, cos, sin)
    out_cos = jnp.where((quarter == 1) | (quarter == 2), -base_cos, base_cos)
    out_sin = jnp.where(quarter >= 2, -base_sin, base_sin)
    return out_cos, out_sin


def transfer_body(depth_ref, rate_ref, t_ref):
    rate = rate_ref[0]
    for p in range(PLANES):
        cos, sin = cos_sin(depth_ref[0, p] * rate)
        rows = slice(p * 16, p * 16 + 16)
        t_ref[0, 0, rows, :] = cos
        t_ref[0, 1, rows, :] = sin


def transfer(depth_all, rate):
    return pl.pallas_call(
        transfer_body,
        grid=(RADIX,),
        in_specs=[
            pl.BlockSpec(memory_space=pltpu.SMEM),
            pl.BlockSpec((1, 16, PART), lambda k: (k, 0, 0)),
        ],
        out_specs=pl.BlockSpec((1, 2, PLANES * 16, PART), lambda k: (k, 0, 0, 0)),
        out_shape=jax.ShapeDtypeStruct((RADIX, 2, PLANES * 16, PART), F32),
        compiler_params=params(62),
        cost_estimate=pl.CostEstimate(
            flops=10**7, bytes_accessed=4 * MIB, transcendentals=0
        ),
        name="transfer",
    )(depth_all, rate)


COLS = PLANES * 16
MESSAGE = 72
WITH_HOLO = COLS + 16


def planes_of(q):
    return pl.ds(q * 4, 4)


def spectral_body(
    z_in, h_in, t_in, sq_ref, g_in, tw_ref, o_out, norm_ref,
    hi, lo, spec, bhi, blo, back, z_ref, g_ref, o_ref, h_ref, t_ref, sems, out_sems, t_sems,
):
    norm_ref[...] = jnp.zeros_like(norm_ref)
    pairs = [(z_in.at[:, planes_of(q)], z_ref.at[:, planes_of(q)]) for q in range(4)]
    copies = stage_copies(pairs + [(h_in, h_ref), (g_in, g_ref)], sems)

    def take(k):
        return pltpu.make_async_copy(t_in.at[k], t_ref.at[k], t_sems.at[k])

    def begin(k, carry):
        take(k).start()
        return carry

    lax.fori_loop(0, RADIX, begin, 0)

    def chunk(p, carry):
        rows = pl.ds(pl.multiple_of(p * 16, 16), 16)
        for half in range(2):
            at = slice(half * 128, half * 128 + 128)

            def load(i):
                return (z_ref[i, p, 0, :, at], z_ref[i, p, 1, :, at])

            forward_radix(load, tw_ref, hi, lo, rows, half)
        return carry

    for q in range(4):
        copies[q].wait()
        lax.fori_loop(q * 4, q * 4 + 4, chunk, 0)
    copies[4].wait()
    for half in range(2):

        def load_holo(i):
            return (h_ref[i, :, half, :], h_ref[i, :, 2 + half, :])

        forward_radix(load_holo, tw_ref, hi, lo, slice(COLS, WITH_HOLO), half)
    copies[5].wait()

    def per_k(k, carry):
        spec[...] = dot3(hi[k], lo[k], g_ref[0], g_ref[1], NN)
        take(k).wait()

        for half in range(2):
            at = slice(half * 128, half * 128 + 128)
            at_im = slice(PART + half * 128, PART + half * 128 + 128)

            def gather(p, total):
                rows = pl.ds(pl.multiple_of(p * 16, 16), 16)
                xr, xi = spec[rows, at], spec[rows, at_im]
                tr, ti = t_ref[k, 0, rows, at], t_ref[k, 1, rows, at]
                return (total[0] + (tr * xr - ti * xi), total[1] + (tr * xi + ti * xr))

            zero = jnp.zeros((16, 128), F32)
            pred = lax.fori_loop(0, PLANES, gather, (zero, zero), unroll=4)
            holo = (spec[COLS:WITH_HOLO, at], spec[COLS:WITH_HOLO, at_im])
            res = (holo[0] - pred[0], holo[1] - pred[1])
            norm_ref[...] += res[0] * (holo[0] + pred[0]) + res[1] * (holo[1] + pred[1])

            def scatter(p, carry):
                rows = pl.ds(pl.multiple_of(p * 16, 16), 16)
                tr, ti = t_ref[k, 0, rows, at], t_ref[k, 1, rows, at]
                br = tr * res[0] + ti * res[1]
                bi = tr * res[1] - ti * res[0]
                for where, value in ((at, br), (at_im, bi)):
                    high, low = split(value)
                    bhi[rows, where] = high
                    blo[rows, where] = low
                return carry

            lax.fori_loop(0, PLANES, scatter, 0, unroll=4)

        c = tw_ref[k, 0:1, :]
        s = tw_ref[k, 1:2, :]
        out = dot3(bhi[...], blo[...], g_ref[2], g_ref[3], NN)
        re, im = out[:, :PART], out[:, PART:]
        back[k, 0] = re * c + im * s
        back[k, 1] = im * c - re * s
        return carry

    lax.fori_loop(0, RADIX, per_k, 0)

    square = sq_ref[...] + norm_ref[...] * (1.0 / PLANES)
    square = square[:8, :] + square[8:, :]
    square = square + pltpu.roll(square, 64, 1)
    lane = lax.broadcasted_iota(jnp.int32, (8, 128), 1)
    square = jnp.where(lane < 64, 0.0, square)

    def chunk(p, carry):
        rows = pl.ds(pl.multiple_of(p * 16, 16), 16)
        for half in range(2):
            at = slice(half * 128, half * 128 + 128)
            out = dft8([(back[i, 0, rows, at], back[i, 1, rows, at]) for i in range(RADIX)], 1)
            for i in range(RADIX):
                o_ref[i, p, half * 16 : half * 16 + 16, :] = out[i][0]
                o_ref[i, p, half * 16 + 32 : half * 16 + 48, :] = out[i][1]
        for i in range(RADIX):
            tile = square
            for high in range(2):
                for c in range(2):
                    low_rows = slice(c * 32 + high * 8, c * 32 + high * 8 + 8)
                    high_rows = slice(c * 32 + 16 + high * 8, c * 32 + 24 + high * 8)
                    edge = jnp.where(
                        lane < 2,
                        o_ref[min(i + 1, RADIX - 1), p, low_rows, :],
                        o_ref[max(i - 1, 0), p, high_rows, :],
                    )
                    base = high * 8 + c * 4
                    edge = pltpu.roll(edge, base + 2, 1)
                    tile = jnp.where((lane >= base) & (lane < base + 4), edge, tile)
            o_ref[i, p, 64:MESSAGE, :] = tile
        return carry

    sends = []
    for q in range(4):
        lax.fori_loop(q * 4, q * 4 + 4, chunk, 0)
        sends.append(
            pltpu.make_async_copy(
                o_ref.at[:, planes_of(q)], o_out.at[:, planes_of(q)], out_sems.at[q]
            )
        )
        sends[-1].start()
    for send in sends:
        send.wait()


def spectral(z, holo, trans, squares, table, tw):
    anywhere = pl.BlockSpec(memory_space=pl.ANY)
    vmem = pl.BlockSpec(memory_space=pltpu.VMEM)
    return pl.pallas_call(
        spectral_body,
        in_specs=[anywhere, anywhere, anywhere, vmem, anywhere, vmem],
        out_specs=anywhere,
        out_shape=jax.ShapeDtypeStruct((RADIX, PLANES, MESSAGE, 128), F32),
        scratch_shapes=[
            pltpu.VMEM((16, 128), F32),
            pltpu.VMEM((RADIX, WITH_HOLO, 2 * PART), BF16),
            pltpu.VMEM((RADIX, WITH_HOLO, 2 * PART), BF16),
            pltpu.VMEM((WITH_HOLO, 2 * PART), F32),
            pltpu.VMEM((COLS, 2 * PART), BF16),
            pltpu.VMEM((COLS, 2 * PART), BF16),
            pltpu.VMEM((RADIX, 2, COLS, PART), F32),
            pltpu.VMEM((RADIX, PLANES, 2, 16, PART), F32),
            pltpu.VMEM((4, 2 * PART, 2 * PART), BF16),
            pltpu.VMEM((RADIX, PLANES, MESSAGE, 128), F32),
            pltpu.VMEM((RADIX, 16, 8, 128), F32),
            pltpu.VMEM((RADIX, 2, COLS, PART), F32),
            pltpu.SemaphoreType.DMA((6,)),
            pltpu.SemaphoreType.DMA((4,)),
            pltpu.SemaphoreType.DMA((RADIX,)),
        ],
        compiler_params=params(62),
        cost_estimate=pl.CostEstimate(
            flops=8 * 10**9, bytes_accessed=14 * MIB, transcendentals=0
        ),
        name="spectral",
    )(z, holo, trans, squares, table, tw)


def rows_back_body(
    w_in, x_in, xt_ref, xb_ref, p_in, e_in, tw_ref, re_out, im_out, sum_ref,
    back, edge_back, w_ref, x_ref, parts, p_ref, e_ref, w_sems, sems, out_sems,
):
    tables = stage_copies([(p_in, p_ref), (e_in, e_ref)], sems)

    def take(k):
        return pltpu.make_async_copy(w_in.at[k], w_ref.at[k], w_sems.at[k])

    def begin(k, carry):
        take(k).start()
        return carry

    lax.fori_loop(0, RADIX, begin, 0)
    fetch = pltpu.make_async_copy(x_in, x_ref, sems.at[2])
    fetch.start()
    sum_ref[...] = jnp.zeros_like(sum_ref)
    for copy in tables:
        copy.wait()

    def per_k(k, carry):
        take(k).wait()
        tiles = w_ref[k, :, 64:MESSAGE, :]
        lane = lax.broadcasted_iota(jnp.int32, (8, 128), 1)
        sum_ref[...] += jnp.where(lane < 64, 0.0, jnp.sum(tiles, axis=0))
        turned = tiles.reshape(128, 128).T
        edge = jnp.concatenate([turned[0:8, :], turned[8:16, :]], axis=1)
        edge_high, edge_low = split(jnp.concatenate([edge, jnp.zeros_like(edge)], axis=0))
        mixed = dot3(edge_high, edge_low, e_ref[0], e_ref[1], NN)[0:8, :]
        swapped = pltpu.roll(mixed, 4, 0)
        edge_re = mixed[:, :PART] - swapped[:, PART:]
        edge_im = mixed[:, PART:] + swapped[:, :PART]

        halves = []
        for c in range(2):
            for h in range(2):
                rows = slice(c * 32 + h * 16, c * 32 + h * 16 + 16)
                halves.append(w_ref[k, :, rows, :].reshape(PART, 128).T)
        turned = [jnp.concatenate(halves[c * 2 : c * 2 + 2], axis=0) for c in range(2)]
        high, low = split(jnp.concatenate(turned, axis=1))
        out = dot3(high, low, p_ref[0], p_ref[1], NN)
        c = tw_ref[k, 0:1, :]
        s = tw_ref[k, 1:2, :]
        re, im = out[:, :PART], out[:, PART:]
        back[k, 0] = re * c + im * s
        back[k, 1] = im * c - re * s
        edge_back[k, 0] = edge_re * c + edge_im * s
        edge_back[k, 1] = edge_im * c - edge_re * s
        return carry

    lax.fori_loop(0, RADIX, per_k, 0)
    fetch.wait()
    low_rows = lax.broadcasted_iota(jnp.int32, (8, 128), 0) < 4
    for half in range(2):
        at = slice(half * 128, half * 128 + 128)
        out = dft8([(edge_back[i, 0, :, at], edge_back[i, 1, :, at]) for i in range(RADIX)], 1)
        for i in range(RADIX):
            to = slice(i * PART + half * 128, i * PART + half * 128 + 128)
            for c in range(2):
                value = pltpu.roll(out[i][c], 6, 0)
                x = jnp.where(low_rows, xb_ref[c, 0, :, to], xt_ref[c, 0, :, to])
                parts[c, ROWS:PACK, to] = value + x

    def chunk(t, carry):
        rows = pl.ds(pl.multiple_of(t * 16, 16), 16)
        for half in range(2):
            at = slice(half * 128, half * 128 + 128)
            out = dft8([(back[i, 0, rows, at], back[i, 1, rows, at]) for i in range(RADIX)], 1)
            for i in range(RADIX):
                to = slice(i * PART + half * 128, i * PART + half * 128 + 128)
                for c in range(2):
                    parts[c, rows, to] = x_ref[c, 0, rows, to] + out[i][c]
        return carry

    sends = []
    for q in range(4):
        lax.fori_loop(q * 4, q * 4 + 4, chunk, 0)
        span = pl.ds(q * 64, 72 if q == 3 else 64)
        for c, target in enumerate((re_out, im_out)):
            sends.append(
                pltpu.make_async_copy(
                    parts.at[c, span, :], target.at[span, :], out_sems.at[c, q]
                )
            )
            sends[-1].start()
    for send in sends:
        send.wait()


def rows_back(w, x_now, x_top, x_bottom, table, edge_table, tw):
    anywhere = pl.BlockSpec(memory_space=pl.ANY)
    vmem = pl.BlockSpec(memory_space=pltpu.VMEM)
    return pl.pallas_call(
        rows_back_body,
        in_specs=[anywhere, anywhere, vmem, vmem, anywhere, anywhere, vmem],
        out_specs=[anywhere, anywhere, vmem],
        out_shape=[
            jax.ShapeDtypeStruct((PACK, N), F32),
            jax.ShapeDtypeStruct((PACK, N), F32),
            jax.ShapeDtypeStruct((8, 128), F32),
        ],
        scratch_shapes=[
            pltpu.VMEM((RADIX, 2, ROWS, PART), F32),
            pltpu.VMEM((RADIX, 2, 8, PART), F32),
            pltpu.VMEM((RADIX, 16, MESSAGE, 128), F32),
            pltpu.VMEM((2, 1, ROWS, N), F32),
            pltpu.VMEM((2, PACK, N), F32),
            pltpu.VMEM((2, 2 * PART, 2 * PART), BF16),
            pltpu.VMEM((2, PART, 2 * PART), BF16),
            pltpu.SemaphoreType.DMA((RADIX,)),
            pltpu.SemaphoreType.DMA((3,)),
            pltpu.SemaphoreType.DMA((2, 4)),
        ],
        compiler_params=params(62),
        cost_estimate=pl.CostEstimate(
            flops=4 * 10**9, bytes_accessed=13 * MIB, transcendentals=0
        ),
        name="rows_back",
    )(w, x_now, x_top, x_bottom, table, edge_table, tw)


TILES = EXT // 8
WIDE = 512
STAGES = 4


def shift_up(x, after):
    row = lax.broadcasted_iota(jnp.int32, x.shape, 0)
    return pltpu.roll(jnp.where(row == 0, after, x), 7, 0)


def shift_down(x, before):
    row = lax.broadcasted_iota(jnp.int32, x.shape, 0)
    return pltpu.roll(jnp.where(row == 7, before, x), 1, 0)


def from_right(x, after):
    if after is None:
        col = lax.broadcasted_iota(jnp.int32, x.shape, 1)
        return jnp.where(col == WIDE - 1, x, pltpu.roll(x, WIDE - 1, 1))
    return pltpu.roll(jnp.concatenate([x, after], axis=1), WIDE + 127, 1)[:, :WIDE]


def from_left(x, before):
    if before is None:
        col = lax.broadcasted_iota(jnp.int32, x.shape, 1)
        return jnp.where(col == 0, 0.0, pltpu.roll(x, 1, 1))
    return pltpu.roll(jnp.concatenate([before, x], axis=1), 1, 1)[:, 128:]


def reciprocal(x):
    guess = pl.reciprocal(x, approx=True)
    return guess * (2.0 - x * guess)


def norm(gz, gy, gx):
    square = gz * gz + gy * gy + gx * gx
    return square * lax.rsqrt(square + 1e-30)


def patch(ref, lead, rows, start):
    at = slice(start, start + WIDE)
    after = None
    if start + WIDE < N:
        after = ref[lead + (rows, slice(start + WIDE, start + WIDE + 128))]
    return ref[lead + (rows, at)], after


def arrivals(source, target, q, first, last, sems, edge_sems):
    copies = [
        pltpu.make_async_copy(
            source.at[pl.ds(first, last - first), :],
            target.at[pl.ds(first + 8, last - first), :],
            sems.at[q],
        )
    ]
    halo = source.at[pl.ds(ROWS, 8), :]
    if q == 0:
        copies.append(pltpu.make_async_copy(halo, target.at[pl.ds(0, 8), :], edge_sems.at[0]))
    if q == STAGES - 1:
        copies.append(
            pltpu.make_async_copy(halo, target.at[pl.ds(ROWS + 8, 8), :], edge_sems.at[1])
        )
    return copies


def tv_first_body(
    halves, num_ref, at_ref, own, nxt, prv, inner_out, *rest
):
    high_out = rest[0] if halves else None
    dual_out, ext, inner, dual, in_sems, edge_sems, out_sems = rest[-7:]
    size = ROWS // STAGES
    mains = []
    for q in range(STAGES):
        mains.append([])
        for which, main in enumerate((own, nxt, prv)):
            mains[q] += arrivals(
                main,
                ext.at[which],
                q,
                q * size,
                (q + 1) * size,
                in_sems.at[which],
                edge_sems.at[which],
            )
        for copy in mains[q]:
            copy.start()
    scale = num_ref[0]
    inverse = num_ref[1]
    size_of = num_ref[5]
    keep_next = num_ref[2]
    keep_prev = num_ref[3]
    band = at_ref[0]

    def tile(t, carry):
        rows = pl.ds(pl.multiple_of(t * 8, 8), 8)
        later = pl.ds(pl.multiple_of(jnp.minimum(t + 1, TILES - 1) * 8, 8), 8)
        earlier = pl.ds(pl.multiple_of(jnp.maximum(t - 1, 0) * 8, 8), 8)
        left = None
        for start in range(0, N, WIDE):
            at = slice(start, start + WIDE)
            u, u_after = patch(ext, (0,), rows, start)
            q, q_after = patch(ext, (2,), rows, start)
            gz = (ext[1, rows, at] - u) * keep_next
            gy = shift_up(u, ext[0, later, at]) - u
            gx = from_right(u, u_after) - u
            w = scale * reciprocal(1.0 + size_of * norm(gz, gy, gx))
            dz, dy, dx = gz * w, gy * w, gx * w
            gz = (u - q) * keep_prev
            gy = shift_up(q, ext[2, later, at]) - q
            gx = from_right(q, q_after) - q
            dq = gz * (scale * reciprocal(1.0 + size_of * norm(gz, gy, gx)))
            above = shift_down(dy, dual[1, earlier, at])
            div = (dz - dq) + (dy - above) + (dx - from_left(dx, left))
            left = dx[:, WIDE - 128 :]
            inner[rows, at] = (div + u * inverse) * STEP_TV
            dual[0, rows, at] = dz
            dual[1, rows, at] = dy
            dual[2, rows, at] = dx
            dual[3, rows, at] = dq
        return carry

    outs = []
    done = 0
    for q in range(STAGES):
        for copy in mains[q]:
            copy.wait()
        if q == 0:

            @pl.when(band == 0)
            def _():
                for which in range(3):
                    ext[which, 7:8, :] = ext[which, 8:9, :]

        if q == STAGES - 1:

            @pl.when(band == N // ROWS - 1)
            def _():
                for which in range(3):
                    ext[which, ROWS + 8 : ROWS + 9, :] = ext[which, ROWS + 7 : ROWS + 8, :]

        upto = TILES if q == STAGES - 1 else (q + 1) * size // 8
        lax.fori_loop(done, upto, tile, 0)
        if q == 0:

            @pl.when(band == 0)
            def _():
                inner[7:8, :] = inner[8:9, :]

        if q == STAGES - 1:

            @pl.when(band == N // ROWS - 1)
            def _():
                inner[ROWS + 8 : ROWS + 9, :] = inner[ROWS + 7 : ROWS + 8, :]

        if q == STAGES - 1 and not halves:
            row = lax.broadcasted_iota(jnp.int32, (8, N), 0)
            inner[0:8, :] = jnp.where(row < 4, inner[ROWS + 8 : EXT, :], inner[0:8, :])
            outs.append(
                pltpu.make_async_copy(
                    inner.at[pl.ds(0, 8), :], inner_out.at[pl.ds(ROWS, 8), :], out_sems.at[2, 0]
                )
            )
            outs[-1].start()

        first = max(done, 1)
        last = min(upto, TILES - 1)
        span = pl.ds(done * 8, (upto - done) * 8)
        if halves:
            moves = []
            if done * 8 < HALF + 16:
                moves.append((inner_out, 0, done * 8, min(upto * 8, HALF + 16), 0))
            if upto * 8 > HALF:
                moves.append((high_out, HALF, max(done * 8, HALF), upto * 8, 2))
        else:
            moves = [(inner_out, 8, first * 8, last * 8, 0)]
        for target, shift, begin, end, lane in moves:
            outs.append(
                pltpu.make_async_copy(
                    inner.at[pl.ds(begin, end - begin), :],
                    target.at[pl.ds(begin - shift, end - begin), :],
                    out_sems.at[lane, q],
                )
            )
            outs[-1].start()
        outs.append(
            pltpu.make_async_copy(dual.at[:, span, :], dual_out.at[:, span, :], out_sems.at[1, q])
        )
        outs[-1].start()
        done = upto
    for copy in outs:
        copy.wait()


def tv_first(halves, numbers, place, own, nxt, prv):
    smem = pl.BlockSpec(memory_space=pltpu.SMEM)
    anywhere = pl.BlockSpec(memory_space=pl.ANY)
    inner = [jax.ShapeDtypeStruct((PACK, N), F32)]
    if halves:
        inner = [jax.ShapeDtypeStruct((HALF + 16, N), F32)] * 2
    return pl.pallas_call(
        functools.partial(tv_first_body, halves),
        in_specs=[smem, smem] + [anywhere] * 3,
        out_specs=[anywhere] * (len(inner) + 1),
        out_shape=inner + [jax.ShapeDtypeStruct((4, EXT, N), F32)],
        scratch_shapes=[
            pltpu.VMEM((3, EXT, N), F32),
            pltpu.VMEM((EXT, N), F32),
            pltpu.VMEM((4, EXT, N), F32),
            pltpu.SemaphoreType.DMA((3, STAGES)),
            pltpu.SemaphoreType.DMA((3, 2)),
            pltpu.SemaphoreType.DMA((3, STAGES)),
        ],
        compiler_params=params(63),
        cost_estimate=pl.CostEstimate(
            flops=10**8, bytes_accessed=17 * MIB, transcendentals=2 * 10**6
        ),
        name="tv_first",
    )(numbers, place, own, nxt, prv)


def tv_second_body(
    comp, half, num_ref, own_in, nxt_in, prv_in, dual_in, parts_in, x_prev_in, x_now_in, *rest
):
    out_ref, inner, dual, plain, below, sems, edge_sems, out_sems = rest[-8:]
    count = ROWS if half is None else HALF
    offset = 0 if half is None else HALF * half
    size = ROWS // STAGES
    stages = count // size
    copies = []
    for q in range(stages):
        first = 0 if q == 0 else q * size + 16
        span = pl.ds(first, (q + 1) * size + 16 - first)
        main = pl.ds(q * size, size)
        place = pl.ds(offset + q * size, size)
        dual_span = pl.ds(offset + first, (q + 1) * size + 16 - first)
        begin = 0 if q == 0 else q * size + 8
        end = min((q + 1) * size + 8, ROWS)
        blocks = []
        for i, ref in enumerate((own_in, nxt_in, prv_in)):
            if half is None:
                blocks += arrivals(ref, inner.at[i], q, begin, end, sems.at[i], edge_sems.at[i])
            else:
                blocks.append(
                    pltpu.make_async_copy(ref.at[span, :], inner.at[i, span, :], sems.at[i, q])
                )
        pairs = [
            (dual_in.at[:, dual_span, :], dual.at[:, span, :]),
            (parts_in.at[place, :], plain.at[0, main, :]),
            (x_prev_in.at[comp, 0, place, :], plain.at[1, main, :]),
            (x_now_in.at[comp, 0, place, :], plain.at[2, main, :]),
        ]
        copies.append(
            blocks
            + [pltpu.make_async_copy(a, b, sems.at[i + 3, q]) for i, (a, b) in enumerate(pairs)]
        )
        for copy in copies[-1]:
            copy.start()
    strength = num_ref[4]
    keep_next = num_ref[2]
    keep_prev = num_ref[3]

    def tile(t, carry):
        rows = pl.ds(pl.multiple_of(t * 8, 8), 8)
        later = pl.ds(pl.multiple_of(t * 8 + 8, 8), 8)
        main = pl.ds(pl.multiple_of(jnp.maximum(t - 1, 0) * 8, 8), 8)
        left = None
        for start in range(0, N, WIDE):
            at = slice(start, start + WIDE)
            u, u_after = patch(inner, (0,), rows, start)
            q, q_after = patch(inner, (2,), rows, start)
            gz = (inner[1, rows, at] - u) * keep_next
            gy = shift_up(u, inner[0, later, at]) - u
            gx = from_right(u, u_after) - u
            w = reciprocal(1.0 + norm(gz, gy, gx))
            dz = (dual[0, rows, at] + gz) * w
            dy = (dual[1, rows, at] + gy) * w
            dx = (dual[2, rows, at] + gx) * w
            gz = (u - q) * keep_prev
            gy = shift_up(q, inner[2, later, at]) - q
            gx = from_right(q, q_after) - q
            dq = (dual[3, rows, at] + gz) * reciprocal(1.0 + norm(gz, gy, gx))
            above = shift_down(dy, below[:, at])
            below[:, at] = dy
            div = (dz - dq) + (dy - above) + (dx - from_left(dx, left))
            left = dx[:, WIDE - 128 :]
            denoised = plain[0, main, at] - strength * div
            plain[1, main, at] = (
                (1.0 - ALPHA_TWIST) * plain[1, main, at]
                + (ALPHA_TWIST - BETA_TWIST) * plain[2, main, at]
                + BETA_TWIST * denoised
            )
        return carry

    def first_rows(start):
        at = slice(start, start + WIDE)
        u, u_after = patch(inner, (0,), slice(0, 8), start)
        gz = (inner[1, 0:8, at] - u) * keep_next
        gy = shift_up(u, inner[0, 8:16, at]) - u
        gx = from_right(u, u_after) - u
        below[:, at] = (dual[1, 0:8, at] + gy) * reciprocal(1.0 + norm(gz, gy, gx))

    outs = []
    for q in range(stages):
        for copy in copies[q]:
            copy.wait()
        if q == 0:
            for start in range(0, N, WIDE):
                first_rows(start)
        lax.fori_loop(1 + q * size // 8, 1 + (q + 1) * size // 8, tile, 0)
        main = pl.ds(q * size, size)
        outs.append(
            pltpu.make_async_copy(
                plain.at[1, main, :],
                out_ref.at[comp, 0, pl.ds(offset + q * size, size), :],
                out_sems.at[q],
            )
        )
        outs[-1].start()
    for copy in outs:
        copy.wait()


def tv_second(comp, half, numbers, own, nxt, prv, dual, parts, x_prev, x_now, into):
    smem = pl.BlockSpec(memory_space=pltpu.SMEM)
    anywhere = pl.BlockSpec(memory_space=pl.ANY)
    count = ROWS if half is None else HALF
    args = [numbers, own, nxt, prv, dual, parts, x_prev, x_now]
    aliases = {}
    if into is not None:
        args.append(into)
        aliases = {len(args) - 1: 0}
    return pl.pallas_call(
        functools.partial(tv_second_body, comp, half),
        in_specs=[smem] + [anywhere] * (len(args) - 1),
        out_specs=anywhere,
        out_shape=jax.ShapeDtypeStruct((2, 1, ROWS, N), F32),
        scratch_shapes=[
            pltpu.VMEM((3, count + 16, N), F32),
            pltpu.VMEM((4, count + 16, N), F32),
            pltpu.VMEM((3, count, N), F32),
            pltpu.VMEM((8, N), F32),
            pltpu.SemaphoreType.DMA((7, STAGES)),
            pltpu.SemaphoreType.DMA((3, 2)),
            pltpu.SemaphoreType.DMA((STAGES,)),
        ],
        input_output_aliases=aliases,
        compiler_params=params(63),
        cost_estimate=pl.CostEstimate(
            flops=10**8, bytes_accessed=23 * MIB, transcendentals=2 * 10**6
        ),
        name="tv_second",
    )(*args)


def from_behind(x, axis, by):
    count = lax.axis_size(axis)
    pairs = [(i, i + by) for i in range(count) if 0 <= i + by < count]
    return lax.ppermute(x, axis, pairs)


def signed_freq(freq):
    signed = jnp.where(freq < N // 2, freq, freq - N)
    return signed.astype(F32) * (2.0 * math.pi / N)


def phase_rate(qx_grid, qy_grid):
    square = qx_grid * qx_grid + qy_grid * qy_grid
    return -square / (WAVENUMBER + jnp.sqrt(WAVENUMBER * WAVENUMBER - square))


def shards(x_now, x_prev, hologram, depths):
    d = lax.axis_index("depth")
    r = lax.axis_index("rows")
    forward, inverse = dft_blocks(1.0 / math.sqrt(N))
    g_high, g_low = split_np(forward)
    i_high, i_low = split_np(inverse)
    p_high, p_low = split_np(inverse / PLANES)
    e_high, e_low = split_np(halo_table(inverse / PLANES))
    t_high, t_low = split_np(forward.T)
    pick = np.stack([t_high, t_low]).reshape(2, 2, 16, 16, 2 * PART)
    pick = np.ascontiguousarray(pick.transpose(3, 0, 1, 2, 4)).reshape(16, 2, 32, 2 * PART)
    tw = jnp.asarray(twiddles())
    both = ("rows", "depth")

    chosen = lax.dynamic_index_in_dim(jnp.asarray(pick), d, 0, keepdims=False)
    holo = holo_forward(depths, hologram, chosen[0], chosen[1], tw)
    holo = lax.all_to_all(holo.reshape(128, 8, 128), both, 0, 0, tiled=True)
    depth_all = holo[:PLANES, 4, 0].reshape(1, PLANES)
    kx = r + RADIX * (16 * d + jnp.arange(16, dtype=jnp.int32))
    ky = (
        jnp.arange(RADIX, dtype=jnp.int32)[:, None]
        + RADIX * jnp.arange(PART, dtype=jnp.int32)[None, :]
    )
    rate = phase_rate(signed_freq(kx)[None, :, None], signed_freq(ky)[:, None, :])
    trans = transfer(depth_all, rate)

    sent, squares = rows_forward(x_now, jnp.asarray(np.stack([t_high, t_low])), tw)
    got = lax.all_to_all(sent.reshape(128, 2, 16, ROWS), both, 0, 0, tiled=True)
    x_top = from_behind(x_now[:, :, ROWS - 8 :], "rows", 1)
    x_bottom = from_behind(x_now[:, :, :8], "rows", -1)
    back = spectral(
        got.reshape(RADIX, PLANES, 2, 16, ROWS),
        holo.reshape(RADIX, PLANES, 8, 128),
        trans,
        squares,
        jnp.asarray(np.stack([g_high, g_low, i_high, i_low])),
        tw,
    )
    ret = lax.all_to_all(back.reshape(128, MESSAGE, 128), both, 0, 0, tiled=True)
    re, im, sums = rows_back(
        ret.reshape(RADIX, PLANES, MESSAGE, 128),
        x_now,
        x_top,
        x_bottom,
        jnp.asarray(np.stack([p_high, p_low])),
        jnp.asarray(np.stack([e_high, e_low])),
        tw,
    )

    total = jnp.sum(sums)
    mean_square = jnp.maximum(total, 0.0) / (2.0 * PLANES * N * N)
    strength = LAMBDA_TV * jnp.sqrt(mean_square + EPSILON)
    numbers = jnp.stack(
        [
            -STEP_TV / strength,
            -1.0 / strength,
            (d < PLANES - 1).astype(F32),
            (d > 0).astype(F32),
            strength,
            STEP_TV / strength,
        ]
    )
    place = jnp.stack([r])

    own = (re, im)
    nxt = [from_behind(part, "depth", -1) for part in own]
    prv = [from_behind(part, "depth", 1) for part in own]
    inner_re, dual_re = tv_first(False, numbers, place, own[0], nxt[0], prv[0])
    inner_low, inner_high, dual_im = tv_first(True, numbers, place, own[1], nxt[1], prv[1])
    steps = ((0, None, inner_re, dual_re), (1, 0, inner_low, dual_im), (1, 1, inner_high, dual_im))
    out = None
    for c, half, inner, dual in steps:
        ahead = from_behind(inner, "depth", -1)
        behind = from_behind(inner, "depth", 1)
        out = tv_second(
            c, half, numbers, inner, ahead, behind, dual, own[c], x_prev, x_now, out
        )
    return out


def solution(mesh):
    return jax.shard_map(
        shards,
        mesh=mesh,
        in_specs=(
            P(None, "depth", "rows", None),
            P(None, "depth", "rows", None),
            P(None, "rows", None),
            P("depth"),
        ),
        out_specs=P(None, "depth", "rows", None),
        check_vma=False,
    )
```

```python
import functools
import math

import jax
import jax.numpy as jnp
import ml_dtypes
import numpy as np
from jax import lax
from jax.experimental import pallas as pl
from jax.experimental.pallas import tpu as pltpu
from jax.sharding import PartitionSpec as P

ALPHA_TWIST = 1.8
BETA_TWIST = 1.2
LAMBDA_TV = 0.2
STEP_TV = 1.0 / 12.0
EPSILON = 1e-06
WAVENUMBER = 4.0 * math.pi

N = 2048
PLANES = 16
ROWS = 256
RADIX = 8
PART = 256
EXT = ROWS + 16
PACK = ROWS + 8
HALF = ROWS // 2
F32 = jnp.float32
BF16 = jnp.bfloat16
MIB = 1024 * 1024


def split_np(table):
    high = table.astype(np.float32).astype(ml_dtypes.bfloat16)
    low = (table - high.astype(np.float64)).astype(np.float32).astype(ml_dtypes.bfloat16)
    return high, low


def dft_blocks(scale):
    index = np.arange(PART)
    angle = 2.0 * np.pi * ((index[:, None] * index[None, :]) % PART) / PART
    cos = np.cos(angle) * scale
    sin = np.sin(angle) * scale
    forward = np.block([[cos, -sin], [sin, cos]])
    inverse = np.block([[cos, sin], [-sin, cos]])
    return forward, inverse


def halo_table(inverse):
    rows = inverse[:PART].reshape(16, 2, 8, 2 * PART)
    return np.ascontiguousarray(rows.transpose(1, 0, 2, 3)).reshape(PART, 2 * PART)


def twiddles():
    index = np.arange(PART)
    angle = 2.0 * np.pi * (np.arange(RADIX)[:, None] * index[None, :]) / N
    return np.stack([np.cos(angle), -np.sin(angle)], axis=1).astype(np.float32)


def dft4(a, b, c, d, sign):
    t0 = (a[0] + c[0], a[1] + c[1])
    t1 = (a[0] - c[0], a[1] - c[1])
    t2 = (b[0] + d[0], b[1] + d[1])
    t3 = (b[0] - d[0], b[1] - d[1])
    if sign > 0:
        turned = (-t3[1], t3[0])
    else:
        turned = (t3[1], -t3[0])
    return (
        (t0[0] + t2[0], t0[1] + t2[1]),
        (t1[0] + turned[0], t1[1] + turned[1]),
        (t0[0] - t2[0], t0[1] - t2[1]),
        (t1[0] - turned[0], t1[1] - turned[1]),
    )


def dft8(v, sign):
    even = dft4(v[0], v[2], v[4], v[6], sign)
    odd = dft4(v[1], v[3], v[5], v[7], sign)
    half = math.sqrt(0.5)
    o1, o2, o3 = odd[1], odd[2], odd[3]
    if sign > 0:
        w1 = ((o1[0] - o1[1]) * half, (o1[0] + o1[1]) * half)
        w2 = (-o2[1], o2[0])
        w3 = ((-o3[0] - o3[1]) * half, (o3[0] - o3[1]) * half)
    else:
        w1 = ((o1[0] + o1[1]) * half, (o1[1] - o1[0]) * half)
        w2 = (o2[1], -o2[0])
        w3 = ((o3[1] - o3[0]) * half, (-o3[0] - o3[1]) * half)
    turned = (odd[0], w1, w2, w3)
    low = [(even[k][0] + turned[k][0], even[k][1] + turned[k][1]) for k in range(4)]
    high = [(even[k][0] - turned[k][0], even[k][1] - turned[k][1]) for k in range(4)]
    return low + high


def split(x):
    high = x.astype(BF16)
    return high, (x - high.astype(F32)).astype(BF16)


def dot(a, b, contract):
    return lax.dot_general(a, b, (contract, ((), ())), preferred_element_type=F32)


def dot3(a_high, a_low, b_high, b_low, contract):
    return (
        dot(a_high, b_high, contract) + dot(a_high, b_low, contract) + dot(a_low, b_high, contract)
    )


NT = ((1,), (1,))
NN = ((1,), (0,))


def forward_radix(load, tw_ref, hi, lo, rows, half):
    lanes = slice(half * 128, half * 128 + 128)
    out = dft8([load(i) for i in range(RADIX)], -1)
    for k in range(RADIX):
        re, im = out[k]
        if k:
            c = tw_ref[k, 0:1, lanes]
            s = tw_ref[k, 1:2, lanes]
            re, im = re * c - im * s, re * s + im * c
        for part, value in ((0, re), (1, im)):
            high, low = split(value)
            at = slice(part * PART + half * 128, part * PART + half * 128 + 128)
            hi[k, rows, at] = high
            lo[k, rows, at] = low


def params(limit_mib):
    return pltpu.CompilerParams(vmem_limit_bytes=limit_mib * MIB)


def whole(shape):
    return pl.BlockSpec(shape, lambda *_: (0,) * len(shape))


def stage_copies(pairs, sems):
    copies = [pltpu.make_async_copy(a, b, sems.at[i]) for i, (a, b) in enumerate(pairs)]
    for copy in copies:
        copy.start()
    return copies


def quarter(q):
    return pl.ds(q * (ROWS // 4), ROWS // 4)


def rows_body(x_in, g_in, tw_ref, y_out, ss_ref, hi, lo, x_ref, g_ref, y_ref, sems, out_sems):
    pairs = [(x_in.at[:, :, quarter(q), :], x_ref.at[:, :, quarter(q), :]) for q in range(4)]
    copies = stage_copies(pairs + [(g_in, g_ref)], sems)

    def chunk(t, total):
        rows = pl.ds(pl.multiple_of(t * 16, 16), 16)
        for half in range(2):

            def load(i):
                at = slice(i * PART + half * 128, i * PART + half * 128 + 128)
                return (x_ref[0, 0, rows, at], x_ref[1, 0, rows, at])

            patches = [load(i) for i in range(RADIX)]
            for re, im in patches:
                total = total + (re * re + im * im)
            forward_radix(lambda i: patches[i], tw_ref, hi, lo, rows, half)
        return total

    total = jnp.zeros((16, 128), F32)
    for q in range(4):
        copies[q].wait()
        total = lax.fori_loop(q * 4, q * 4 + 4, chunk, total)
    ss_ref[...] = total
    copies[4].wait()

    def send(k):
        return pltpu.make_async_copy(y_ref.at[k], y_out.at[k], out_sems.at[k])

    def per_k(k, carry):
        high, low = hi[k], lo[k]
        for part in range(2):
            at = slice(part * PART, part * PART + PART)
            out = dot3(g_ref[0, at, :], g_ref[1, at, :], high, low, NT)
            y_ref[k, :, part] = out.reshape(16, 16, ROWS)
        send(k).start()
        return carry

    def finish(k, carry):
        send(k).wait()
        return carry

    lax.fori_loop(0, RADIX, per_k, 0)
    lax.fori_loop(0, RADIX, finish, 0)


def rows_forward(x_now, table, tw):
    anywhere = pl.BlockSpec(memory_space=pl.ANY)
    vmem = pl.BlockSpec(memory_space=pltpu.VMEM)
    return pl.pallas_call(
        rows_body,
        in_specs=[anywhere, anywhere, vmem],
        out_specs=[anywhere, vmem],
        out_shape=[
            jax.ShapeDtypeStruct((RADIX, 16, 2, 16, ROWS), F32),
            jax.ShapeDtypeStruct((16, 128), F32),
        ],
        scratch_shapes=[
            pltpu.VMEM((RADIX, ROWS, 2 * PART), BF16),
            pltpu.VMEM((RADIX, ROWS, 2 * PART), BF16),
            pltpu.VMEM((2, 1, ROWS, N), F32),
            pltpu.VMEM((2, 2 * PART, 2 * PART), BF16),
            pltpu.VMEM((RADIX, 16, 2, 16, ROWS), F32),
            pltpu.SemaphoreType.DMA((5,)),
            pltpu.SemaphoreType.DMA((RADIX,)),
        ],
        compiler_params=params(62),
        cost_estimate=pl.CostEstimate(
            flops=4 * 10**9, bytes_accessed=10 * MIB, transcendentals=0
        ),
        name="rows_forward",
    )(x_now, table, tw)


def holo_body(depth_ref, x_in, gh_ref, gl_ref, tw_ref, y_ref, hi, lo, x_ref, sems):
    pairs = [(x_in.at[:, quarter(q), :], x_ref.at[:, quarter(q), :]) for q in range(4)]
    copies = stage_copies(pairs, sems)

    def chunk(t, carry):
        rows = pl.ds(pl.multiple_of(t * 16, 16), 16)
        for half in range(2):

            def load(i):
                at = slice(i * PART + half * 128, i * PART + half * 128 + 128)
                return (x_ref[0, rows, at], x_ref[1, rows, at])

            forward_radix(load, tw_ref, hi, lo, rows, half)
        return carry

    for q in range(4):
        copies[q].wait()
        lax.fori_loop(q * 4, q * 4 + 4, chunk, 0)
    y_ref[...] = jnp.full(y_ref.shape, depth_ref[0], F32)

    def per_k(k, carry):
        out = dot3(gh_ref[...], gl_ref[...], hi[k], lo[k], NT)
        for part in range(2):
            for half in range(2):
                y_ref[k, :, part * 2 + half, :] = out[
                    part * 16 : part * 16 + 16, half * 128 : half * 128 + 128
                ]
        return carry

    lax.fori_loop(0, RADIX, per_k, 0)


def holo_forward(depths, hologram, gt_high, gt_low, tw):
    return pl.pallas_call(
        holo_body,
        out_shape=jax.ShapeDtypeStruct((RADIX, 16, 8, 128), F32),
        scratch_shapes=[
            pltpu.VMEM((RADIX, ROWS, 2 * PART), BF16),
            pltpu.VMEM((RADIX, ROWS, 2 * PART), BF16),
            pltpu.VMEM((2, ROWS, N), F32),
            pltpu.SemaphoreType.DMA((4,)),
        ],
        in_specs=[
            pl.BlockSpec(memory_space=pltpu.SMEM),
            pl.BlockSpec(memory_space=pl.ANY),
        ]
        + [pl.BlockSpec(memory_space=pltpu.VMEM)] * 3,
        out_specs=pl.BlockSpec(memory_space=pltpu.VMEM),
        compiler_params=params(62),
        cost_estimate=pl.CostEstimate(
            flops=4 * 10**8, bytes_accessed=5 * MIB, transcendentals=0
        ),
        name="holo_forward",
    )(depths, hologram, gt_high, gt_low, tw)


def cos_sin(phase):
    turns = jnp.floor(phase * (2.0 / math.pi) + 0.5)
    rest = phase - turns * 1.5703125
    rest = rest - turns * 4.837512969970703e-4
    rest = rest - turns * 7.549789948768648e-8
    z = rest * rest
    sin = rest + rest * z * (
        -1.6666654611e-1 + z * (8.3321608736e-3 + z * -1.9515295891e-4)
    )
    cos = (
        1.0
        - 0.5 * z
        + z
        * z
        * (4.166664568298827e-2 + z * (-1.388731625493765e-3 + z * 2.443315711809948e-5))
    )
    quarter = turns.astype(jnp.int32) & 3
    odd = (quarter & 1) == 1
    base_cos = jnp.where(odd, sin, cos)
    base_sin = jnp.where(odd, cos, sin)
    out_cos = jnp.where((quarter == 1) | (quarter == 2), -base_cos, base_cos)
    out_sin = jnp.where(quarter >= 2, -base_sin, base_sin)
    return out_cos, out_sin


def transfer_body(depth_ref, rate_ref, t_ref):
    rate = rate_ref[0]
    for p in range(PLANES):
        cos, sin = cos_sin(depth_ref[0, p] * rate)
        rows = slice(p * 16, p * 16 + 16)
        t_ref[0, 0, rows, :] = cos
        t_ref[0, 1, rows, :] = sin


def transfer(depth_all, rate):
    return pl.pallas_call(
        transfer_body,
        grid=(RADIX,),
        in_specs=[
            pl.BlockSpec(memory_space=pltpu.SMEM),
            pl.BlockSpec((1, 16, PART), lambda k: (k, 0, 0)),
        ],
        out_specs=pl.BlockSpec((1, 2, PLANES * 16, PART), lambda k: (k, 0, 0, 0)),
        out_shape=jax.ShapeDtypeStruct((RADIX, 2, PLANES * 16, PART), F32),
        compiler_params=params(62),
        cost_estimate=pl.CostEstimate(
            flops=10**7, bytes_accessed=4 * MIB, transcendentals=0
        ),
        name="transfer",
    )(depth_all, rate)


COLS = PLANES * 16
MESSAGE = 72
WITH_HOLO = COLS + 16


def planes_of(q):
    return pl.ds(q * 4, 4)


def spectral_body(
    z_in, h_in, t_in, sq_ref, g_in, tw_ref, o_out, norm_ref,
    hi, lo, spec, bhi, blo, back, z_ref, g_ref, o_ref, h_ref, t_ref, sems, out_sems, t_sems,
):
    norm_ref[...] = jnp.zeros_like(norm_ref)
    pairs = [(z_in.at[:, planes_of(q)], z_ref.at[:, planes_of(q)]) for q in range(4)]
    copies = stage_copies(pairs + [(h_in, h_ref), (g_in, g_ref)], sems)

    def take(k):
        return pltpu.make_async_copy(t_in.at[k], t_ref.at[k], t_sems.at[k])

    def begin(k, carry):
        take(k).start()
        return carry

    lax.fori_loop(0, RADIX, begin, 0)

    def chunk(p, carry):
        rows = pl.ds(pl.multiple_of(p * 16, 16), 16)
        for half in range(2):
            at = slice(half * 128, half * 128 + 128)

            def load(i):
                return (z_ref[i, p, 0, :, at], z_ref[i, p, 1, :, at])

            forward_radix(load, tw_ref, hi, lo, rows, half)
        return carry

    for q in range(4):
        copies[q].wait()
        lax.fori_loop(q * 4, q * 4 + 4, chunk, 0)
    copies[4].wait()
    for half in range(2):

        def load_holo(i):
            return (h_ref[i, :, half, :], h_ref[i, :, 2 + half, :])

        forward_radix(load_holo, tw_ref, hi, lo, slice(COLS, WITH_HOLO), half)
    copies[5].wait()

    def per_k(k, carry):
        spec[...] = dot3(hi[k], lo[k], g_ref[0], g_ref[1], NN)
        take(k).wait()

        for half in range(2):
            at = slice(half * 128, half * 128 + 128)
            at_im = slice(PART + half * 128, PART + half * 128 + 128)

            def gather(p, total):
                rows = pl.ds(pl.multiple_of(p * 16, 16), 16)
                xr, xi = spec[rows, at], spec[rows, at_im]
                tr, ti = t_ref[k, 0, rows, at], t_ref[k, 1, rows, at]
                return (total[0] + (tr * xr - ti * xi), total[1] + (tr * xi + ti * xr))

            zero = jnp.zeros((16, 128), F32)
            pred = lax.fori_loop(0, PLANES, gather, (zero, zero), unroll=4)
            holo = (spec[COLS:WITH_HOLO, at], spec[COLS:WITH_HOLO, at_im])
            res = (holo[0] - pred[0], holo[1] - pred[1])
            norm_ref[...] += res[0] * (holo[0] + pred[0]) + res[1] * (holo[1] + pred[1])

            def scatter(p, carry):
                rows = pl.ds(pl.multiple_of(p * 16, 16), 16)
                tr, ti = t_ref[k, 0, rows, at], t_ref[k, 1, rows, at]
                br = tr * res[0] + ti * res[1]
                bi = tr * res[1] - ti * res[0]
                for where, value in ((at, br), (at_im, bi)):
                    high, low = split(value)
                    bhi[rows, where] = high
                    blo[rows, where] = low
                return carry

            lax.fori_loop(0, PLANES, scatter, 0, unroll=4)

        c = tw_ref[k, 0:1, :]
        s = tw_ref[k, 1:2, :]
        out = dot3(bhi[...], blo[...], g_ref[2], g_ref[3], NN)
        re, im = out[:, :PART], out[:, PART:]
        back[k, 0] = re * c + im * s
        back[k, 1] = im * c - re * s
        return carry

    lax.fori_loop(0, RADIX, per_k, 0)

    square = sq_ref[...] + norm_ref[...] * (1.0 / PLANES)
    square = square[:8, :] + square[8:, :]
    square = square + pltpu.roll(square, 64, 1)
    lane = lax.broadcasted_iota(jnp.int32, (8, 128), 1)
    square = jnp.where(lane < 64, 0.0, square)

    def chunk(p, carry):
        rows = pl.ds(pl.multiple_of(p * 16, 16), 16)
        for half in range(2):
            at = slice(half * 128, half * 128 + 128)
            out = dft8([(back[i, 0, rows, at], back[i, 1, rows, at]) for i in range(RADIX)], 1)
            for i in range(RADIX):
                o_ref[i, p, half * 16 : half * 16 + 16, :] = out[i][0]
                o_ref[i, p, half * 16 + 32 : half * 16 + 48, :] = out[i][1]
        for i in range(RADIX):
            tile = square
            for high in range(2):
                for c in range(2):
                    low_rows = slice(c * 32 + high * 8, c * 32 + high * 8 + 8)
                    high_rows = slice(c * 32 + 16 + high * 8, c * 32 + 24 + high * 8)
                    edge = jnp.where(
                        lane < 2,
                        o_ref[min(i + 1, RADIX - 1), p, low_rows, :],
                        o_ref[max(i - 1, 0), p, high_rows, :],
                    )
                    base = high * 8 + c * 4
                    edge = pltpu.roll(edge, base + 2, 1)
                    tile = jnp.where((lane >= base) & (lane < base + 4), edge, tile)
            o_ref[i, p, 64:MESSAGE, :] = tile
        return carry

    sends = []
    for q in range(4):
        lax.fori_loop(q * 4, q * 4 + 4, chunk, 0)
        sends.append(
            pltpu.make_async_copy(
                o_ref.at[:, planes_of(q)], o_out.at[:, planes_of(q)], out_sems.at[q]
            )
        )
        sends[-1].start()
    for send in sends:
        send.wait()


def spectral(z, holo, trans, squares, table, tw):
    anywhere = pl.BlockSpec(memory_space=pl.ANY)
    vmem = pl.BlockSpec(memory_space=pltpu.VMEM)
    return pl.pallas_call(
        spectral_body,
        in_specs=[anywhere, anywhere, anywhere, vmem, anywhere, vmem],
        out_specs=anywhere,
        out_shape=jax.ShapeDtypeStruct((RADIX, PLANES, MESSAGE, 128), F32),
        scratch_shapes=[
            pltpu.VMEM((16, 128), F32),
            pltpu.VMEM((RADIX, WITH_HOLO, 2 * PART), BF16),
            pltpu.VMEM((RADIX, WITH_HOLO, 2 * PART), BF16),
            pltpu.VMEM((WITH_HOLO, 2 * PART), F32),
            pltpu.VMEM((COLS, 2 * PART), BF16),
            pltpu.VMEM((COLS, 2 * PART), BF16),
            pltpu.VMEM((RADIX, 2, COLS, PART), F32),
            pltpu.VMEM((RADIX, PLANES, 2, 16, PART), F32),
            pltpu.VMEM((4, 2 * PART, 2 * PART), BF16),
            pltpu.VMEM((RADIX, PLANES, MESSAGE, 128), F32),
            pltpu.VMEM((RADIX, 16, 8, 128), F32),
            pltpu.VMEM((RADIX, 2, COLS, PART), F32),
            pltpu.SemaphoreType.DMA((6,)),
            pltpu.SemaphoreType.DMA((4,)),
            pltpu.SemaphoreType.DMA((RADIX,)),
        ],
        compiler_params=params(62),
        cost_estimate=pl.CostEstimate(
            flops=8 * 10**9, bytes_accessed=14 * MIB, transcendentals=0
        ),
        name="spectral",
    )(z, holo, trans, squares, table, tw)


def rows_back_body(
    w_in, x_in, xt_ref, xb_ref, p_in, e_in, tw_ref, re_out, im_out, sum_ref,
    back, edge_back, w_ref, x_ref, parts, p_ref, e_ref, w_sems, sems, out_sems,
):
    tables = stage_copies([(p_in, p_ref), (e_in, e_ref)], sems)

    def take(k):
        return pltpu.make_async_copy(w_in.at[k], w_ref.at[k], w_sems.at[k])

    def begin(k, carry):
        take(k).start()
        return carry

    lax.fori_loop(0, RADIX, begin, 0)
    fetch = pltpu.make_async_copy(x_in, x_ref, sems.at[2])
    fetch.start()
    sum_ref[...] = jnp.zeros_like(sum_ref)
    for copy in tables:
        copy.wait()

    def per_k(k, carry):
        take(k).wait()
        tiles = w_ref[k, :, 64:MESSAGE, :]
        lane = lax.broadcasted_iota(jnp.int32, (8, 128), 1)
        sum_ref[...] += jnp.where(lane < 64, 0.0, jnp.sum(tiles, axis=0))
        turned = tiles.reshape(128, 128).T
        edge = jnp.concatenate([turned[0:8, :], turned[8:16, :]], axis=1)
        edge_high, edge_low = split(jnp.concatenate([edge, jnp.zeros_like(edge)], axis=0))
        mixed = dot3(edge_high, edge_low, e_ref[0], e_ref[1], NN)[0:8, :]
        swapped = pltpu.roll(mixed, 4, 0)
        edge_re = mixed[:, :PART] - swapped[:, PART:]
        edge_im = mixed[:, PART:] + swapped[:, :PART]

        halves = []
        for c in range(2):
            for h in range(2):
                rows = slice(c * 32 + h * 16, c * 32 + h * 16 + 16)
                halves.append(w_ref[k, :, rows, :].reshape(PART, 128).T)
        turned = [jnp.concatenate(halves[c * 2 : c * 2 + 2], axis=0) for c in range(2)]
        high, low = split(jnp.concatenate(turned, axis=1))
        out = dot3(high, low, p_ref[0], p_ref[1], NN)
        c = tw_ref[k, 0:1, :]
        s = tw_ref[k, 1:2, :]
        re, im = out[:, :PART], out[:, PART:]
        back[k, 0] = re * c + im * s
        back[k, 1] = im * c - re * s
        edge_back[k, 0] = edge_re * c + edge_im * s
        edge_back[k, 1] = edge_im * c - edge_re * s
        return carry

    lax.fori_loop(0, RADIX, per_k, 0)
    fetch.wait()
    low_rows = lax.broadcasted_iota(jnp.int32, (8, 128), 0) < 4
    for half in range(2):
        at = slice(half * 128, half * 128 + 128)
        out = dft8([(edge_back[i, 0, :, at], edge_back[i, 1, :, at]) for i in range(RADIX)], 1)
        for i in range(RADIX):
            to = slice(i * PART + half * 128, i * PART + half * 128 + 128)
            for c in range(2):
                value = pltpu.roll(out[i][c], 6, 0)
                x = jnp.where(low_rows, xb_ref[c, 0, :, to], xt_ref[c, 0, :, to])
                parts[c, ROWS:PACK, to] = value + x

    def chunk(t, carry):
        rows = pl.ds(pl.multiple_of(t * 16, 16), 16)
        for half in range(2):
            at = slice(half * 128, half * 128 + 128)
            out = dft8([(back[i, 0, rows, at], back[i, 1, rows, at]) for i in range(RADIX)], 1)
            for i in range(RADIX):
                to = slice(i * PART + half * 128, i * PART + half * 128 + 128)
                for c in range(2):
                    parts[c, rows, to] = x_ref[c, 0, rows, to] + out[i][c]
        return carry

    sends = []
    for q in range(4):
        lax.fori_loop(q * 4, q * 4 + 4, chunk, 0)
        span = pl.ds(q * 64, 72 if q == 3 else 64)
        for c, target in enumerate((re_out, im_out)):
            sends.append(
                pltpu.make_async_copy(
                    parts.at[c, span, :], target.at[span, :], out_sems.at[c, q]
                )
            )
            sends[-1].start()
    for send in sends:
        send.wait()


def rows_back(w, x_now, x_top, x_bottom, table, edge_table, tw):
    anywhere = pl.BlockSpec(memory_space=pl.ANY)
    vmem = pl.BlockSpec(memory_space=pltpu.VMEM)
    return pl.pallas_call(
        rows_back_body,
        in_specs=[anywhere, anywhere, vmem, vmem, anywhere, anywhere, vmem],
        out_specs=[anywhere, anywhere, vmem],
        out_shape=[
            jax.ShapeDtypeStruct((PACK, N), F32),
            jax.ShapeDtypeStruct((PACK, N), F32),
            jax.ShapeDtypeStruct((8, 128), F32),
        ],
        scratch_shapes=[
            pltpu.VMEM((RADIX, 2, ROWS, PART), F32),
            pltpu.VMEM((RADIX, 2, 8, PART), F32),
            pltpu.VMEM((RADIX, 16, MESSAGE, 128), F32),
            pltpu.VMEM((2, 1, ROWS, N), F32),
            pltpu.VMEM((2, PACK, N), F32),
            pltpu.VMEM((2, 2 * PART, 2 * PART), BF16),
            pltpu.VMEM((2, PART, 2 * PART), BF16),
            pltpu.SemaphoreType.DMA((RADIX,)),
            pltpu.SemaphoreType.DMA((3,)),
            pltpu.SemaphoreType.DMA((2, 4)),
        ],
        compiler_params=params(62),
        cost_estimate=pl.CostEstimate(
            flops=4 * 10**9, bytes_accessed=13 * MIB, transcendentals=0
        ),
        name="rows_back",
    )(w, x_now, x_top, x_bottom, table, edge_table, tw)


TILES = EXT // 8
WIDE = 512
STAGES = 4


def shift_up(x, after):
    row = lax.broadcasted_iota(jnp.int32, x.shape, 0)
    return pltpu.roll(jnp.where(row == 0, after, x), 7, 0)


def shift_down(x, before):
    row = lax.broadcasted_iota(jnp.int32, x.shape, 0)
    return pltpu.roll(jnp.where(row == 7, before, x), 1, 0)


def from_right(x, after):
    if after is None:
        col = lax.broadcasted_iota(jnp.int32, x.shape, 1)
        return jnp.where(col == WIDE - 1, x, pltpu.roll(x, WIDE - 1, 1))
    return pltpu.roll(jnp.concatenate([x, after], axis=1), WIDE + 127, 1)[:, :WIDE]


def from_left(x, before):
    if before is None:
        col = lax.broadcasted_iota(jnp.int32, x.shape, 1)
        return jnp.where(col == 0, 0.0, pltpu.roll(x, 1, 1))
    return pltpu.roll(jnp.concatenate([before, x], axis=1), 1, 1)[:, 128:]


def reciprocal(x):
    guess = pl.reciprocal(x, approx=True)
    return guess * (2.0 - x * guess)


def norm(gz, gy, gx):
    square = gz * gz + gy * gy + gx * gx
    return square * lax.rsqrt(square + 1e-30)


def patch(ref, lead, rows, start):
    at = slice(start, start + WIDE)
    after = None
    if start + WIDE < N:
        after = ref[lead + (rows, slice(start + WIDE, start + WIDE + 128))]
    return ref[lead + (rows, at)], after


def arrivals(source, target, q, first, last, sems, edge_sems):
    copies = [
        pltpu.make_async_copy(
            source.at[pl.ds(first, last - first), :],
            target.at[pl.ds(first + 8, last - first), :],
            sems.at[q],
        )
    ]
    halo = source.at[pl.ds(ROWS, 8), :]
    if q == 0:
        copies.append(pltpu.make_async_copy(halo, target.at[pl.ds(0, 8), :], edge_sems.at[0]))
    if q == STAGES - 1:
        copies.append(
            pltpu.make_async_copy(halo, target.at[pl.ds(ROWS + 8, 8), :], edge_sems.at[1])
        )
    return copies


def tv_first_body(
    halves, num_ref, at_ref, own, nxt, prv, inner_out, *rest
):
    high_out = rest[0] if halves else None
    dual_out, ext, inner, dual, in_sems, edge_sems, out_sems = rest[-7:]
    size = ROWS // STAGES
    mains = []
    for q in range(STAGES):
        mains.append([])
        for which, main in enumerate((own, nxt, prv)):
            mains[q] += arrivals(
                main,
                ext.at[which],
                q,
                q * size,
                (q + 1) * size,
                in_sems.at[which],
                edge_sems.at[which],
            )
        for copy in mains[q]:
            copy.start()
    scale = num_ref[0]
    inverse = num_ref[1]
    size_of = num_ref[5]
    keep_next = num_ref[2]
    keep_prev = num_ref[3]
    band = at_ref[0]

    def tile(t, carry):
        rows = pl.ds(pl.multiple_of(t * 8, 8), 8)
        later = pl.ds(pl.multiple_of(jnp.minimum(t + 1, TILES - 1) * 8, 8), 8)
        earlier = pl.ds(pl.multiple_of(jnp.maximum(t - 1, 0) * 8, 8), 8)
        left = None
        for start in range(0, N, WIDE):
            at = slice(start, start + WIDE)
            u, u_after = patch(ext, (0,), rows, start)
            q, q_after = patch(ext, (2,), rows, start)
            gz = (ext[1, rows, at] - u) * keep_next
            gy = shift_up(u, ext[0, later, at]) - u
            gx = from_right(u, u_after) - u
            w = scale * reciprocal(1.0 + size_of * norm(gz, gy, gx))
            dz, dy, dx = gz * w, gy * w, gx * w
            gz = (u - q) * keep_prev
            gy = shift_up(q, ext[2, later, at]) - q
            gx = from_right(q, q_after) - q
            dq = gz * (scale * reciprocal(1.0 + size_of * norm(gz, gy, gx)))
            above = shift_down(dy, dual[1, earlier, at])
            div = (dz - dq) + (dy - above) + (dx - from_left(dx, left))
            left = dx[:, WIDE - 128 :]
            inner[rows, at] = (div + u * inverse) * STEP_TV
            dual[0, rows, at] = dz
            dual[1, rows, at] = dy
            dual[2, rows, at] = dx
            dual[3, rows, at] = dq
        return carry

    outs = []
    done = 0
    for q in range(STAGES):
        for copy in mains[q]:
            copy.wait()
        if q == 0:

            @pl.when(band == 0)
            def _():
                for which in range(3):
                    ext[which, 7:8, :] = ext[which, 8:9, :]

        if q == STAGES - 1:

            @pl.when(band == N // ROWS - 1)
            def _():
                for which in range(3):
                    ext[which, ROWS + 8 : ROWS + 9, :] = ext[which, ROWS + 7 : ROWS + 8, :]

        upto = TILES if q == STAGES - 1 else (q + 1) * size // 8
        lax.fori_loop(done, upto, tile, 0)
        if q == 0:

            @pl.when(band == 0)
            def _():
                inner[7:8, :] = inner[8:9, :]

        if q == STAGES - 1:

            @pl.when(band == N // ROWS - 1)
            def _():
                inner[ROWS + 8 : ROWS + 9, :] = inner[ROWS + 7 : ROWS + 8, :]

        if q == STAGES - 1 and not halves:
            row = lax.broadcasted_iota(jnp.int32, (8, N), 0)
            inner[0:8, :] = jnp.where(row < 4, inner[ROWS + 8 : EXT, :], inner[0:8, :])
            outs.append(
                pltpu.make_async_copy(
                    inner.at[pl.ds(0, 8), :], inner_out.at[pl.ds(ROWS, 8), :], out_sems.at[2, 0]
                )
            )
            outs[-1].start()

        first = max(done, 1)
        last = min(upto, TILES - 1)
        span = pl.ds(done * 8, (upto - done) * 8)
        if halves:
            moves = []
            if done * 8 < HALF + 16:
                moves.append((inner_out, 0, done * 8, min(upto * 8, HALF + 16), 0))
            if upto * 8 > HALF:
                moves.append((high_out, HALF, max(done * 8, HALF), upto * 8, 2))
        else:
            moves = [(inner_out, 8, first * 8, last * 8, 0)]
        for target, shift, begin, end, lane in moves:
            outs.append(
                pltpu.make_async_copy(
                    inner.at[pl.ds(begin, end - begin), :],
                    target.at[pl.ds(begin - shift, end - begin), :],
                    out_sems.at[lane, q],
                )
            )
            outs[-1].start()
        outs.append(
            pltpu.make_async_copy(dual.at[:, span, :], dual_out.at[:, span, :], out_sems.at[1, q])
        )
        outs[-1].start()
        done = upto
    for copy in outs:
        copy.wait()


def tv_first(halves, numbers, place, own, nxt, prv):
    smem = pl.BlockSpec(memory_space=pltpu.SMEM)
    anywhere = pl.BlockSpec(memory_space=pl.ANY)
    inner = [jax.ShapeDtypeStruct((PACK, N), F32)]
    if halves:
        inner = [jax.ShapeDtypeStruct((HALF + 16, N), F32)] * 2
    return pl.pallas_call(
        functools.partial(tv_first_body, halves),
        in_specs=[smem, smem] + [anywhere] * 3,
        out_specs=[anywhere] * (len(inner) + 1),
        out_shape=inner + [jax.ShapeDtypeStruct((4, EXT, N), F32)],
        scratch_shapes=[
            pltpu.VMEM((3, EXT, N), F32),
            pltpu.VMEM((EXT, N), F32),
            pltpu.VMEM((4, EXT, N), F32),
            pltpu.SemaphoreType.DMA((3, STAGES)),
            pltpu.SemaphoreType.DMA((3, 2)),
            pltpu.SemaphoreType.DMA((3, STAGES)),
        ],
        compiler_params=params(63),
        cost_estimate=pl.CostEstimate(
            flops=10**8, bytes_accessed=17 * MIB, transcendentals=2 * 10**6
        ),
        name="tv_first",
    )(numbers, place, own, nxt, prv)


def tv_second_body(
    comp, half, num_ref, own_in, nxt_in, prv_in, dual_in, parts_in, x_prev_in, x_now_in, *rest
):
    out_ref, inner, dual, plain, below, sems, edge_sems, out_sems = rest[-8:]
    count = ROWS if half is None else HALF
    offset = 0 if half is None else HALF * half
    size = count // STAGES
    stages = STAGES
    copies = []
    for q in range(stages):
        first = 0 if q == 0 else q * size + 16
        span = pl.ds(first, (q + 1) * size + 16 - first)
        main = pl.ds(q * size, size)
        place = pl.ds(offset + q * size, size)
        dual_span = pl.ds(offset + first, (q + 1) * size + 16 - first)
        begin = 0 if q == 0 else q * size + 8
        end = min((q + 1) * size + 8, ROWS)
        blocks = []
        for i, ref in enumerate((own_in, nxt_in, prv_in)):
            if half is None:
                blocks += arrivals(ref, inner.at[i], q, begin, end, sems.at[i], edge_sems.at[i])
            else:
                blocks.append(
                    pltpu.make_async_copy(ref.at[span, :], inner.at[i, span, :], sems.at[i, q])
                )
        pairs = [
            (dual_in.at[:, dual_span, :], dual.at[:, span, :]),
            (parts_in.at[place, :], plain.at[0, main, :]),
            (x_prev_in.at[comp, 0, place, :], plain.at[1, main, :]),
            (x_now_in.at[comp, 0, place, :], plain.at[2, main, :]),
        ]
        copies.append(
            blocks
            + [pltpu.make_async_copy(a, b, sems.at[i + 3, q]) for i, (a, b) in enumerate(pairs)]
        )
        for copy in copies[-1]:
            copy.start()
    strength = num_ref[4]
    keep_next = num_ref[2]
    keep_prev = num_ref[3]

    def tile(t, carry):
        rows = pl.ds(pl.multiple_of(t * 8, 8), 8)
        later = pl.ds(pl.multiple_of(t * 8 + 8, 8), 8)
        main = pl.ds(pl.multiple_of(jnp.maximum(t - 1, 0) * 8, 8), 8)
        left = None
        for start in range(0, N, WIDE):
            at = slice(start, start + WIDE)
            u, u_after = patch(inner, (0,), rows, start)
            q, q_after = patch(inner, (2,), rows, start)
            gz = (inner[1, rows, at] - u) * keep_next
            gy = shift_up(u, inner[0, later, at]) - u
            gx = from_right(u, u_after) - u
            w = reciprocal(1.0 + norm(gz, gy, gx))
            dz = (dual[0, rows, at] + gz) * w
            dy = (dual[1, rows, at] + gy) * w
            dx = (dual[2, rows, at] + gx) * w
            gz = (u - q) * keep_prev
            gy = shift_up(q, inner[2, later, at]) - q
            gx = from_right(q, q_after) - q
            dq = (dual[3, rows, at] + gz) * reciprocal(1.0 + norm(gz, gy, gx))
            above = shift_down(dy, below[:, at])
            below[:, at] = dy
            div = (dz - dq) + (dy - above) + (dx - from_left(dx, left))
            left = dx[:, WIDE - 128 :]
            denoised = plain[0, main, at] - strength * div
            plain[1, main, at] = (
                (1.0 - ALPHA_TWIST) * plain[1, main, at]
                + (ALPHA_TWIST - BETA_TWIST) * plain[2, main, at]
                + BETA_TWIST * denoised
            )
        return carry

    def first_rows(start):
        at = slice(start, start + WIDE)
        u, u_after = patch(inner, (0,), slice(0, 8), start)
        gz = (inner[1, 0:8, at] - u) * keep_next
        gy = shift_up(u, inner[0, 8:16, at]) - u
        gx = from_right(u, u_after) - u
        below[:, at] = (dual[1, 0:8, at] + gy) * reciprocal(1.0 + norm(gz, gy, gx))

    outs = []
    for q in range(stages):
        for copy in copies[q]:
            copy.wait()
        if q == 0:
            for start in range(0, N, WIDE):
                first_rows(start)
        lax.fori_loop(1 + q * size // 8, 1 + (q + 1) * size // 8, tile, 0)
        main = pl.ds(q * size, size)
        outs.append(
            pltpu.make_async_copy(
                plain.at[1, main, :],
                out_ref.at[comp, 0, pl.ds(offset + q * size, size), :],
                out_sems.at[q],
            )
        )
        outs[-1].start()
    for copy in outs:
        copy.wait()


def tv_second(comp, half, numbers, own, nxt, prv, dual, parts, x_prev, x_now, into):
    smem = pl.BlockSpec(memory_space=pltpu.SMEM)
    anywhere = pl.BlockSpec(memory_space=pl.ANY)
    count = ROWS if half is None else HALF
    args = [numbers, own, nxt, prv, dual, parts, x_prev, x_now]
    aliases = {}
    if into is not None:
        args.append(into)
        aliases = {len(args) - 1: 0}
    return pl.pallas_call(
        functools.partial(tv_second_body, comp, half),
        in_specs=[smem] + [anywhere] * (len(args) - 1),
        out_specs=anywhere,
        out_shape=jax.ShapeDtypeStruct((2, 1, ROWS, N), F32),
        scratch_shapes=[
            pltpu.VMEM((3, count + 16, N), F32),
            pltpu.VMEM((4, count + 16, N), F32),
            pltpu.VMEM((3, count, N), F32),
            pltpu.VMEM((8, N), F32),
            pltpu.SemaphoreType.DMA((7, STAGES)),
            pltpu.SemaphoreType.DMA((3, 2)),
            pltpu.SemaphoreType.DMA((STAGES,)),
        ],
        input_output_aliases=aliases,
        compiler_params=params(63),
        cost_estimate=pl.CostEstimate(
            flops=10**8, bytes_accessed=23 * MIB, transcendentals=2 * 10**6
        ),
        name="tv_second",
    )(*args)


def from_behind(x, axis, by):
    count = lax.axis_size(axis)
    pairs = [(i, i + by) for i in range(count) if 0 <= i + by < count]
    return lax.ppermute(x, axis, pairs)


def signed_freq(freq):
    signed = jnp.where(freq < N // 2, freq, freq - N)
    return signed.astype(F32) * (2.0 * math.pi / N)


def phase_rate(qx_grid, qy_grid):
    square = qx_grid * qx_grid + qy_grid * qy_grid
    return -square / (WAVENUMBER + jnp.sqrt(WAVENUMBER * WAVENUMBER - square))


def shards(x_now, x_prev, hologram, depths):
    d = lax.axis_index("depth")
    r = lax.axis_index("rows")
    forward, inverse = dft_blocks(1.0 / math.sqrt(N))
    g_high, g_low = split_np(forward)
    i_high, i_low = split_np(inverse)
    p_high, p_low = split_np(inverse / PLANES)
    e_high, e_low = split_np(halo_table(inverse / PLANES))
    t_high, t_low = split_np(forward.T)
    pick = np.stack([t_high, t_low]).reshape(2, 2, 16, 16, 2 * PART)
    pick = np.ascontiguousarray(pick.transpose(3, 0, 1, 2, 4)).reshape(16, 2, 32, 2 * PART)
    tw = jnp.asarray(twiddles())
    both = ("rows", "depth")

    chosen = lax.dynamic_index_in_dim(jnp.asarray(pick), d, 0, keepdims=False)
    holo = holo_forward(depths, hologram, chosen[0], chosen[1], tw)
    holo = lax.all_to_all(holo.reshape(128, 8, 128), both, 0, 0, tiled=True)
    depth_all = holo[:PLANES, 4, 0].reshape(1, PLANES)
    kx = r + RADIX * (16 * d + jnp.arange(16, dtype=jnp.int32))
    ky = (
        jnp.arange(RADIX, dtype=jnp.int32)[:, None]
        + RADIX * jnp.arange(PART, dtype=jnp.int32)[None, :]
    )
    rate = phase_rate(signed_freq(kx)[None, :, None], signed_freq(ky)[:, None, :])
    trans = transfer(depth_all, rate)

    sent, squares = rows_forward(x_now, jnp.asarray(np.stack([t_high, t_low])), tw)
    got = lax.all_to_all(sent.reshape(128, 2, 16, ROWS), both, 0, 0, tiled=True)
    x_top = from_behind(x_now[:, :, ROWS - 8 :], "rows", 1)
    x_bottom = from_behind(x_now[:, :, :8], "rows", -1)
    back = spectral(
        got.reshape(RADIX, PLANES, 2, 16, ROWS),
        holo.reshape(RADIX, PLANES, 8, 128),
        trans,
        squares,
        jnp.asarray(np.stack([g_high, g_low, i_high, i_low])),
        tw,
    )
    ret = lax.all_to_all(back.reshape(128, MESSAGE, 128), both, 0, 0, tiled=True)
    re, im, sums = rows_back(
        ret.reshape(RADIX, PLANES, MESSAGE, 128),
        x_now,
        x_top,
        x_bottom,
        jnp.asarray(np.stack([p_high, p_low])),
        jnp.asarray(np.stack([e_high, e_low])),
        tw,
    )

    total = jnp.sum(sums)
    mean_square = jnp.maximum(total, 0.0) / (2.0 * PLANES * N * N)
    strength = LAMBDA_TV * jnp.sqrt(mean_square + EPSILON)
    numbers = jnp.stack(
        [
            -STEP_TV / strength,
            -1.0 / strength,
            (d < PLANES - 1).astype(F32),
            (d > 0).astype(F32),
            strength,
            STEP_TV / strength,
        ]
    )
    place = jnp.stack([r])

    own = (re, im)
    nxt = [from_behind(part, "depth", -1) for part in own]
    prv = [from_behind(part, "depth", 1) for part in own]
    inner_re, dual_re = tv_first(False, numbers, place, own[0], nxt[0], prv[0])
    inner_low, inner_high, dual_im = tv_first(True, numbers, place, own[1], nxt[1], prv[1])
    steps = ((0, None, inner_re, dual_re), (1, 0, inner_low, dual_im), (1, 1, inner_high, dual_im))
    out = None
    for c, half, inner, dual in steps:
        ahead = from_behind(inner, "depth", -1)
        behind = from_behind(inner, "depth", 1)
        out = tv_second(
            c, half, numbers, inner, ahead, behind, dual, own[c], x_prev, x_now, out
        )
    return out


def solution(mesh):
    return jax.shard_map(
        shards,
        mesh=mesh,
        in_specs=(
            P(None, "depth", "rows", None),
            P(None, "depth", "rows", None),
            P(None, "rows", None),
            P("depth"),
        ),
        out_specs=P(None, "depth", "rows", None),
        check_vma=False,
    )
```

```python
import functools
import math

import jax
import jax.numpy as jnp
import ml_dtypes
import numpy as np
from jax import lax
from jax.experimental import pallas as pl
from jax.experimental.pallas import tpu as pltpu
from jax.sharding import PartitionSpec as P

ALPHA_TWIST = 1.8
BETA_TWIST = 1.2
LAMBDA_TV = 0.2
STEP_TV = 1.0 / 12.0
EPSILON = 1e-06
WAVENUMBER = 4.0 * math.pi

N = 2048
PLANES = 16
ROWS = 256
RADIX = 8
PART = 256
EXT = ROWS + 16
PACK = ROWS + 8
HALF = ROWS // 2
F32 = jnp.float32
BF16 = jnp.bfloat16
MIB = 1024 * 1024


def split_np(table):
    high = table.astype(np.float32).astype(ml_dtypes.bfloat16)
    low = (table - high.astype(np.float64)).astype(np.float32).astype(ml_dtypes.bfloat16)
    return high, low


def dft_blocks(scale):
    index = np.arange(PART)
    angle = 2.0 * np.pi * ((index[:, None] * index[None, :]) % PART) / PART
    cos = np.cos(angle) * scale
    sin = np.sin(angle) * scale
    forward = np.block([[cos, -sin], [sin, cos]])
    inverse = np.block([[cos, sin], [-sin, cos]])
    return forward, inverse


def halo_table(inverse):
    rows = inverse[:PART].reshape(16, 2, 8, 2 * PART)
    return np.ascontiguousarray(rows.transpose(1, 0, 2, 3)).reshape(PART, 2 * PART)


def twiddles():
    index = np.arange(PART)
    angle = 2.0 * np.pi * (np.arange(RADIX)[:, None] * index[None, :]) / N
    return np.stack([np.cos(angle), -np.sin(angle)], axis=1).astype(np.float32)


def dft4(a, b, c, d, sign):
    t0 = (a[0] + c[0], a[1] + c[1])
    t1 = (a[0] - c[0], a[1] - c[1])
    t2 = (b[0] + d[0], b[1] + d[1])
    t3 = (b[0] - d[0], b[1] - d[1])
    if sign > 0:
        turned = (-t3[1], t3[0])
    else:
        turned = (t3[1], -t3[0])
    return (
        (t0[0] + t2[0], t0[1] + t2[1]),
        (t1[0] + turned[0], t1[1] + turned[1]),
        (t0[0] - t2[0], t0[1] - t2[1]),
        (t1[0] - turned[0], t1[1] - turned[1]),
    )


def dft8(v, sign):
    even = dft4(v[0], v[2], v[4], v[6], sign)
    odd = dft4(v[1], v[3], v[5], v[7], sign)
    half = math.sqrt(0.5)
    o1, o2, o3 = odd[1], odd[2], odd[3]
    if sign > 0:
        w1 = ((o1[0] - o1[1]) * half, (o1[0] + o1[1]) * half)
        w2 = (-o2[1], o2[0])
        w3 = ((-o3[0] - o3[1]) * half, (o3[0] - o3[1]) * half)
    else:
        w1 = ((o1[0] + o1[1]) * half, (o1[1] - o1[0]) * half)
        w2 = (o2[1], -o2[0])
        w3 = ((o3[1] - o3[0]) * half, (-o3[0] - o3[1]) * half)
    turned = (odd[0], w1, w2, w3)
    low = [(even[k][0] + turned[k][0], even[k][1] + turned[k][1]) for k in range(4)]
    high = [(even[k][0] - turned[k][0], even[k][1] - turned[k][1]) for k in range(4)]
    return low + high


def split(x):
    high = x.astype(BF16)
    return high, (x - high.astype(F32)).astype(BF16)


def dot(a, b, contract):
    return lax.dot_general(a, b, (contract, ((), ())), preferred_element_type=F32)


def dot3(a_high, a_low, b_high, b_low, contract):
    return (
        dot(a_high, b_high, contract) + dot(a_high, b_low, contract) + dot(a_low, b_high, contract)
    )


NT = ((1,), (1,))
NN = ((1,), (0,))


def forward_radix(load, tw_ref, hi, lo, rows, half):
    lanes = slice(half * 128, half * 128 + 128)
    out = dft8([load(i) for i in range(RADIX)], -1)
    for k in range(RADIX):
        re, im = out[k]
        if k:
            c = tw_ref[k, 0:1, lanes]
            s = tw_ref[k, 1:2, lanes]
            re, im = re * c - im * s, re * s + im * c
        for part, value in ((0, re), (1, im)):
            high, low = split(value)
            at = slice(part * PART + half * 128, part * PART + half * 128 + 128)
            hi[k, rows, at] = high
            lo[k, rows, at] = low


def params(limit_mib):
    return pltpu.CompilerParams(vmem_limit_bytes=limit_mib * MIB)


def whole(shape):
    return pl.BlockSpec(shape, lambda *_: (0,) * len(shape))


def stage_copies(pairs, sems):
    copies = [pltpu.make_async_copy(a, b, sems.at[i]) for i, (a, b) in enumerate(pairs)]
    for copy in copies:
        copy.start()
    return copies


PIECES = 8


def piece(q):
    return pl.ds(q * (ROWS // PIECES), ROWS // PIECES)


def rows_body(x_in, g_in, tw_ref, y_out, ss_ref, hi, lo, x_ref, g_ref, y_ref, sems, out_sems):
    pairs = [(x_in.at[:, :, piece(q), :], x_ref.at[:, :, piece(q), :]) for q in range(PIECES)]
    copies = stage_copies(pairs + [(g_in, g_ref)], sems)

    def chunk(t, total):
        rows = pl.ds(pl.multiple_of(t * 16, 16), 16)
        for half in range(2):

            def load(i):
                at = slice(i * PART + half * 128, i * PART + half * 128 + 128)
                return (x_ref[0, 0, rows, at], x_ref[1, 0, rows, at])

            patches = [load(i) for i in range(RADIX)]
            for re, im in patches:
                total = total + (re * re + im * im)
            forward_radix(lambda i: patches[i], tw_ref, hi, lo, rows, half)
        return total

    total = jnp.zeros((16, 128), F32)
    for q in range(PIECES):
        copies[q].wait()
        total = lax.fori_loop(q * 2, q * 2 + 2, chunk, total)
    ss_ref[...] = total
    copies[PIECES].wait()

    def send(k):
        return pltpu.make_async_copy(y_ref.at[k], y_out.at[k], out_sems.at[k])

    def per_k(k, carry):
        high, low = hi[k], lo[k]
        for part in range(2):
            at = slice(part * PART, part * PART + PART)
            out = dot3(g_ref[0, at, :], g_ref[1, at, :], high, low, NT)
            y_ref[k, :, part] = out.reshape(16, 16, ROWS)
        send(k).start()
        return carry

    def finish(k, carry):
        send(k).wait()
        return carry

    lax.fori_loop(0, RADIX, per_k, 0)
    lax.fori_loop(0, RADIX, finish, 0)


def rows_forward(x_now, table, tw):
    anywhere = pl.BlockSpec(memory_space=pl.ANY)
    vmem = pl.BlockSpec(memory_space=pltpu.VMEM)
    return pl.pallas_call(
        rows_body,
        in_specs=[anywhere, anywhere, vmem],
        out_specs=[anywhere, vmem],
        out_shape=[
            jax.ShapeDtypeStruct((RADIX, 16, 2, 16, ROWS), F32),
            jax.ShapeDtypeStruct((16, 128), F32),
        ],
        scratch_shapes=[
            pltpu.VMEM((RADIX, ROWS, 2 * PART), BF16),
            pltpu.VMEM((RADIX, ROWS, 2 * PART), BF16),
            pltpu.VMEM((2, 1, ROWS, N), F32),
            pltpu.VMEM((2, 2 * PART, 2 * PART), BF16),
            pltpu.VMEM((RADIX, 16, 2, 16, ROWS), F32),
            pltpu.SemaphoreType.DMA((PIECES + 1,)),
            pltpu.SemaphoreType.DMA((RADIX,)),
        ],
        compiler_params=params(62),
        cost_estimate=pl.CostEstimate(
            flops=4 * 10**9, bytes_accessed=10 * MIB, transcendentals=0
        ),
        name="rows_forward",
    )(x_now, table, tw)


def holo_body(depth_ref, x_in, gh_ref, gl_ref, tw_ref, y_ref, hi, lo, x_ref, sems):
    pairs = [(x_in.at[:, piece(q), :], x_ref.at[:, piece(q), :]) for q in range(PIECES)]
    copies = stage_copies(pairs, sems)

    def chunk(t, carry):
        rows = pl.ds(pl.multiple_of(t * 16, 16), 16)
        for half in range(2):

            def load(i):
                at = slice(i * PART + half * 128, i * PART + half * 128 + 128)
                return (x_ref[0, rows, at], x_ref[1, rows, at])

            forward_radix(load, tw_ref, hi, lo, rows, half)
        return carry

    for q in range(PIECES):
        copies[q].wait()
        lax.fori_loop(q * 2, q * 2 + 2, chunk, 0)
    y_ref[...] = jnp.full(y_ref.shape, depth_ref[0], F32)

    def per_k(k, carry):
        out = dot3(gh_ref[...], gl_ref[...], hi[k], lo[k], NT)
        for part in range(2):
            for half in range(2):
                y_ref[k, :, part * 2 + half, :] = out[
                    part * 16 : part * 16 + 16, half * 128 : half * 128 + 128
                ]
        return carry

    lax.fori_loop(0, RADIX, per_k, 0)


def holo_forward(depths, hologram, gt_high, gt_low, tw):
    return pl.pallas_call(
        holo_body,
        out_shape=jax.ShapeDtypeStruct((RADIX, 16, 8, 128), F32),
        scratch_shapes=[
            pltpu.VMEM((RADIX, ROWS, 2 * PART), BF16),
            pltpu.VMEM((RADIX, ROWS, 2 * PART), BF16),
            pltpu.VMEM((2, ROWS, N), F32),
            pltpu.SemaphoreType.DMA((PIECES,)),
        ],
        in_specs=[
            pl.BlockSpec(memory_space=pltpu.SMEM),
            pl.BlockSpec(memory_space=pl.ANY),
        ]
        + [pl.BlockSpec(memory_space=pltpu.VMEM)] * 3,
        out_specs=pl.BlockSpec(memory_space=pltpu.VMEM),
        compiler_params=params(62),
        cost_estimate=pl.CostEstimate(
            flops=4 * 10**8, bytes_accessed=5 * MIB, transcendentals=0
        ),
        name="holo_forward",
    )(depths, hologram, gt_high, gt_low, tw)


def cos_sin(phase):
    turns = jnp.floor(phase * (2.0 / math.pi) + 0.5)
    rest = phase - turns * 1.5703125
    rest = rest - turns * 4.837512969970703e-4
    rest = rest - turns * 7.549789948768648e-8
    z = rest * rest
    sin = rest + rest * z * (
        -1.6666654611e-1 + z * (8.3321608736e-3 + z * -1.9515295891e-4)
    )
    cos = (
        1.0
        - 0.5 * z
        + z
        * z
        * (4.166664568298827e-2 + z * (-1.388731625493765e-3 + z * 2.443315711809948e-5))
    )
    quarter = turns.astype(jnp.int32) & 3
    odd = (quarter & 1) == 1
    base_cos = jnp.where(odd, sin, cos)
    base_sin = jnp.where(odd, cos, sin)
    out_cos = jnp.where((quarter == 1) | (quarter == 2), -base_cos, base_cos)
    out_sin = jnp.where(quarter >= 2, -base_sin, base_sin)
    return out_cos, out_sin


def transfer_body(depth_ref, rate_ref, t_ref):
    rate = rate_ref[0]
    for p in range(PLANES):
        cos, sin = cos_sin(depth_ref[0, p] * rate)
        rows = slice(p * 16, p * 16 + 16)
        t_ref[0, 0, rows, :] = cos
        t_ref[0, 1, rows, :] = sin


def transfer(depth_all, rate):
    return pl.pallas_call(
        transfer_body,
        grid=(RADIX,),
        in_specs=[
            pl.BlockSpec(memory_space=pltpu.SMEM),
            pl.BlockSpec((1, 16, PART), lambda k: (k, 0, 0)),
        ],
        out_specs=pl.BlockSpec((1, 2, PLANES * 16, PART), lambda k: (k, 0, 0, 0)),
        out_shape=jax.ShapeDtypeStruct((RADIX, 2, PLANES * 16, PART), F32),
        compiler_params=params(62),
        cost_estimate=pl.CostEstimate(
            flops=10**7, bytes_accessed=4 * MIB, transcendentals=0
        ),
        name="transfer",
    )(depth_all, rate)


COLS = PLANES * 16
MESSAGE = 72
WITH_HOLO = COLS + 16


def planes_of(q):
    return pl.ds(q * 4, 4)


def spectral_body(
    z_in, h_in, t_in, sq_ref, g_in, tw_ref, o_out, norm_ref,
    hi, lo, spec, bhi, blo, back, z_ref, g_ref, o_ref, h_ref, t_ref, sems, out_sems, t_sems,
):
    norm_ref[...] = jnp.zeros_like(norm_ref)
    pairs = [(z_in.at[:, planes_of(q)], z_ref.at[:, planes_of(q)]) for q in range(4)]
    copies = stage_copies(pairs + [(h_in, h_ref), (g_in, g_ref)], sems)

    def take(k):
        return pltpu.make_async_copy(t_in.at[k], t_ref.at[k], t_sems.at[k])

    def begin(k, carry):
        take(k).start()
        return carry

    lax.fori_loop(0, RADIX, begin, 0)

    def chunk(p, carry):
        rows = pl.ds(pl.multiple_of(p * 16, 16), 16)
        for half in range(2):
            at = slice(half * 128, half * 128 + 128)

            def load(i):
                return (z_ref[i, p, 0, :, at], z_ref[i, p, 1, :, at])

            forward_radix(load, tw_ref, hi, lo, rows, half)
        return carry

    for q in range(4):
        copies[q].wait()
        lax.fori_loop(q * 4, q * 4 + 4, chunk, 0)
    copies[4].wait()
    for half in range(2):

        def load_holo(i):
            return (h_ref[i, :, half, :], h_ref[i, :, 2 + half, :])

        forward_radix(load_holo, tw_ref, hi, lo, slice(COLS, WITH_HOLO), half)
    copies[5].wait()

    def per_k(k, carry):
        spec[...] = dot3(hi[k], lo[k], g_ref[0], g_ref[1], NN)
        take(k).wait()

        for half in range(2):
            at = slice(half * 128, half * 128 + 128)
            at_im = slice(PART + half * 128, PART + half * 128 + 128)

            def gather(p, total):
                rows = pl.ds(pl.multiple_of(p * 16, 16), 16)
                xr, xi = spec[rows, at], spec[rows, at_im]
                tr, ti = t_ref[k, 0, rows, at], t_ref[k, 1, rows, at]
                return (total[0] + (tr * xr - ti * xi), total[1] + (tr * xi + ti * xr))

            zero = jnp.zeros((16, 128), F32)
            pred = lax.fori_loop(0, PLANES, gather, (zero, zero), unroll=4)
            holo = (spec[COLS:WITH_HOLO, at], spec[COLS:WITH_HOLO, at_im])
            res = (holo[0] - pred[0], holo[1] - pred[1])
            norm_ref[...] += res[0] * (holo[0] + pred[0]) + res[1] * (holo[1] + pred[1])

            def scatter(p, carry):
                rows = pl.ds(pl.multiple_of(p * 16, 16), 16)
                tr, ti = t_ref[k, 0, rows, at], t_ref[k, 1, rows, at]
                br = tr * res[0] + ti * res[1]
                bi = tr * res[1] - ti * res[0]
                for where, value in ((at, br), (at_im, bi)):
                    high, low = split(value)
                    bhi[rows, where] = high
                    blo[rows, where] = low
                return carry

            lax.fori_loop(0, PLANES, scatter, 0, unroll=4)

        c = tw_ref[k, 0:1, :]
        s = tw_ref[k, 1:2, :]
        out = dot3(bhi[...], blo[...], g_ref[2], g_ref[3], NN)
        re, im = out[:, :PART], out[:, PART:]
        back[k, 0] = re * c + im * s
        back[k, 1] = im * c - re * s
        return carry

    lax.fori_loop(0, RADIX, per_k, 0)

    square = sq_ref[...] + norm_ref[...] * (1.0 / PLANES)
    square = square[:8, :] + square[8:, :]
    square = square + pltpu.roll(square, 64, 1)
    lane = lax.broadcasted_iota(jnp.int32, (8, 128), 1)
    square = jnp.where(lane < 64, 0.0, square)

    def chunk(p, carry):
        rows = pl.ds(pl.multiple_of(p * 16, 16), 16)
        for half in range(2):
            at = slice(half * 128, half * 128 + 128)
            out = dft8([(back[i, 0, rows, at], back[i, 1, rows, at]) for i in range(RADIX)], 1)
            for i in range(RADIX):
                o_ref[i, p, half * 16 : half * 16 + 16, :] = out[i][0]
                o_ref[i, p, half * 16 + 32 : half * 16 + 48, :] = out[i][1]
        for i in range(RADIX):
            tile = square
            for high in range(2):
                for c in range(2):
                    low_rows = slice(c * 32 + high * 8, c * 32 + high * 8 + 8)
                    high_rows = slice(c * 32 + 16 + high * 8, c * 32 + 24 + high * 8)
                    edge = jnp.where(
                        lane < 2,
                        o_ref[min(i + 1, RADIX - 1), p, low_rows, :],
                        o_ref[max(i - 1, 0), p, high_rows, :],
                    )
                    base = high * 8 + c * 4
                    edge = pltpu.roll(edge, base + 2, 1)
                    tile = jnp.where((lane >= base) & (lane < base + 4), edge, tile)
            o_ref[i, p, 64:MESSAGE, :] = tile
        return carry

    sends = []
    for q in range(4):
        lax.fori_loop(q * 4, q * 4 + 4, chunk, 0)
        sends.append(
            pltpu.make_async_copy(
                o_ref.at[:, planes_of(q)], o_out.at[:, planes_of(q)], out_sems.at[q]
            )
        )
        sends[-1].start()
    for send in sends:
        send.wait()


def spectral(z, holo, trans, squares, table, tw):
    anywhere = pl.BlockSpec(memory_space=pl.ANY)
    vmem = pl.BlockSpec(memory_space=pltpu.VMEM)
    return pl.pallas_call(
        spectral_body,
        in_specs=[anywhere, anywhere, anywhere, vmem, anywhere, vmem],
        out_specs=anywhere,
        out_shape=jax.ShapeDtypeStruct((RADIX, PLANES, MESSAGE, 128), F32),
        scratch_shapes=[
            pltpu.VMEM((16, 128), F32),
            pltpu.VMEM((RADIX, WITH_HOLO, 2 * PART), BF16),
            pltpu.VMEM((RADIX, WITH_HOLO, 2 * PART), BF16),
            pltpu.VMEM((WITH_HOLO, 2 * PART), F32),
            pltpu.VMEM((COLS, 2 * PART), BF16),
            pltpu.VMEM((COLS, 2 * PART), BF16),
            pltpu.VMEM((RADIX, 2, COLS, PART), F32),
            pltpu.VMEM((RADIX, PLANES, 2, 16, PART), F32),
            pltpu.VMEM((4, 2 * PART, 2 * PART), BF16),
            pltpu.VMEM((RADIX, PLANES, MESSAGE, 128), F32),
            pltpu.VMEM((RADIX, 16, 8, 128), F32),
            pltpu.VMEM((RADIX, 2, COLS, PART), F32),
            pltpu.SemaphoreType.DMA((6,)),
            pltpu.SemaphoreType.DMA((4,)),
            pltpu.SemaphoreType.DMA((RADIX,)),
        ],
        compiler_params=params(62),
        cost_estimate=pl.CostEstimate(
            flops=8 * 10**9, bytes_accessed=14 * MIB, transcendentals=0
        ),
        name="spectral",
    )(z, holo, trans, squares, table, tw)


def rows_back_body(
    w_in, x_in, xt_ref, xb_ref, p_in, e_in, tw_ref, re_out, im_out, sum_ref,
    back, edge_back, w_ref, x_ref, parts, p_ref, e_ref, w_sems, sems, out_sems,
):
    tables = stage_copies([(p_in, p_ref), (e_in, e_ref)], sems)

    def take(k):
        return pltpu.make_async_copy(w_in.at[k], w_ref.at[k], w_sems.at[k])

    def begin(k, carry):
        take(k).start()
        return carry

    lax.fori_loop(0, RADIX, begin, 0)
    fetch = pltpu.make_async_copy(x_in, x_ref, sems.at[2])
    fetch.start()
    sum_ref[...] = jnp.zeros_like(sum_ref)
    for copy in tables:
        copy.wait()

    def per_k(k, carry):
        take(k).wait()
        tiles = w_ref[k, :, 64:MESSAGE, :]
        lane = lax.broadcasted_iota(jnp.int32, (8, 128), 1)
        sum_ref[...] += jnp.where(lane < 64, 0.0, jnp.sum(tiles, axis=0))
        turned = tiles.reshape(128, 128).T
        edge = jnp.concatenate([turned[0:8, :], turned[8:16, :]], axis=1)
        edge_high, edge_low = split(jnp.concatenate([edge, jnp.zeros_like(edge)], axis=0))
        mixed = dot3(edge_high, edge_low, e_ref[0], e_ref[1], NN)[0:8, :]
        swapped = pltpu.roll(mixed, 4, 0)
        edge_re = mixed[:, :PART] - swapped[:, PART:]
        edge_im = mixed[:, PART:] + swapped[:, :PART]

        halves = []
        for c in range(2):
            for h in range(2):
                rows = slice(c * 32 + h * 16, c * 32 + h * 16 + 16)
                halves.append(w_ref[k, :, rows, :].reshape(PART, 128).T)
        turned = [jnp.concatenate(halves[c * 2 : c * 2 + 2], axis=0) for c in range(2)]
        high, low = split(jnp.concatenate(turned, axis=1))
        out = dot3(high, low, p_ref[0], p_ref[1], NN)
        c = tw_ref[k, 0:1, :]
        s = tw_ref[k, 1:2, :]
        re, im = out[:, :PART], out[:, PART:]
        back[k, 0] = re * c + im * s
        back[k, 1] = im * c - re * s
        edge_back[k, 0] = edge_re * c + edge_im * s
        edge_back[k, 1] = edge_im * c - edge_re * s
        return carry

    lax.fori_loop(0, RADIX, per_k, 0)
    fetch.wait()
    low_rows = lax.broadcasted_iota(jnp.int32, (8, 128), 0) < 4
    for half in range(2):
        at = slice(half * 128, half * 128 + 128)
        out = dft8([(edge_back[i, 0, :, at], edge_back[i, 1, :, at]) for i in range(RADIX)], 1)
        for i in range(RADIX):
            to = slice(i * PART + half * 128, i * PART + half * 128 + 128)
            for c in range(2):
                value = pltpu.roll(out[i][c], 6, 0)
                x = jnp.where(low_rows, xb_ref[c, 0, :, to], xt_ref[c, 0, :, to])
                parts[c, ROWS:PACK, to] = value + x

    def chunk(t, carry):
        rows = pl.ds(pl.multiple_of(t * 16, 16), 16)
        for half in range(2):
            at = slice(half * 128, half * 128 + 128)
            out = dft8([(back[i, 0, rows, at], back[i, 1, rows, at]) for i in range(RADIX)], 1)
            for i in range(RADIX):
                to = slice(i * PART + half * 128, i * PART + half * 128 + 128)
                for c in range(2):
                    parts[c, rows, to] = x_ref[c, 0, rows, to] + out[i][c]
        return carry

    sends = []
    for q in range(4):
        lax.fori_loop(q * 4, q * 4 + 4, chunk, 0)
        span = pl.ds(q * 64, 72 if q == 3 else 64)
        for c, target in enumerate((re_out, im_out)):
            sends.append(
                pltpu.make_async_copy(
                    parts.at[c, span, :], target.at[span, :], out_sems.at[c, q]
                )
            )
            sends[-1].start()
    for send in sends:
        send.wait()


def rows_back(w, x_now, x_top, x_bottom, table, edge_table, tw):
    anywhere = pl.BlockSpec(memory_space=pl.ANY)
    vmem = pl.BlockSpec(memory_space=pltpu.VMEM)
    return pl.pallas_call(
        rows_back_body,
        in_specs=[anywhere, anywhere, vmem, vmem, anywhere, anywhere, vmem],
        out_specs=[anywhere, anywhere, vmem],
        out_shape=[
            jax.ShapeDtypeStruct((PACK, N), F32),
            jax.ShapeDtypeStruct((PACK, N), F32),
            jax.ShapeDtypeStruct((8, 128), F32),
        ],
        scratch_shapes=[
            pltpu.VMEM((RADIX, 2, ROWS, PART), F32),
            pltpu.VMEM((RADIX, 2, 8, PART), F32),
            pltpu.VMEM((RADIX, 16, MESSAGE, 128), F32),
            pltpu.VMEM((2, 1, ROWS, N), F32),
            pltpu.VMEM((2, PACK, N), F32),
            pltpu.VMEM((2, 2 * PART, 2 * PART), BF16),
            pltpu.VMEM((2, PART, 2 * PART), BF16),
            pltpu.SemaphoreType.DMA((RADIX,)),
            pltpu.SemaphoreType.DMA((3,)),
            pltpu.SemaphoreType.DMA((2, 4)),
        ],
        compiler_params=params(62),
        cost_estimate=pl.CostEstimate(
            flops=4 * 10**9, bytes_accessed=13 * MIB, transcendentals=0
        ),
        name="rows_back",
    )(w, x_now, x_top, x_bottom, table, edge_table, tw)


TILES = EXT // 8
WIDE = 512
STAGES = 4


def shift_up(x, after):
    row = lax.broadcasted_iota(jnp.int32, x.shape, 0)
    return pltpu.roll(jnp.where(row == 0, after, x), 7, 0)


def shift_down(x, before):
    row = lax.broadcasted_iota(jnp.int32, x.shape, 0)
    return pltpu.roll(jnp.where(row == 7, before, x), 1, 0)


def from_right(x, after):
    if after is None:
        col = lax.broadcasted_iota(jnp.int32, x.shape, 1)
        return jnp.where(col == WIDE - 1, x, pltpu.roll(x, WIDE - 1, 1))
    return pltpu.roll(jnp.concatenate([x, after], axis=1), WIDE + 127, 1)[:, :WIDE]


def from_left(x, before):
    if before is None:
        col = lax.broadcasted_iota(jnp.int32, x.shape, 1)
        return jnp.where(col == 0, 0.0, pltpu.roll(x, 1, 1))
    return pltpu.roll(jnp.concatenate([before, x], axis=1), 1, 1)[:, 128:]


def reciprocal(x):
    guess = pl.reciprocal(x, approx=True)
    return guess * (2.0 - x * guess)


def norm(gz, gy, gx):
    square = gz * gz + gy * gy + gx * gx
    return square * lax.rsqrt(square + 1e-30)


def patch(ref, lead, rows, start):
    at = slice(start, start + WIDE)
    after = None
    if start + WIDE < N:
        after = ref[lead + (rows, slice(start + WIDE, start + WIDE + 128))]
    return ref[lead + (rows, at)], after


def arrivals(source, target, q, first, last, sems, edge_sems):
    copies = [
        pltpu.make_async_copy(
            source.at[pl.ds(first, last - first), :],
            target.at[pl.ds(first + 8, last - first), :],
            sems.at[q],
        )
    ]
    halo = source.at[pl.ds(ROWS, 8), :]
    if q == 0:
        copies.append(pltpu.make_async_copy(halo, target.at[pl.ds(0, 8), :], edge_sems.at[0]))
    if q == STAGES - 1:
        copies.append(
            pltpu.make_async_copy(halo, target.at[pl.ds(ROWS + 8, 8), :], edge_sems.at[1])
        )
    return copies


def tv_first_body(
    halves, num_ref, at_ref, own, nxt, prv, inner_out, *rest
):
    high_out = rest[0] if halves else None
    dual_out, ext, inner, dual, in_sems, edge_sems, out_sems = rest[-7:]
    size = ROWS // STAGES
    mains = []
    for q in range(STAGES):
        mains.append([])
        for which, main in enumerate((own, nxt, prv)):
            mains[q] += arrivals(
                main,
                ext.at[which],
                q,
                q * size,
                (q + 1) * size,
                in_sems.at[which],
                edge_sems.at[which],
            )
        for copy in mains[q]:
            copy.start()
    scale = num_ref[0]
    inverse = num_ref[1]
    size_of = num_ref[5]
    keep_next = num_ref[2]
    keep_prev = num_ref[3]
    band = at_ref[0]

    def tile(t, carry):
        rows = pl.ds(pl.multiple_of(t * 8, 8), 8)
        later = pl.ds(pl.multiple_of(jnp.minimum(t + 1, TILES - 1) * 8, 8), 8)
        earlier = pl.ds(pl.multiple_of(jnp.maximum(t - 1, 0) * 8, 8), 8)
        left = None
        for start in range(0, N, WIDE):
            at = slice(start, start + WIDE)
            u, u_after = patch(ext, (0,), rows, start)
            q, q_after = patch(ext, (2,), rows, start)
            gz = (ext[1, rows, at] - u) * keep_next
            gy = shift_up(u, ext[0, later, at]) - u
            gx = from_right(u, u_after) - u
            w = scale * reciprocal(1.0 + size_of * norm(gz, gy, gx))
            dz, dy, dx = gz * w, gy * w, gx * w
            gz = (u - q) * keep_prev
            gy = shift_up(q, ext[2, later, at]) - q
            gx = from_right(q, q_after) - q
            dq = gz * (scale * reciprocal(1.0 + size_of * norm(gz, gy, gx)))
            above = shift_down(dy, dual[1, earlier, at])
            div = (dz - dq) + (dy - above) + (dx - from_left(dx, left))
            left = dx[:, WIDE - 128 :]
            inner[rows, at] = (div + u * inverse) * STEP_TV
            dual[0, rows, at] = dz
            dual[1, rows, at] = dy
            dual[2, rows, at] = dx
            dual[3, rows, at] = dq
        return carry

    outs = []
    done = 0
    for q in range(STAGES):
        for copy in mains[q]:
            copy.wait()
        if q == 0:

            @pl.when(band == 0)
            def _():
                for which in range(3):
                    ext[which, 7:8, :] = ext[which, 8:9, :]

        if q == STAGES - 1:

            @pl.when(band == N // ROWS - 1)
            def _():
                for which in range(3):
                    ext[which, ROWS + 8 : ROWS + 9, :] = ext[which, ROWS + 7 : ROWS + 8, :]

        upto = TILES if q == STAGES - 1 else (q + 1) * size // 8
        lax.fori_loop(done, upto, tile, 0)
        if q == 0:

            @pl.when(band == 0)
            def _():
                inner[7:8, :] = inner[8:9, :]

        if q == STAGES - 1:

            @pl.when(band == N // ROWS - 1)
            def _():
                inner[ROWS + 8 : ROWS + 9, :] = inner[ROWS + 7 : ROWS + 8, :]

        if q == STAGES - 1 and not halves:
            row = lax.broadcasted_iota(jnp.int32, (8, N), 0)
            inner[0:8, :] = jnp.where(row < 4, inner[ROWS + 8 : EXT, :], inner[0:8, :])
            outs.append(
                pltpu.make_async_copy(
                    inner.at[pl.ds(0, 8), :], inner_out.at[pl.ds(ROWS, 8), :], out_sems.at[2, 0]
                )
            )
            outs[-1].start()

        first = max(done, 1)
        last = min(upto, TILES - 1)
        span = pl.ds(done * 8, (upto - done) * 8)
        if halves:
            moves = []
            if done * 8 < HALF + 16:
                moves.append((inner_out, 0, done * 8, min(upto * 8, HALF + 16), 0))
            if upto * 8 > HALF:
                moves.append((high_out, HALF, max(done * 8, HALF), upto * 8, 2))
        else:
            moves = [(inner_out, 8, first * 8, last * 8, 0)]
        for target, shift, begin, end, lane in moves:
            outs.append(
                pltpu.make_async_copy(
                    inner.at[pl.ds(begin, end - begin), :],
                    target.at[pl.ds(begin - shift, end - begin), :],
                    out_sems.at[lane, q],
                )
            )
            outs[-1].start()
        outs.append(
            pltpu.make_async_copy(dual.at[:, span, :], dual_out.at[:, span, :], out_sems.at[1, q])
        )
        outs[-1].start()
        done = upto
    for copy in outs:
        copy.wait()


def tv_first(halves, numbers, place, own, nxt, prv):
    smem = pl.BlockSpec(memory_space=pltpu.SMEM)
    anywhere = pl.BlockSpec(memory_space=pl.ANY)
    inner = [jax.ShapeDtypeStruct((PACK, N), F32)]
    if halves:
        inner = [jax.ShapeDtypeStruct((HALF + 16, N), F32)] * 2
    return pl.pallas_call(
        functools.partial(tv_first_body, halves),
        in_specs=[smem, smem] + [anywhere] * 3,
        out_specs=[anywhere] * (len(inner) + 1),
        out_shape=inner + [jax.ShapeDtypeStruct((4, EXT, N), F32)],
        scratch_shapes=[
            pltpu.VMEM((3, EXT, N), F32),
            pltpu.VMEM((EXT, N), F32),
            pltpu.VMEM((4, EXT, N), F32),
            pltpu.SemaphoreType.DMA((3, STAGES)),
            pltpu.SemaphoreType.DMA((3, 2)),
            pltpu.SemaphoreType.DMA((3, STAGES)),
        ],
        compiler_params=params(63),
        cost_estimate=pl.CostEstimate(
            flops=10**8, bytes_accessed=17 * MIB, transcendentals=2 * 10**6
        ),
        name="tv_first",
    )(numbers, place, own, nxt, prv)


def tv_second_body(
    comp, half, num_ref, own_in, nxt_in, prv_in, dual_in, parts_in, x_prev_in, x_now_in, *rest
):
    out_ref, inner, dual, plain, below, sems, edge_sems, out_sems = rest[-8:]
    count = ROWS if half is None else HALF
    offset = 0 if half is None else HALF * half
    size = count // STAGES
    stages = STAGES
    copies = []
    for q in range(stages):
        first = 0 if q == 0 else q * size + 16
        span = pl.ds(first, (q + 1) * size + 16 - first)
        main = pl.ds(q * size, size)
        place = pl.ds(offset + q * size, size)
        dual_span = pl.ds(offset + first, (q + 1) * size + 16 - first)
        begin = 0 if q == 0 else q * size + 8
        end = min((q + 1) * size + 8, ROWS)
        blocks = []
        for i, ref in enumerate((own_in, nxt_in, prv_in)):
            if half is None:
                blocks += arrivals(ref, inner.at[i], q, begin, end, sems.at[i], edge_sems.at[i])
            else:
                blocks.append(
                    pltpu.make_async_copy(ref.at[span, :], inner.at[i, span, :], sems.at[i, q])
                )
        pairs = [
            (dual_in.at[:, dual_span, :], dual.at[:, span, :]),
            (parts_in.at[place, :], plain.at[0, main, :]),
            (x_prev_in.at[comp, 0, place, :], plain.at[1, main, :]),
            (x_now_in.at[comp, 0, place, :], plain.at[2, main, :]),
        ]
        copies.append(
            blocks
            + [pltpu.make_async_copy(a, b, sems.at[i + 3, q]) for i, (a, b) in enumerate(pairs)]
        )
        for copy in copies[-1]:
            copy.start()
    strength = num_ref[4]
    keep_next = num_ref[2]
    keep_prev = num_ref[3]

    def tile(t, carry):
        rows = pl.ds(pl.multiple_of(t * 8, 8), 8)
        later = pl.ds(pl.multiple_of(t * 8 + 8, 8), 8)
        main = pl.ds(pl.multiple_of(jnp.maximum(t - 1, 0) * 8, 8), 8)
        left = None
        for start in range(0, N, WIDE):
            at = slice(start, start + WIDE)
            u, u_after = patch(inner, (0,), rows, start)
            q, q_after = patch(inner, (2,), rows, start)
            gz = (inner[1, rows, at] - u) * keep_next
            gy = shift_up(u, inner[0, later, at]) - u
            gx = from_right(u, u_after) - u
            w = reciprocal(1.0 + norm(gz, gy, gx))
            dz = (dual[0, rows, at] + gz) * w
            dy = (dual[1, rows, at] + gy) * w
            dx = (dual[2, rows, at] + gx) * w
            gz = (u - q) * keep_prev
            gy = shift_up(q, inner[2, later, at]) - q
            gx = from_right(q, q_after) - q
            dq = (dual[3, rows, at] + gz) * reciprocal(1.0 + norm(gz, gy, gx))
            above = shift_down(dy, below[:, at])
            below[:, at] = dy
            div = (dz - dq) + (dy - above) + (dx - from_left(dx, left))
            left = dx[:, WIDE - 128 :]
            denoised = plain[0, main, at] - strength * div
            plain[1, main, at] = (
                (1.0 - ALPHA_TWIST) * plain[1, main, at]
                + (ALPHA_TWIST - BETA_TWIST) * plain[2, main, at]
                + BETA_TWIST * denoised
            )
        return carry

    def first_rows(start):
        at = slice(start, start + WIDE)
        u, u_after = patch(inner, (0,), slice(0, 8), start)
        gz = (inner[1, 0:8, at] - u) * keep_next
        gy = shift_up(u, inner[0, 8:16, at]) - u
        gx = from_right(u, u_after) - u
        below[:, at] = (dual[1, 0:8, at] + gy) * reciprocal(1.0 + norm(gz, gy, gx))

    outs = []
    for q in range(stages):
        for copy in copies[q]:
            copy.wait()
        if q == 0:
            for start in range(0, N, WIDE):
                first_rows(start)
        lax.fori_loop(1 + q * size // 8, 1 + (q + 1) * size // 8, tile, 0)
        main = pl.ds(q * size, size)
        outs.append(
            pltpu.make_async_copy(
                plain.at[1, main, :],
                out_ref.at[comp, 0, pl.ds(offset + q * size, size), :],
                out_sems.at[q],
            )
        )
        outs[-1].start()
    for copy in outs:
        copy.wait()


def tv_second(comp, half, numbers, own, nxt, prv, dual, parts, x_prev, x_now, into):
    smem = pl.BlockSpec(memory_space=pltpu.SMEM)
    anywhere = pl.BlockSpec(memory_space=pl.ANY)
    count = ROWS if half is None else HALF
    args = [numbers, own, nxt, prv, dual, parts, x_prev, x_now]
    aliases = {}
    if into is not None:
        args.append(into)
        aliases = {len(args) - 1: 0}
    return pl.pallas_call(
        functools.partial(tv_second_body, comp, half),
        in_specs=[smem] + [anywhere] * (len(args) - 1),
        out_specs=anywhere,
        out_shape=jax.ShapeDtypeStruct((2, 1, ROWS, N), F32),
        scratch_shapes=[
            pltpu.VMEM((3, count + 16, N), F32),
            pltpu.VMEM((4, count + 16, N), F32),
            pltpu.VMEM((3, count, N), F32),
            pltpu.VMEM((8, N), F32),
            pltpu.SemaphoreType.DMA((7, STAGES)),
            pltpu.SemaphoreType.DMA((3, 2)),
            pltpu.SemaphoreType.DMA((STAGES,)),
        ],
        input_output_aliases=aliases,
        compiler_params=params(63),
        cost_estimate=pl.CostEstimate(
            flops=10**8, bytes_accessed=23 * MIB, transcendentals=2 * 10**6
        ),
        name="tv_second",
    )(*args)


def from_behind(x, axis, by):
    count = lax.axis_size(axis)
    pairs = [(i, i + by) for i in range(count) if 0 <= i + by < count]
    return lax.ppermute(x, axis, pairs)


def signed_freq(freq):
    signed = jnp.where(freq < N // 2, freq, freq - N)
    return signed.astype(F32) * (2.0 * math.pi / N)


def phase_rate(qx_grid, qy_grid):
    square = qx_grid * qx_grid + qy_grid * qy_grid
    return -square / (WAVENUMBER + jnp.sqrt(WAVENUMBER * WAVENUMBER - square))


def shards(x_now, x_prev, hologram, depths):
    d = lax.axis_index("depth")
    r = lax.axis_index("rows")
    forward, inverse = dft_blocks(1.0 / math.sqrt(N))
    g_high, g_low = split_np(forward)
    i_high, i_low = split_np(inverse)
    p_high, p_low = split_np(inverse / PLANES)
    e_high, e_low = split_np(halo_table(inverse / PLANES))
    t_high, t_low = split_np(forward.T)
    pick = np.stack([t_high, t_low]).reshape(2, 2, 16, 16, 2 * PART)
    pick = np.ascontiguousarray(pick.transpose(3, 0, 1, 2, 4)).reshape(16, 2, 32, 2 * PART)
    tw = jnp.asarray(twiddles())
    both = ("rows", "depth")

    chosen = lax.dynamic_index_in_dim(jnp.asarray(pick), d, 0, keepdims=False)
    holo = holo_forward(depths, hologram, chosen[0], chosen[1], tw)
    holo = lax.all_to_all(holo.reshape(128, 8, 128), both, 0, 0, tiled=True)
    depth_all = holo[:PLANES, 4, 0].reshape(1, PLANES)
    kx = r + RADIX * (16 * d + jnp.arange(16, dtype=jnp.int32))
    ky = (
        jnp.arange(RADIX, dtype=jnp.int32)[:, None]
        + RADIX * jnp.arange(PART, dtype=jnp.int32)[None, :]
    )
    rate = phase_rate(signed_freq(kx)[None, :, None], signed_freq(ky)[:, None, :])
    trans = transfer(depth_all, rate)

    sent, squares = rows_forward(x_now, jnp.asarray(np.stack([t_high, t_low])), tw)
    got = lax.all_to_all(sent.reshape(128, 2, 16, ROWS), both, 0, 0, tiled=True)
    x_top = from_behind(x_now[:, :, ROWS - 8 :], "rows", 1)
    x_bottom = from_behind(x_now[:, :, :8], "rows", -1)
    back = spectral(
        got.reshape(RADIX, PLANES, 2, 16, ROWS),
        holo.reshape(RADIX, PLANES, 8, 128),
        trans,
        squares,
        jnp.asarray(np.stack([g_high, g_low, i_high, i_low])),
        tw,
    )
    ret = lax.all_to_all(back.reshape(128, MESSAGE, 128), both, 0, 0, tiled=True)
    re, im, sums = rows_back(
        ret.reshape(RADIX, PLANES, MESSAGE, 128),
        x_now,
        x_top,
        x_bottom,
        jnp.asarray(np.stack([p_high, p_low])),
        jnp.asarray(np.stack([e_high, e_low])),
        tw,
    )

    total = jnp.sum(sums)
    mean_square = jnp.maximum(total, 0.0) / (2.0 * PLANES * N * N)
    strength = LAMBDA_TV * jnp.sqrt(mean_square + EPSILON)
    numbers = jnp.stack(
        [
            -STEP_TV / strength,
            -1.0 / strength,
            (d < PLANES - 1).astype(F32),
            (d > 0).astype(F32),
            strength,
            STEP_TV / strength,
        ]
    )
    place = jnp.stack([r])

    own = (re, im)
    nxt = [from_behind(part, "depth", -1) for part in own]
    prv = [from_behind(part, "depth", 1) for part in own]
    inner_re, dual_re = tv_first(False, numbers, place, own[0], nxt[0], prv[0])
    inner_low, inner_high, dual_im = tv_first(True, numbers, place, own[1], nxt[1], prv[1])
    steps = ((0, None, inner_re, dual_re), (1, 0, inner_low, dual_im), (1, 1, inner_high, dual_im))
    out = None
    for c, half, inner, dual in steps:
        ahead = from_behind(inner, "depth", -1)
        behind = from_behind(inner, "depth", 1)
        out = tv_second(
            c, half, numbers, inner, ahead, behind, dual, own[c], x_prev, x_now, out
        )
    return out


def solution(mesh):
    return jax.shard_map(
        shards,
        mesh=mesh,
        in_specs=(
            P(None, "depth", "rows", None),
            P(None, "depth", "rows", None),
            P(None, "rows", None),
            P("depth"),
        ),
        out_specs=P(None, "depth", "rows", None),
        check_vma=False,
    )
```
